256 devices in a mesh: space: 32 (over x_lo, z, core), mode: 8 (over y, x_hi).
Axes of the slice: x: 4 (x_hi: 2, x_lo: 2; x = x_hi * 2 + x_lo), y: 4, z: 8, core: 2. Of those that a mesh axis runs over, the one named last changes fastest.
Arguments:
- load: float32 [128, 64, 8, 256], P('mode', 'space'), may hold values from -48 to 48
- mean_coeff: float32 [64, 8, 256], P('space'), may hold values from 0.5 to 2
- kl_ratio: float32 [10, 64, 8, 256], P(None, 'space'), may hold values from -0.04 to 0.04
- chaos_table: int32 [128, 10], replicated, may hold values from 0 to 3, as said below
Outputs:
- solution: float32 [128, 64, 8, 256], P('mode', 'space')
- residual: float32 [128, 64, 8, 256], P('mode', 'space')
The draws below stay inside these ranges and needn't reach their ends.
Inputs may be any that keep to these rules, and one draw needn't show every extreme that they name: `chaos_table`: the rows are distinct multi-indices of total degree at most 3; every multi-index of total degree at most 2 is a row, and exactly one row has an entry equal to 3.
All inputs are finite; a program needn't handle non-finite values.
Results may differ from the reference program's by a relative error of at most 0.00014.
Values sent between devices are 32-bit elements; how exact they have to be, the bound alone decides.
No kernel may reach another device: no remote copies, remote signals or barrier semaphores. Data moves between devices by JAX's collectives and lax.ppermute only.
A program may use at most 64 MiB of HBM per device.

```python
import math
import jax
import jax.numpy as jnp
import numpy as np
from jax import lax

MODES = 128
KL = 10
ITERS = 2
NY = 8
NZ = 256
NX = 64


def degree_rows(count, degree, first):
    if degree == 0:
        return [[0] * count]
    result = []
    for index in range(first, count):
        for tail in degree_rows(count, degree - 1, index):
            row = list(tail)
            row[index] += 1
            result.append(row)
    return result


def draw_chaos_table(key, part):
    key = jax.random.fold_in(key, 7)
    lower = degree_rows(KL, 0, 0) + degree_rows(KL, 1, 0) + degree_rows(KL, 2, 0)
    cubes = [row for row in degree_rows(KL, 3, 0) if max(row) == 3]
    others = [row for row in degree_rows(KL, 3, 0) if max(row) < 3]
    lower_rows = jnp.asarray(np.array(lower, dtype=np.int32))
    cube_rows = jnp.asarray(np.array(cubes, dtype=np.int32))
    other_rows = jnp.asarray(np.array(others, dtype=np.int32))
    needed = MODES - len(lower) - 1
    cube_pick = jax.random.randint(jax.random.fold_in(key, 1), (1,), 0, len(cubes))
    other_pick = jax.random.permutation(jax.random.fold_in(key, 2), len(others))[:needed]
    table = jnp.concatenate([lower_rows, cube_rows[cube_pick], other_rows[other_pick]], axis=0)
    order = jax.random.permutation(jax.random.fold_in(key, 3), MODES)
    return table[order].astype(jnp.int32)


def steps_of(stream_key, shape, cuts, smallest, top_value):
    def one(axis_at, parts):
        draws = jax.random.uniform(jax.random.fold_in(jax.random.fold_in(stream_key, 6), axis_at), (parts,), jnp.float32, smallest / len(cuts), top_value / len(cuts))
        return jnp.repeat(jnp.exp(draws), shape[axis_at] // parts).reshape((-1,) + (1,) * (len(shape) - axis_at - 1))

    gain = one(*cuts[0])
    for cut in cuts[1:]:
        gain = gain * one(*cut)
    return gain


def noise(key, dims, scale, most, pieces=(), kind=jnp.bfloat16):
    gain = steps_of(key, dims, pieces, -0.22, 0.18) if pieces else 1.0
    values = jax.random.normal(key, dims, jnp.float32) * scale * gain
    return jnp.minimum(jnp.maximum(values, -most), most).astype(kind)


def setup_inputs(seed: int = 0) -> dict:
    key_list = jax.random.split(jax.random.key(seed), 5)
    return {
        "load": noise(key_list[0], (MODES, NX, NY, NZ), 8.0, 48.0, ((0, 8), (1, 32)), jnp.float32),
        "mean_coeff": jnp.clip(jnp.exp(math.log(2.0) - 1.3862944 * jax.random.uniform(key_list[1], (NX, NY, NZ), jnp.float32) ** steps_of(key_list[1], (NX, NY, NZ), ((0, 32),), -0.2, 0.2)), 0.5, 2.0),
        "kl_ratio": jnp.clip(jax.random.uniform(key_list[2], (KL, NX, NY, NZ), jnp.float32, -0.04, 0.04) * steps_of(key_list[2], (KL, NX, NY, NZ), ((1, 32),), -0.4, 0.0), -0.04, 0.04),
        "chaos_table": draw_chaos_table(jax.random.fold_in(key_list[4], 71), 0),
    }


theta_value = 24.5
delta_value = 23.5
reaction = 1.0

def coupling(chaos_table):
    modes = chaos_table.shape[0]
    differ = chaos_table[:, None, :] - chaos_table[None, :, :]
    distance = lax.optimization_barrier(jnp.sum(jnp.abs(differ), axis=2))
    larger = jnp.maximum(chaos_table[:, None, :], chaos_table[None, :, :]).astype(jnp.float32)
    linked = (distance[:, :, None] == 1) & (jnp.abs(differ) == 1)
    values = jnp.where(linked, jnp.sqrt(larger), jnp.zeros_like(larger))
    values = jnp.transpose(values, (2, 0, 1))
    identity = jnp.eye(modes, dtype=jnp.float32)
    return jnp.concatenate([identity[None], values], axis=0)

def face_terms(padded):
    face_x = 0.5 * (padded[:, 1:, 1:-1, 1:-1] + padded[:, :-1, 1:-1, 1:-1])
    face_y = 0.5 * (padded[:, 1:-1, 1:, 1:-1] + padded[:, 1:-1, :-1, 1:-1])
    face_z = 0.5 * (padded[:, 1:-1, 1:-1, 1:] + padded[:, 1:-1, 1:-1, :-1])
    return (face_x, face_y, face_z)

def stencil(field_pad, face_x, face_y, face_z):
    flux_x = face_x * (field_pad[..., 1:, 1:-1, 1:-1] - field_pad[..., :-1, 1:-1, 1:-1])
    flux_y = face_y * (field_pad[..., 1:-1, 1:, 1:-1] - field_pad[..., 1:-1, :-1, 1:-1])
    flux_z = face_z * (field_pad[..., 1:-1, 1:-1, 1:] - field_pad[..., 1:-1, 1:-1, :-1])
    result = flux_x[..., :-1, :, :] - flux_x[..., 1:, :, :]
    result = result + (flux_y[..., :, :-1, :] - flux_y[..., :, 1:, :])
    return result + (flux_z[..., :-1] - flux_z[..., 1:])

def reference(load, mean_coeff, kl_ratio, chaos_table):
    couple = coupling(chaos_table)
    coefficient = jnp.concatenate([mean_coeff[None], mean_coeff[None] * kl_ratio], axis=0)
    padded_coeff = jnp.pad(coefficient, ((0, 0), (1, 1), (1, 1), (1, 1)))
    face_x, face_y, face_z = face_terms(padded_coeff)
    modes = load.shape[0]

    def operate(search):
        flat = search.reshape(modes, -1)

        def term(totals, inputs):
            matrix, fx, fy, fz = inputs
            mixture = jnp.dot(matrix, flat, precision=lax.Precision.HIGHEST, preferred_element_type=jnp.float32)
            mixture = mixture.reshape(search.shape)
            padded = jnp.pad(mixture, ((0, 0), (1, 1), (1, 1), (1, 1)))
            return (totals + stencil(padded, fx, fy, fz), None)
        totals, unused = lax.scan(term, jnp.zeros_like(search), (couple, face_x, face_y, face_z))
        return reaction * search + totals
    sigma = theta_value / delta_value
    rho_now = 1.0 / sigma
    solution = jnp.zeros_like(load)
    residual = load
    search = load / theta_value
    for sweep in range(ITERS):
        solution = solution + search
        residual = residual - operate(search)
        if sweep + 1 < ITERS:
            rho_next = 1.0 / (2.0 * sigma - rho_now)
            search = rho_next * rho_now * search + 2.0 * rho_next / delta_value * residual
            rho_now = rho_next
    return (solution, residual)
```

```python
import functools

import jax
import jax.numpy as jnp
from jax import lax
from jax.experimental import pallas as pl
from jax.experimental.pallas import tpu as pltpu
from jax.sharding import PartitionSpec as P

ITERS = 2
THETA = 24.5
DELTA = 23.5
KL = 10
MODES = 128
GROUPS = 8
OWN = MODES // GROUPS
NX_OWN = 2
NY = 8
NZ = 256
ROWS = NX_OWN * NY
ZC = NZ // GROUPS
HALO = 2
ZW = ZC + 2 * HALO
PLANE = NY * ZW
SLAB = NX_OWN * PLANE
SLAB_TILES = -(-SLAB // 128)
SLAB_LANES = SLAB_TILES * 128
WIDE_TILES = -(-3 * SLAB // 128)
WIDE = WIDE_TILES * 128
COEF_ROWS = 16
SEND_ROWS = SLAB_TILES * OWN + COEF_ROWS
OUT_TILES = ROWS * ZC // 128
SQRT2 = 2.0**0.5
SQRT6 = 6.0**0.5
VMEM = 40 * 1024 * 1024


def lanes(shape):
    return lax.broadcasted_iota(jnp.int32, shape, len(shape) - 1)


def mode_scale(table):
    t = table
    f = jnp.where(t >= 3, SQRT6, jnp.where(t == 2, SQRT2, 1.0)).astype(jnp.float32)
    return jnp.max(f, axis=1, keepdims=True)


def pack_kernel(load_ref, mean_ref, ratio_ref, table_ref, out_ref, halves):
    me = lax.axis_index("mode")
    flip = 1 - lax.rem(lax.axis_index("space"), 2)
    scale = mode_scale(table_ref[pl.ds(pl.multiple_of(me * OWN, OWN), OWN), :])
    lane = lanes((OWN, 128))
    out_ref[...] = jnp.zeros_like(out_ref)
    for h in range(NZ // 128):
        halves[h] = load_ref[:, 128 * h : 128 * h + 128]
    for p in range(ROWS):
        plane, y = p // NY, p % NY
        row = (plane + flip * (1 - 2 * plane)) * NY + y
        v = [halves[h, pl.ds(row, OWN, stride=ROWS), :] * scale for h in range(NZ // 128)]
        v = jnp.concatenate(v, axis=1)
        j, q = divmod(p * ZW, 128)
        for d in range(GROUPS):
            w = pltpu.roll(v, (q - (ZC * d - HALO)) % NZ, 1)
            lo = q + (HALO if d == 0 else 0)
            hi = q + ZW - (HALO if d == GROUPS - 1 else 0)
            for part in range(2):
                a, b = max(lo - 128 * part, 0), min(hi - 128 * part, 128)
                if b <= a:
                    continue
                at = slice((j + part) * OWN, (j + part + 1) * OWN)
                keep = (lane >= a) & (lane < b)
                out_ref[d, at, :] = jnp.where(keep, w[:, 128 * part : 128 * part + 128], out_ref[d, at, :])
    top = SLAB_TILES * OWN
    lane8 = lanes((COEF_ROWS, 128))
    for i in range(2):
        p = 2 * me + i
        plane, y = p // NY, lax.rem(p, NY)
        row = (plane + flip * (1 - 2 * plane)) * NY + y
        mean = mean_ref[pl.ds(row, 1), :]
        terms = [mean * ratio_ref[pl.ds(row + k * ROWS, 1), :] for k in range(KL)]
        c = jnp.concatenate(terms + [mean] + [jnp.zeros_like(mean)] * (COEF_ROWS - KL - 1), axis=0)
        q = i * ZW
        for d in range(GROUPS):
            w = pltpu.roll(c, (q - (ZC * d - HALO)) % NZ, 1)[:, :128]
            lo = q + (HALO if d == 0 else 0)
            hi = q + ZW - (HALO if d == GROUPS - 1 else 0)
            keep = (lane8 >= lo) & (lane8 < hi)
            out_ref[d, top:, :] = jnp.where(keep, w, out_ref[d, top:, :])


def neighbours(x, masks):
    width = x.shape[-1]
    total = pltpu.roll(x, 1, 1) + pltpu.roll(x, width - 1, 1)
    total = total + (pltpu.roll(x, ZW, 1) * masks[0] + pltpu.roll(x, width - ZW, 1) * masks[1])
    return total + (pltpu.roll(x, PLANE, 1) + pltpu.roll(x, width - PLANE, 1))


def slab_fields(ref):
    return jnp.concatenate(
        [ref[:, OWN * j : OWN * (j + 1), :].reshape(MODES, 128) for j in range(SLAB_TILES)], axis=1
    )


def slab_coefs(ref):
    top = SLAB_TILES * OWN
    lane = lanes((COEF_ROWS, SLAB_LANES))
    total = jnp.zeros((COEF_ROWS, SLAB_LANES), jnp.float32)
    for m in range(GROUPS):
        part = jnp.concatenate(
            [ref[m, top:, :], jnp.zeros((COEF_ROWS, SLAB_LANES - 128), jnp.float32)], axis=1
        )
        at = 2 * ZW * m
        total = total + pltpu.roll(part, at, 1) if at else total + part
    return total


def turned(x):
    lane = lanes(x.shape)
    out = jnp.where(lane < PLANE, pltpu.roll(x, SLAB_LANES - PLANE, 1), pltpu.roll(x, PLANE, 1))
    return jnp.where(lane < SLAB, out, 0.0)


def join(dst, inner, own, outer):
    start = SLAB // 128 * 128
    shift = SLAB - start
    own = pltpu.roll(own, shift, 1)
    lane = lanes((inner.shape[0], 128))
    dst[:, :start] = inner[:, :start]
    dst[:, start : start + 128] = jnp.where(lane < shift, inner[:, start : start + 128], own[:, :128])
    dst[:, start + 128 : start + SLAB_LANES] = own[:, 128:]
    dst[:, 2 * SLAB : 2 * SLAB + SLAB_LANES] = outer


def build_links(table_ref, links, pad):
    pad[...] = jnp.zeros_like(pad)
    pad[:, :KL] = table_ref[...].astype(jnp.float32)
    rows = pad[...]
    cols = jnp.transpose(rows)
    apart = jnp.zeros((MODES, MODES), jnp.float32)
    for k in range(KL):
        apart = apart + jnp.abs(rows[:, k : k + 1] - cols[k : k + 1, :])
    near = apart == 1.0
    for k in range(KL):
        mine = rows[:, k : k + 1]
        d = mine - cols[k : k + 1, :]
        t = jnp.where(near, jnp.where(d == -1.0, 1.0, jnp.where(d == 1.0, mine + jnp.zeros_like(d), 0.0)), 0.0)
        t = t.astype(jnp.bfloat16)
        links[MODES * k : MODES * (k + 1), :MODES] = t
        links[MODES * k : MODES * (k + 1), MODES:] = t


def step_kernel(own_ref, inner_ref, outer_ref, table_ref, out_ref, u, v, pc, qc, sol, res, coef, ecoef, links, pad, mixed, masks):
    build_links(table_ref, links, pad)
    join(u, turned(slab_fields(inner_ref)), slab_fields(own_ref), turned(slab_fields(outer_ref)))
    join(coef, turned(slab_coefs(inner_ref)), slab_coefs(own_ref), turned(slab_coefs(outer_ref)))
    lane = lanes((8, WIDE))
    first = jnp.zeros((8, WIDE), jnp.bool_)
    last = jnp.zeros((8, WIDE), jnp.bool_)
    for t in range(6):
        first = first | ((lane >= PLANE * t) & (lane < PLANE * t + ZW))
        last = last | ((lane >= PLANE * (t + 1) - ZW) & (lane < PLANE * (t + 1)))
    masks[0] = jnp.where(first, 0.0, 1.0)
    masks[1] = jnp.where(last, 0.0, 1.0)
    for r in range(0, COEF_ROWS, 8):
        c = coef[r : r + 8, :]
        ecoef[r : r + 8, :] = neighbours(c, masks) + 6.0 * c

    def spread(src, dst):
        def one(r, carry):
            at = pl.ds(pl.multiple_of(8 * r, 8), 8)
            dst[at, :] = neighbours(src[at, :], masks)
            return carry

        lax.fori_loop(0, MODES // 8, one, 0)

    def mix(src, at):
        x = src[:, at]
        high = x.astype(jnp.bfloat16)
        low = (x - high.astype(jnp.float32)).astype(jnp.bfloat16)
        pair = jnp.concatenate([high, low], axis=0)
        mixed[...] = jnp.dot(links[...], pair, preferred_element_type=jnp.float32)

    def weigh(src, at, weights, r):
        rows = slice(r, r + 32)
        total = src[rows, at] * weights[KL : KL + 1, at]
        for k in range(KL):
            total = total + mixed[MODES * k + r : MODES * k + r + 32, :] * weights[k : k + 1, at]
        return total

    def operate(wide, narrow):
        spread(u, v)

        def first_pass(c, both):
            at = pl.ds(pl.multiple_of(256 * c, 256), 256)
            mix(u, at)
            for r in range(0, MODES, 32):
                pc[r : r + 32, at] = weigh(u, at, coef, r)
                if both:
                    qc[r : r + 32, at] = weigh(u, at, ecoef, r)

        def second_pass(c):
            at = pl.ds(pl.multiple_of(256 * c, 256), 256)
            mix(v, at)
            for r in range(0, MODES, 32):
                qc[r : r + 32, at] = qc[r : r + 32, at] - weigh(v, at, coef, r)

        lax.fori_loop(wide[0], wide[1], lambda c, carry: (first_pass(c, True), carry)[1], 0)
        lax.fori_loop(narrow[0], narrow[1], lambda c, carry: (second_pass(c), carry)[1], 0)

    sigma = THETA / DELTA
    rho = 1.0 / sigma
    rho_next = 1.0 / (2.0 * sigma - rho)
    valid = coef[KL : KL + 1, :] > 0.0

    operate((0, 7), (1, 6))

    def close_first(r, carry):
        at = pl.ds(pl.multiple_of(8 * r, 8), 8)
        x = u[at, :]
        au = x + 0.5 * (qc[at, :] - neighbours(pc[at, :], masks))
        begin = x * (1.0 / THETA)
        r1 = x - au * (1.0 / THETA)
        search = (rho_next * rho) * begin + (2.0 * rho_next / DELTA) * r1
        search = jnp.where(valid, search, 0.0)
        lane = lanes((8, WIDE))
        search = jnp.where((lane >= PLANE) & (lane < 5 * PLANE), search, 0.0)
        res[at, :] = r1
        sol[at, :] = begin + search
        u[at, :] = search
        return carry

    lax.fori_loop(0, MODES // 8, close_first, 0)
    operate((1, 6), (2, 5))

    def close_second(r, carry):
        at = pl.ds(pl.multiple_of(8 * r, 8), 8)
        x = u[at, :]
        au = x + 0.5 * (qc[at, :] - neighbours(pc[at, :], masks))
        res[at, :] = res[at, :] - au
        return carry

    lax.fori_loop(0, MODES // 8, close_second, 0)

    lane16 = lanes((OWN, 128))

    def ship(g, carry):
        at = pl.ds(pl.multiple_of(OWN * g, OWN), OWN)
        for f, field in enumerate((sol, res)):
            for j in range(OUT_TILES):
                tile = jnp.zeros((OWN, 128), jnp.float32)
                for i in range(128 // ZC):
                    p = j * (128 // ZC) + i
                    start = SLAB + p * ZW + HALO
                    base, off = start // 128 * 128, start % 128
                    if off + ZC <= 128:
                        w = field[at, base : base + 128]
                        w = pltpu.roll(w, (ZC * i - off) % 128, 1)
                    else:
                        w = field[at, base : base + 256]
                        w = pltpu.roll(w, (ZC * i - off) % 256, 1)[:, :128]
                    tile = w if i == 0 else jnp.where(lane16 >= ZC * i, w, tile)
                out_ref[g, (f * OUT_TILES + j) * OWN : (f * OUT_TILES + j + 1) * OWN, :] = tile
        return carry

    lax.fori_loop(0, GROUPS, ship, 0)


def unpack_kernel(in_ref, table_ref, sol_ref, res_ref, halves):
    me = lax.axis_index("mode")
    flip = 1 - lax.rem(lax.axis_index("space"), 2)
    scale = 1.0 / mode_scale(table_ref[pl.ds(pl.multiple_of(me * OWN, OWN), OWN), :])
    lane = lanes((OWN, 128))
    per = 128 // ZC
    for f, ref in enumerate((sol_ref, res_ref)):
        for p in range(ROWS):
            plane, y = p // NY, p % NY
            row = (plane + flip * (1 - 2 * plane)) * NY + y
            j, i = p // per, p % per
            for h in range(NZ // 128):
                tile = None
                for n in range(per):
                    w = in_ref[per * h + n, (f * OUT_TILES + j) * OWN : (f * OUT_TILES + j + 1) * OWN, :]
                    if n != i:
                        w = pltpu.roll(w, (ZC * (n - i)) % 128, 1)
                    tile = w if n == 0 else jnp.where(lane >= ZC * n, w, tile)
                halves[f, h, pl.ds(row, OWN, stride=ROWS), :] = tile * scale
        for h in range(NZ // 128):
            ref[:, 128 * h : 128 * h + 128] = halves[f, h]


def whole(count):
    return [pl.BlockSpec(memory_space=pltpu.VMEM)] * count


def body(load, mean_coeff, kl_ratio, chaos_table):
    params = pltpu.CompilerParams(vmem_limit_bytes=VMEM)
    f32 = jnp.float32
    send = pl.pallas_call(
        pack_kernel,
        out_shape=jax.ShapeDtypeStruct((GROUPS, SEND_ROWS, 128), f32),
        in_specs=whole(4),
        out_specs=pl.BlockSpec(memory_space=pltpu.VMEM),
        scratch_shapes=[pltpu.VMEM((NZ // 128, OWN * ROWS, 128), f32)],
        compiler_params=params,
        name="pack",
    )(load.reshape(OWN * ROWS, NZ), mean_coeff.reshape(ROWS, NZ), kl_ratio.reshape(KL * ROWS, NZ), chaos_table)
    own = lax.all_to_all(send, "mode", 0, 0, tiled=True)
    count = lax.axis_size("space")
    on_chip = [e for i in range(0, count, 2) for e in ((i, i + 1), (i + 1, i))]
    off_chip = [e for i in range(1, count - 1, 2) for e in ((i, i + 1), (i + 1, i))]
    outer = lax.ppermute(own, "space", off_chip)
    inner = lax.ppermute(own, "space", on_chip)
    back = pl.pallas_call(
        step_kernel,
        out_shape=jax.ShapeDtypeStruct((GROUPS, 2 * OUT_TILES * OWN, 128), f32),
        in_specs=whole(4),
        out_specs=pl.BlockSpec(memory_space=pltpu.VMEM),
        scratch_shapes=[pltpu.VMEM((MODES, WIDE), f32)] * 6
        + [pltpu.VMEM((COEF_ROWS, WIDE), f32)] * 2
        + [
            pltpu.VMEM((KL * MODES, 2 * MODES), jnp.bfloat16),
            pltpu.VMEM((MODES, MODES), f32),
            pltpu.VMEM((KL * MODES, 256), f32),
            pltpu.VMEM((2, 8, WIDE), f32),
        ],
        compiler_params=params,
        name="step",
    )(own, inner, outer, chaos_table)
    back = lax.all_to_all(back, "mode", 0, 0, tiled=True)
    flat = jax.ShapeDtypeStruct((OWN * ROWS, NZ), f32)
    sol, res = pl.pallas_call(
        unpack_kernel,
        out_shape=(flat, flat),
        in_specs=whole(2),
        out_specs=tuple(whole(2)),
        scratch_shapes=[pltpu.VMEM((2, NZ // 128, OWN * ROWS, 128), f32)],
        compiler_params=params,
        name="unpack",
    )(back, chaos_table)
    return sol.reshape(load.shape), res.reshape(load.shape)


def solution(mesh):
    in_specs = (
        P("mode", "space", None, None),
        P("space", None, None),
        P(None, "space", None, None),
        P(),
    )
    out_specs = (P("mode", "space", None, None), P("mode", "space", None, None))
    return jax.shard_map(body, mesh=mesh, in_specs=in_specs, out_specs=out_specs, check_vma=False)
```

```python
import functools

import jax
import jax.numpy as jnp
from jax import lax
from jax.experimental import pallas as pl
from jax.experimental.pallas import tpu as pltpu
from jax.sharding import PartitionSpec as P

ITERS = 2
THETA = 24.5
DELTA = 23.5
KL = 10
MODES = 128
GROUPS = 8
OWN = MODES // GROUPS
NX_OWN = 2
NY = 8
NZ = 256
ROWS = NX_OWN * NY
ZC = NZ // GROUPS
HALO = 2
PLANE = NY * ZC
CORE_TILES = NX_OWN * PLANE // 128
RIM = 2 * HALO
RIM_PLANE = NY * RIM
SPARE = NX_OWN * RIM_PLANE
SLOTS = 6
RIMS = SLOTS * PLANE
WIDE = RIMS + 256
NEAR = slice(RIMS, RIMS + 128)
TERMS = KL + 1
COEF_ROWS = 16
SEND_ROWS = (CORE_TILES + 1) * OWN
OUT_TILES = CORE_TILES
SQRT2 = 2.0**0.5
SQRT6 = 6.0**0.5
VMEM = 40 * 1024 * 1024


def lanes(shape):
    return lax.broadcasted_iota(jnp.int32, shape, len(shape) - 1)


def mode_scale(table):
    t = table
    f = jnp.where(t >= 3, SQRT6, jnp.where(t == 2, SQRT2, 1.0)).astype(jnp.float32)
    return jnp.max(f, axis=1, keepdims=True)


def turn(x, by):
    by = by % x.shape[1]
    return pltpu.roll(x, by, 1) if by else x


def rim_of(tiles, d, at, lane):
    out = None
    for side, z in enumerate((ZC * d - HALO, ZC * (d + 1))):
        if not 0 <= z < NZ:
            continue
        lo = at + HALO * side
        w = turn(tiles[z // 128], lo - z % 128)
        w = jnp.where((lane >= lo) & (lane < lo + HALO), w, 0.0)
        out = w if out is None else out + w
    return out


def pack_kernel(load_ref, mean_ref, ratio_ref, table_ref, out_ref, halves):
    me = lax.axis_index("mode")
    flip = 1 - lax.rem(lax.axis_index("space"), 2)
    scale = mode_scale(table_ref[pl.ds(pl.multiple_of(me * OWN, OWN), OWN), :])
    lane = lanes((OWN, 128))
    per = 128 // ZC
    for h in range(NZ // 128):
        halves[h] = load_ref[:, 128 * h : 128 * h + 128]

    def row_of(p):
        plane, y = p // NY, lax.rem(p, NY)
        return (plane + flip * (1 - 2 * plane)) * NY + y

    coefs = []
    for i in range(2):
        row = row_of(2 * me + i)
        mean = mean_ref[pl.ds(row, 1), :]
        terms = [mean * ratio_ref[pl.ds(row + k * ROWS, 1), :] for k in range(KL)] + [mean]
        zero = jnp.zeros_like(mean)
        low = jnp.concatenate(terms + terms[:5], axis=0)
        mid = jnp.concatenate([zero] * 11 + terms[5:10], axis=0)
        top = jnp.concatenate([zero] * 11 + terms[10:] + [zero] * 4, axis=0)
        coefs.append([(c[:, :128], c[:, 128:]) for c in (low, mid, top)])
    sub = lax.broadcasted_iota(jnp.int32, (OWN, 128), 0)
    for d in range(GROUPS):
        total = jnp.zeros((OWN, 128), jnp.float32)
        for i in range(2):
            lo = SPARE + ZC * i
            w = turn(coefs[i][0][d // per], lo - ZC * (d % per))
            total = total + jnp.where((lane >= lo) & (lane < lo + ZC) & (sub < TERMS), w, 0.0)
            for g in range(3):
                w = rim_of(coefs[i][g], d, SPARE + 2 * RIM * g + RIM * i, lane)
                total = total + jnp.where(sub >= TERMS, w, 0.0)
        out_ref[d, CORE_TILES * OWN :, :] = total

    for j in range(CORE_TILES):
        rows = []
        for i in range(per):
            row = row_of(jnp.int32(per * j + i))
            rows.append([halves[h, pl.ds(row, OWN, stride=ROWS), :] * scale for h in range(NZ // 128)])
        for d in range(GROUPS):
            tile = None
            rim = out_ref[d, CORE_TILES * OWN :, :]
            for i in range(per):
                w = turn(rows[i][d // per], ZC * (i - d % per))
                tile = w if i == 0 else jnp.where(lane >= ZC * i, w, tile)
                rim = rim + rim_of(rows[i], d, RIM * (per * j + i), lane)
            out_ref[d, OWN * j : OWN * (j + 1), :] = tile
            out_ref[d, CORE_TILES * OWN :, :] = rim


def build_links(table_ref, links, pad):
    pad[...] = jnp.zeros_like(pad)
    pad[:, :KL] = table_ref[...].astype(jnp.float32)
    rows = pad[...]
    cols = jnp.transpose(rows)
    apart = jnp.zeros((MODES, MODES), jnp.float32)
    for k in range(KL):
        apart = apart + jnp.abs(rows[:, k : k + 1] - cols[k : k + 1, :])
    near = apart == 1.0
    for k in range(KL):
        mine = rows[:, k : k + 1]
        d = mine - cols[k : k + 1, :]
        t = jnp.where(near, jnp.where(d == -1.0, 1.0, jnp.where(d == 1.0, mine + jnp.zeros_like(d), 0.0)), 0.0)
        t = t.astype(jnp.bfloat16)
        links[MODES * k : MODES * (k + 1), :MODES] = t
        links[MODES * k : MODES * (k + 1), MODES:] = t


def core_cell(l):
    return lax.div(l, ZC), lax.rem(l, ZC)


def rim_cell(l):
    zi = lax.rem(l, RIM)
    return lax.rem(lax.div(l, RIM), NY), jnp.where(zi < HALO, zi - HALO, zi + ZC - HALO)


def grid_of(shape, rows_of, cols_of):
    a = rows_of(lax.broadcasted_iota(jnp.int32, shape, 0))
    b = cols_of(lax.broadcasted_iota(jnp.int32, shape, 1))
    return sum(jnp.abs(x - y) for x, y in zip(a, b))


def build_steps(core_step, near_step, far_step):
    def put(ref, at, to, apart):
        ref[at[0] : at[0] + apart.shape[0], to : to + apart.shape[1]] = jnp.where(
            apart == 1, 1.0, 0.0
        ).astype(jnp.bfloat16)

    square = (PLANE, PLANE)
    put(core_step, (0,), 0, grid_of(square, core_cell, core_cell))
    for t in range(4):

        def rim_at(l, t=t):
            y, z = rim_cell(l)
            return y + jnp.where(lax.div(l, RIM_PLANE) == t, 0, 100), z

        put(core_step, (0,), PLANE + 128 * t, grid_of((PLANE, 128), core_cell, rim_at))
        put(near_step, (0,), PLANE * t, grid_of((128, PLANE), rim_at, core_cell))

    def near(l):
        return (lax.div(l, RIM_PLANE) + 1,) + rim_cell(l)

    def far(l):
        t = lax.div(l, RIM_PLANE)
        return (jnp.where(t == 0, 5, jnp.where(t == 1, 0, 100)),) + rim_cell(l)

    put(near_step, (0,), 4 * PLANE, grid_of((128, 128), near, near))
    put(far_step, (0,), 0, grid_of((128, 128), far, near))


def tile_of(ref, j):
    return ref[:, OWN * j : OWN * (j + 1), :].reshape(MODES, 128)


def join(dst, own_ref, inner_ref, outer_ref):
    half = PLANE // 128
    slots = ((inner_ref, 1), (inner_ref, 0), (own_ref, 0), (own_ref, 1), (outer_ref, 1), (outer_ref, 0))
    for t, (ref, plane) in enumerate(slots):
        for h in range(half):
            dst[:, PLANE * t + 128 * h : PLANE * t + 128 * (h + 1)] = tile_of(ref, half * plane + h)
    lane = lanes((MODES, 128))
    inner, own, outer = (tile_of(ref, CORE_TILES) for ref in (inner_ref, own_ref, outer_ref))
    near = jnp.where(lane < RIM_PLANE, inner, turn(own, RIM_PLANE))
    dst[:, NEAR] = jnp.where(lane < 3 * RIM_PLANE, near, turn(outer, 2 * RIM_PLANE))
    far = jnp.where(lane < RIM_PLANE, outer, inner)
    dst[:, RIMS + 128 :] = jnp.where(lane < 2 * RIM_PLANE, far, 0.0)


def slab_coefs(ref):
    lane = lanes((OWN, 128))
    raw = [ref[m, CORE_TILES * OWN :, :] for m in range(GROUPS)]
    core = [jnp.where(lane < SPARE, turn(raw[2 * j], -SPARE), raw[2 * j + 1]) for j in range(CORE_TILES)]
    lane8 = lanes((8, 128))
    parts = []
    for g in range(3):
        total = jnp.zeros((8, 128), jnp.float32)
        for m in range(GROUPS):
            lo = 2 * RIM * m
            w = turn(raw[m][8:, :], lo - SPARE - 2 * RIM * g)
            total = jnp.where((lane8 >= lo) & (lane8 < lo + 2 * RIM), w, total)
        parts.append(total[3:, :])
    rim = jnp.concatenate(parts + [jnp.zeros((1, 128), jnp.float32)], axis=0)
    return core, rim


def join_coefs(dst, own_ref, inner_ref, outer_ref):
    half = PLANE // 128
    own, inner, outer = (slab_coefs(ref) for ref in (own_ref, inner_ref, outer_ref))
    slots = ((inner, 1), (inner, 0), (own, 0), (own, 1), (outer, 1), (outer, 0))
    for t, (slab, plane) in enumerate(slots):
        for h in range(half):
            dst[:, PLANE * t + 128 * h : PLANE * t + 128 * (h + 1)] = slab[0][half * plane + h]
    lane = lanes((COEF_ROWS, 128))
    near = jnp.where(lane < RIM_PLANE, inner[1], turn(own[1], RIM_PLANE))
    dst[:, NEAR] = jnp.where(lane < 3 * RIM_PLANE, near, turn(outer[1], 2 * RIM_PLANE))
    far = jnp.where(lane < RIM_PLANE, outer[1], inner[1])
    dst[:, RIMS + 128 :] = jnp.where(lane < 2 * RIM_PLANE, far, 0.0)


def parts_of(x, count, axis=0):
    out = []
    for _ in range(count - 1):
        h = x.astype(jnp.bfloat16)
        out.append(h)
        x = x - h.astype(jnp.float32)
    return jnp.concatenate(out + [x.astype(jnp.bfloat16)], axis=axis)


def neighbours(src, slots, rims, steps, parts=2):
    core_step, near_step, far_step = steps
    rows = src.shape[0]

    def product(at, matrix):
        out = jnp.dot(parts_of(src[:, at], parts), matrix, preferred_element_type=jnp.float32)
        return sum(out[rows * i : rows * (i + 1)] for i in range(parts))

    plane = lambda t: slice(PLANE * t, PLANE * (t + 1))
    first, last = PLANE * (slots[0] - 1), PLANE * slots[-1]
    if rims:
        rim = product(NEAR, near_step[:, 4 * PLANE :]) + product(slice(RIMS + 128, WIDE), far_step[...])
    edge = product(NEAR, near_step[:, first:last])
    out = {}
    for t in slots:
        x = product(plane(t), core_step[:, :PLANE])
        if rims:
            rim = rim + product(plane(t), core_step[:, PLANE + 128 * (t - 1) : PLANE + 128 * t])
        x = x + edge[:, PLANE * t - PLANE - first : PLANE * t - first]
        out[t] = x + (src[:, plane(t - 1)] + src[:, plane(t + 1)])
    if rims:
        out["rim"] = rim
    return out


def step_kernel(own_ref, inner_ref, outer_ref, table_ref, out_ref, u, v, pc, qc, sol, res, coef, ecoef, links, pad, mixed, core_step, near_step, far_step):
    build_links(table_ref, links, pad)
    steps = (core_step, near_step, far_step)
    build_steps(*steps)
    join(u, own_ref, inner_ref, outer_ref)
    join_coefs(coef, own_ref, inner_ref, outer_ref)
    plane = lambda t: slice(PLANE * t, PLANE * (t + 1))
    for t, x in neighbours(coef, (1, 2, 3, 4), True, steps, 3).items():
        at = NEAR if t == "rim" else plane(t)
        ecoef[:, at] = x + 6.0 * coef[:, at]

    def mix(src, at):
        width = at.stop - at.start
        mixed[:, :width] = jnp.dot(links[...], parts_of(src[:, at], 2), preferred_element_type=jnp.float32)

    def weigh(src, at, weights, r):
        width = at.stop - at.start
        total = src[r : r + 32, at] * weights[KL : KL + 1, at]
        for k in range(KL):
            total = total + mixed[MODES * k + r : MODES * k + r + 32, :width] * weights[k : k + 1, at]
        return total

    def operate(only, both, slots, rims):
        for t, x in neighbours(u, slots, rims, steps).items():
            v[:, NEAR if t == "rim" else plane(t)] = x
        for at, with_q in [(a, False) for a in only] + [(a, True) for a in both]:
            mix(u, at)
            for r in range(0, MODES, 32):
                pc[r : r + 32, at] = weigh(u, at, coef, r)
                if with_q:
                    qc[r : r + 32, at] = weigh(u, at, ecoef, r)
        for at in both:
            mix(v, at)
            for r in range(0, MODES, 32):
                qc[r : r + 32, at] = qc[r : r + 32, at] - weigh(v, at, coef, r)

    sigma = THETA / DELTA
    rho = 1.0 / sigma
    rho_next = 1.0 / (2.0 * sigma - rho)

    operate([plane(0), plane(5), slice(RIMS + 128, WIDE)], [plane(t) for t in (1, 2, 3, 4)] + [NEAR], (1, 2, 3, 4), True)
    for t, around in neighbours(pc, (1, 2, 3, 4), True, steps).items():
        at = NEAR if t == "rim" else plane(t)
        x = u[:, at]
        au = x + 0.5 * (qc[:, at] - around)
        begin = x * (1.0 / THETA)
        r1 = x - au * (1.0 / THETA)
        search = (rho_next * rho) * begin + (2.0 * rho_next / DELTA) * r1
        search = jnp.where(coef[KL : KL + 1, at] > 0.0, search, 0.0)
        if t in (2, 3):
            res[:, plane(t - 2)] = r1
            sol[:, plane(t - 2)] = begin + search
        u[:, at] = search
    operate([plane(1), plane(4), NEAR], [plane(2), plane(3)], (2, 3), False)
    for t, around in neighbours(pc, (2, 3), False, steps).items():
        at = plane(t)
        res[:, plane(t - 2)] = res[:, plane(t - 2)] - (u[:, at] + 0.5 * (qc[:, at] - around))
    for f, field in enumerate((sol, res)):
        for j in range(OUT_TILES):
            n = (f * OUT_TILES + j) * OWN
            out_ref[:, n : n + OWN, :] = field[:, 128 * j : 128 * (j + 1)].reshape(GROUPS, OWN, 128)


def unpack_kernel(in_ref, table_ref, sol_ref, res_ref, halves):
    me = lax.axis_index("mode")
    flip = 1 - lax.rem(lax.axis_index("space"), 2)
    scale = 1.0 / mode_scale(table_ref[pl.ds(pl.multiple_of(me * OWN, OWN), OWN), :])
    lane = lanes((OWN, 128))
    per = 128 // ZC
    for f, ref in enumerate((sol_ref, res_ref)):
        for p in range(ROWS):
            plane, y = p // NY, p % NY
            row = (plane + flip * (1 - 2 * plane)) * NY + y
            j, i = p // per, p % per
            for h in range(NZ // 128):
                tile = None
                for n in range(per):
                    w = in_ref[per * h + n, (f * OUT_TILES + j) * OWN : (f * OUT_TILES + j + 1) * OWN, :]
                    if n != i:
                        w = pltpu.roll(w, (ZC * (n - i)) % 128, 1)
                    tile = w if n == 0 else jnp.where(lane >= ZC * n, w, tile)
                halves[f, h, pl.ds(row, OWN, stride=ROWS), :] = tile * scale
        for h in range(NZ // 128):
            ref[:, 128 * h : 128 * h + 128] = halves[f, h]


def whole(count):
    return [pl.BlockSpec(memory_space=pltpu.VMEM)] * count


def body(load, mean_coeff, kl_ratio, chaos_table):
    params = pltpu.CompilerParams(vmem_limit_bytes=VMEM)
    f32 = jnp.float32
    send = pl.pallas_call(
        pack_kernel,
        out_shape=jax.ShapeDtypeStruct((GROUPS, SEND_ROWS, 128), f32),
        in_specs=whole(4),
        out_specs=pl.BlockSpec(memory_space=pltpu.VMEM),
        scratch_shapes=[pltpu.VMEM((NZ // 128, OWN * ROWS, 128), f32)],
        compiler_params=params,
        name="pack",
    )(load.reshape(OWN * ROWS, NZ), mean_coeff.reshape(ROWS, NZ), kl_ratio.reshape(KL * ROWS, NZ), chaos_table)
    own = lax.all_to_all(send, "mode", 0, 0, tiled=True)
    count = lax.axis_size("space")
    on_chip = [e for i in range(0, count, 2) for e in ((i, i + 1), (i + 1, i))]
    off_chip = [e for i in range(1, count - 1, 2) for e in ((i, i + 1), (i + 1, i))]
    outer = lax.ppermute(own, "space", off_chip)
    inner = lax.ppermute(own, "space", on_chip)
    back = pl.pallas_call(
        step_kernel,
        out_shape=jax.ShapeDtypeStruct((GROUPS, 2 * OUT_TILES * OWN, 128), f32),
        in_specs=whole(4),
        out_specs=pl.BlockSpec(memory_space=pltpu.VMEM),
        scratch_shapes=[pltpu.VMEM((MODES, WIDE), f32)] * 4
        + [pltpu.VMEM((MODES, 2 * PLANE), f32)] * 2
        + [pltpu.VMEM((COEF_ROWS, WIDE), f32)] * 2
        + [
            pltpu.VMEM((KL * MODES, 2 * MODES), jnp.bfloat16),
            pltpu.VMEM((MODES, MODES), f32),
            pltpu.VMEM((KL * MODES, 256), f32),
            pltpu.VMEM((PLANE, PLANE + 4 * 128), jnp.bfloat16),
            pltpu.VMEM((128, 4 * PLANE + 128), jnp.bfloat16),
            pltpu.VMEM((128, 128), jnp.bfloat16),
        ],
        compiler_params=params,
        name="step",
    )(own, inner, outer, chaos_table)
    back = lax.all_to_all(back, "mode", 0, 0, tiled=True)
    flat = jax.ShapeDtypeStruct((OWN * ROWS, NZ), f32)
    sol, res = pl.pallas_call(
        unpack_kernel,
        out_shape=(flat, flat),
        in_specs=whole(2),
        out_specs=tuple(whole(2)),
        scratch_shapes=[pltpu.VMEM((2, NZ // 128, OWN * ROWS, 128), f32)],
        compiler_params=params,
        name="unpack",
    )(back, chaos_table)
    return sol.reshape(load.shape), res.reshape(load.shape)


def solution(mesh):
    in_specs = (
        P("mode", "space", None, None),
        P("space", None, None),
        P(None, "space", None, None),
        P(),
    )
    out_specs = (P("mode", "space", None, None), P("mode", "space", None, None))
    return jax.shard_map(body, mesh=mesh, in_specs=in_specs, out_specs=out_specs, check_vma=False)
```

```python
import functools

import jax
import jax.numpy as jnp
from jax import lax
from jax.experimental import pallas as pl
from jax.experimental.pallas import tpu as pltpu
from jax.sharding import PartitionSpec as P

ITERS = 2
THETA = 24.5
DELTA = 23.5
KL = 10
MODES = 128
GROUPS = 8
OWN = MODES // GROUPS
NX_OWN = 2
NY = 8
NZ = 256
ROWS = NX_OWN * NY
ZC = NZ // GROUPS
HALO = 2
PLANE = NY * ZC
CORE_TILES = NX_OWN * PLANE // 128
RIM = 2 * HALO
RIM_PLANE = NY * RIM
SPARE = NX_OWN * RIM_PLANE
TERMS = KL + 1
COEF_ROWS = 16
SEND_ROWS = (CORE_TILES + 1) * OWN
OUT_TILES = CORE_TILES
BLOCK = 32
SQRT2 = 2.0**0.5
SQRT6 = 6.0**0.5
VMEM = 40 * 1024 * 1024
PACK_VMEM = 62 * 1024 * 1024


def lanes(shape):
    return lax.broadcasted_iota(jnp.int32, shape, len(shape) - 1)


def mode_scale(t):
    f = jnp.where(t >= 3, SQRT6, jnp.where(t == 2, SQRT2, 1.0)).astype(jnp.float32)
    f = jnp.max(f, axis=0, keepdims=True)
    shape = (OWN, MODES)
    mine = lanes(shape) == lax.broadcasted_iota(jnp.int32, shape, 0) + OWN * lax.axis_index("mode")
    return jnp.sum(jnp.where(mine, f, 0.0), axis=1, keepdims=True)


def turn(x, by):
    by = by % x.shape[1]
    return pltpu.roll(x, by, 1) if by else x


def edges_of(tiles, at, lane):
    out = []
    for e in range(GROUPS + 1):
        z = ZC * e - HALO
        total = None
        for n, tile in enumerate(tiles):
            lo, hi = max(z, 128 * n), min(z + RIM, 128 * (n + 1))
            if lo >= hi:
                continue
            w = turn(tile, at - z)
            w = jnp.where((lane >= at + lo - z) & (lane < at + hi - z), w, 0.0)
            total = w if total is None else total + w
        out.append(total)
    return out


def pack_kernel(load_hbm, mean_hbm, ratio_hbm, table_hbm, out_ref, halves, mean_ref, ratio_ref, table_ref, sems):
    copies = [
        pltpu.make_async_copy(ratio_hbm, ratio_ref, sems.at[0]),
        pltpu.make_async_copy(mean_hbm, mean_ref, sems.at[1]),
        pltpu.make_async_copy(table_hbm, table_ref, sems.at[2]),
    ] + [
        pltpu.make_async_copy(load_hbm.at[:, pl.ds(128 * h, 128)], halves.at[h], sems.at[3 + h])
        for h in range(NZ // 128)
    ]
    for copy in copies:
        copy.start()
    me = lax.axis_index("mode")
    flip = 1 - lax.rem(lax.axis_index("space"), 2)
    lane = lanes((OWN, 128))
    per = 128 // ZC
    for copy in copies:
        copy.wait()
    scale = mode_scale(table_ref[...])

    def row_of(p):
        plane, y = p // NY, lax.rem(p, NY)
        return (plane + flip * (1 - 2 * plane)) * NY + y

    coefs = []
    for i in range(2):
        row = row_of(2 * me + i)
        mean = mean_ref[pl.ds(row, 1), :]
        terms = [mean * ratio_ref[pl.ds(row + k * ROWS, 1), :] for k in range(KL)] + [mean]
        zero = jnp.zeros_like(mean)
        low = jnp.concatenate(terms + terms[:5], axis=0)
        mid = jnp.concatenate([zero] * 11 + terms[5:10], axis=0)
        top = jnp.concatenate([zero] * 11 + terms[10:] + [zero] * 4, axis=0)
        coefs.append([(c[:, :128], c[:, 128:]) for c in (low, mid, top)])
    lane8 = lanes((8, 128))
    sub8 = lax.broadcasted_iota(jnp.int32, (8, 128), 0)
    first = lax.rem(lane8, RIM) < HALO
    borders = [jnp.zeros((8, 128), jnp.float32)] * (GROUPS + 1)
    for i in range(2):
        for g in range(3):
            tiles = [c[8:, :] for c in coefs[i][g]]
            more = edges_of(tiles, SPARE + 2 * RIM * g + RIM * i, lane8)
            borders = [x + y for x, y in zip(borders, more)]
    base = []
    for d in range(GROUPS):
        own_cells = []
        for i in range(2):
            w = turn(coefs[i][0][d // per], SPARE + ZC * i - ZC * (d % per))
            own_cells.append(jnp.where((lane >= SPARE + ZC * i) & (lane < SPARE + ZC * (i + 1)), w, 0.0))
        own_cells = own_cells[0] + own_cells[1]
        low = jnp.where(sub8 < TERMS - 8, own_cells[8:, :], jnp.where(first, borders[d], borders[d + 1]))
        base.append(jnp.concatenate([own_cells[:8, :], low], axis=0))

    first = lax.rem(lane, RIM) < HALO
    borders = [jnp.zeros((OWN, 128), jnp.float32)] * (GROUPS + 1)
    for j in range(CORE_TILES):
        rows = []
        for i in range(per):
            row = row_of(jnp.int32(per * j + i))
            rows.append([halves[h, pl.ds(row, OWN, stride=ROWS), :] * scale for h in range(NZ // 128)])
            more = edges_of(rows[i], RIM * (per * j + i), lane)
            borders = [x + y for x, y in zip(borders, more)]
        for d in range(GROUPS):
            tile = None
            for i in range(per):
                w = turn(rows[i][d // per], ZC * (i - d % per))
                tile = w if i == 0 else jnp.where(lane >= ZC * i, w, tile)
            out_ref[d, OWN * j : OWN * (j + 1), :] = tile
    for d in range(GROUPS):
        out_ref[d, CORE_TILES * OWN :, :] = base[d] + jnp.where(first, borders[d], borders[d + 1])


def build_links(table_ref, links, pad):
    pad[...] = jnp.zeros_like(pad)
    pad[:KL, :] = table_ref[...].astype(jnp.float32)
    cols = pad[...]
    rows = jnp.transpose(cols)
    apart = jnp.zeros((MODES, MODES), jnp.float32)
    for k in range(KL):
        apart = apart + jnp.abs(rows[:, k : k + 1] - cols[k : k + 1, :])
    near = apart == 1.0
    for k in range(KL):
        mine = rows[:, k : k + 1]
        d = mine - cols[k : k + 1, :]
        t = jnp.where(near, jnp.where(d == -1.0, 1.0, jnp.where(d == 1.0, mine + jnp.zeros_like(d), 0.0)), 0.0)
        t = t.astype(jnp.bfloat16)
        for b in range(MODES // BLOCK):
            at = (KL * b + k) * BLOCK
            links[at : at + BLOCK, :MODES] = t[BLOCK * b : BLOCK * (b + 1), :]
            links[at : at + BLOCK, MODES:] = t[BLOCK * b : BLOCK * (b + 1), :]


def core_cell(l):
    return lax.div(l, ZC), lax.rem(l, ZC)


def rim_cell(l):
    zi = lax.rem(l, RIM)
    return lax.rem(lax.div(l, RIM), NY), jnp.where(zi < HALO, zi - HALO, zi + ZC - HALO)


def grid_of(shape, rows_of, cols_of):
    a = rows_of(lax.broadcasted_iota(jnp.int32, shape, 0))
    b = cols_of(lax.broadcasted_iota(jnp.int32, shape, 1))
    return sum(jnp.abs(x - y) for x, y in zip(a, b))


def build_steps(core_step, near_step, far_step):
    def fill(ref, at, to, apart):
        ref[at[0] : at[0] + apart.shape[0], to : to + apart.shape[1]] = jnp.where(
            apart == 1, 1.0, 0.0
        ).astype(jnp.bfloat16)

    square = (PLANE, PLANE)
    fill(core_step, (0,), 0, grid_of(square, core_cell, core_cell))
    for t in range(4):

        def rim_at(l, t=t):
            y, z = rim_cell(l)
            return y + jnp.where(lax.div(l, RIM_PLANE) == t, 0, 100), z

        fill(core_step, (0,), PLANE + 128 * t, grid_of((PLANE, 128), core_cell, rim_at))
        fill(near_step, (0,), PLANE * t, grid_of((128, PLANE), rim_at, core_cell))

    def near(l):
        return (lax.div(l, RIM_PLANE) + 1,) + rim_cell(l)

    def far(l):
        t = lax.div(l, RIM_PLANE)
        return (jnp.where(t == 0, 5, jnp.where(t == 1, 0, 100)),) + rim_cell(l)

    fill(near_step, (0,), 4 * PLANE, grid_of((128, 128), near, near))
    fill(far_step, (0,), 0, grid_of((128, 128), far, near))


def tile_of(ref, j):
    return ref[:, OWN * j : OWN * (j + 1), :].reshape(MODES, 128)


def plane_of(ref, plane):
    half = PLANE // 128
    return jnp.concatenate([tile_of(ref, half * plane + h) for h in range(half)], axis=1)


def near_of(inner, own, outer):
    lane = lanes(own.shape)
    out = jnp.where((lane >= RIM_PLANE) & (lane < 3 * RIM_PLANE), turn(own, RIM_PLANE), 0.0)
    if inner is not None:
        out = jnp.where(lane < RIM_PLANE, inner, out)
    if outer is not None:
        out = jnp.where(lane < 3 * RIM_PLANE, out, turn(outer, 2 * RIM_PLANE))
    return out


def far_of(inner, outer):
    lane = lanes(inner.shape)
    return jnp.where(lane < RIM_PLANE, outer, jnp.where(lane < 2 * RIM_PLANE, inner, 0.0))


def slab_coefs(ref):
    lane = lanes((OWN, 128))
    raw = [ref[m, CORE_TILES * OWN :, :] for m in range(GROUPS)]
    core = [jnp.where(lane < SPARE, turn(raw[2 * j], -SPARE), raw[2 * j + 1]) for j in range(CORE_TILES)]
    lane8 = lanes((8, 128))
    parts = []
    for g in range(3):
        total = jnp.zeros((8, 128), jnp.float32)
        for m in range(GROUPS):
            lo = 2 * RIM * m
            w = turn(raw[m][8:, :], lo - SPARE - 2 * RIM * g)
            total = jnp.where((lane8 >= lo) & (lane8 < lo + 2 * RIM), w, total)
        parts.append(total[3:, :])
    rim = jnp.concatenate(parts + [jnp.zeros((1, 128), jnp.float32)], axis=0)
    return jnp.concatenate(core + [rim], axis=1)


def parts_of(x, count, axis=0):
    out = []
    for _ in range(count - 1):
        h = x.astype(jnp.bfloat16)
        out.append(h)
        x = x - h.astype(jnp.float32)
    return jnp.concatenate(out + [x.astype(jnp.bfloat16)], axis=axis)


def get(field, t):
    part = field[t]
    return part() if callable(part) else part[0][:, part[1]]


def put(field, t, x):
    ref, at = field[t]
    ref[:, at] = x


def product(x, matrix, parts=2):
    out = jnp.dot(parts_of(x, parts), matrix, preferred_element_type=jnp.float32)
    return sum(out[x.shape[0] * i : x.shape[0] * (i + 1)] for i in range(parts))


def neighbours(src, slots, rims, steps, parts=2, along_x=True):
    core_step, near_step, far_step = steps
    out = {}
    for t in slots:
        x = product(get(src, t), core_step[:, :PLANE], parts)
        x = x + product(get(src, "near"), near_step[:, PLANE * (t - 1) : PLANE * t], parts)
        out[t] = x + (get(src, t - 1) + get(src, t + 1)) if along_x else x
    if rims:
        out["near"] = product(get(src, "near"), near_step[:, 4 * PLANE :], parts)
        out["near"] += product(get(src, "far"), far_step[...], parts)
        for t in (1, 2, 3, 4):
            out["near"] += product(get(src, t), core_step[:, PLANE + 128 * (t - 1) : PLANE + 128 * t], parts)
    return out


def mix(links, x, sums):
    width = x.shape[1]
    pair = parts_of(x, 2)
    rows_of = [
        [jnp.broadcast_to(ref[k : k + 1, at], (8, width)) for k in range(TERMS)] for (ref, at), _ in sums
    ]
    split = lambda x: x.reshape(BLOCK // 8, 8, width)
    for b in range(MODES // BLOCK):
        rows = slice(BLOCK * b, BLOCK * (b + 1))
        mixed = jnp.dot(
            links[KL * BLOCK * b : KL * BLOCK * (b + 1), :], pair, preferred_element_type=jnp.float32
        )
        here = split(x[rows, :])
        totals = [here * weights[KL][None] for weights in rows_of]
        for k in range(KL):
            part = split(mixed[BLOCK * k : BLOCK * (k + 1), :])
            totals = [total + part * weights[k][None] for total, weights in zip(totals, rows_of)]
        for total, (_, finish) in zip(totals, sums):
            finish(rows, total.reshape(BLOCK, width))


def into(field, t, sign=0):
    ref, at = field[t]

    def finish(rows, total):
        if sign:
            total = ref[rows, at] + total if sign > 0 else ref[rows, at] - total
        ref[rows, at] = total

    return finish


def prep_kernel(own_ref, table_ref, coef, pc, links, core_step, near_step, far_step, pad):
    build_links(table_ref, links, pad)
    build_steps(core_step, near_step, far_step)
    coef[...] = slab_coefs(own_ref)
    for plane in range(2):
        at = slice(PLANE * plane, PLANE * (plane + 1))
        mix(links, plane_of(own_ref, plane), [((coef, at), into({plane: (pc, at)}, plane))])


def lo(n):
    return slice(PLANE * n, PLANE * (n + 1))


NEAR, FAR = slice(0, 128), slice(128, 256)
TAIL = slice(2 * PLANE, 2 * PLANE + 128)
FAR_TAIL = slice(2 * PLANE + 128, 2 * PLANE + 256)
NEAR_TAIL = slice(4 * PLANE, 4 * PLANE + 128)


def between_kernel(own_ref, inner_ref, coef_own, pc_own, links, core_step, near_step, far_step, coef_inner, ecoef, pc, qc, near):
    steps = (core_step, near_step, far_step)
    uf = {0: functools.partial(plane_of, inner_ref, 1), 1: functools.partial(plane_of, inner_ref, 0)}
    uf.update({2: functools.partial(plane_of, own_ref, 0), 3: functools.partial(plane_of, own_ref, 1)})
    near[...] = near_of(tile_of(inner_ref, CORE_TILES), tile_of(own_ref, CORE_TILES), None)
    uf["near"] = (near, NEAR)
    coef_inner[...] = slab_coefs(inner_ref)
    cf = {0: (coef_inner, lo(1)), 1: (coef_inner, lo(0)), 2: (coef_own, lo(0)), 3: (coef_own, lo(1))}
    cf["near"] = lambda: near_of(coef_inner[:, TAIL], coef_own[:, TAIL], None)
    ef = {t: (ecoef, lo(t - 1)) for t in (1, 2)}
    for t, x in neighbours(cf, (1, 2), False, steps, 3).items():
        put(ef, t, x + 6.0 * get(cf, t))
    pf = {t: (pc, lo(t)) for t in (0, 1)}
    qf = {t: (qc, lo(t - 1)) for t in (1, 2)}
    mix(links, get(uf, 1), [(cf[1], into(pf, 1)), (ef[1], into(qf, 1))])
    mix(links, get(uf, 2), [(ef[2], into(qf, 2))])
    mix(links, get(uf, 0), [(cf[0], into(pf, 0))])
    for t, x in neighbours(uf, (1, 2), False, steps).items():
        mix(links, x, [(cf[t], into(qf, t, -1))])


def step_kernel(own_ref, inner_ref, outer_ref, coef_own, pc_own, links, core_step, near_step, far_step, coef_inner, ecoef_known, pc_known, qc_known, out_ref, rims, coef_outer, coef_rims, ecoef, pc, qc, search, pc2, qc2, sol, res):
    steps = (core_step, near_step, far_step)
    uf = {}
    for t, (ref, plane) in enumerate(((inner_ref, 1), (inner_ref, 0), (own_ref, 0), (own_ref, 1), (outer_ref, 1), (outer_ref, 0))):
        uf[t] = functools.partial(plane_of, ref, plane)
    inner, own, outer = (tile_of(ref, CORE_TILES) for ref in (inner_ref, own_ref, outer_ref))
    rims[:, NEAR] = near_of(inner, own, outer)
    rims[:, FAR] = far_of(inner, outer)
    uf.update(near=(rims, NEAR), far=(rims, FAR))

    coef_outer[...] = slab_coefs(outer_ref)
    coef_rims[:, NEAR] = near_of(coef_inner[:, TAIL], coef_own[:, TAIL], coef_outer[:, TAIL])
    coef_rims[:, FAR] = far_of(coef_inner[:, TAIL], coef_outer[:, TAIL])
    cf = {0: (coef_inner, lo(1)), 1: (coef_inner, lo(0)), 2: (coef_own, lo(0)), 3: (coef_own, lo(1))}
    cf.update({4: (coef_outer, lo(1)), 5: (coef_outer, lo(0)), "near": (coef_rims, NEAR), "far": (coef_rims, FAR)})
    ef = {t: (ecoef_known, lo(t - 1)) for t in (1, 2)}
    ef.update({3: (ecoef, lo(0)), 4: (ecoef, lo(1)), "near": (ecoef, TAIL)})
    for t, x in neighbours(cf, (3, 4), True, steps, 3).items():
        put(ef, t, x + 6.0 * get(cf, t))
    ecoef[:, FAR_TAIL] = jnp.zeros((COEF_ROWS, 128), jnp.float32)

    pf = {0: (pc_known, lo(0)), 1: (pc_known, lo(1)), 2: (pc_own, lo(0)), 3: (pc_own, lo(1)), 4: (pc, lo(0)), 5: (pc, lo(1))}
    pf.update(near=(pc, TAIL), far=(pc, FAR_TAIL))
    qf = {1: (qc_known, lo(0)), 2: (qc_known, lo(1)), 3: (qc, lo(0)), 4: (qc, lo(1)), "near": (qc, TAIL)}
    all_rims = slice(TAIL.start, FAR_TAIL.stop)

    mix(links, get(uf, 3), [(ef[3], into(qf, 3))])
    mix(links, get(uf, 4), [(cf[4], into(pf, 4)), (ef[4], into(qf, 4))])
    mix(links, get(uf, 5), [(cf[5], into(pf, 5))])
    rim_sums = [((coef_rims, slice(0, 256)), pc), ((ecoef, all_rims), qc)]
    mix(links, rims[...], [(weights, into({0: (ref, all_rims)}, 0)) for weights, ref in rim_sums])
    for t, x in neighbours(uf, (3, 4), True, steps).items():
        mix(links, x, [(cf[t], into(qf, t, -1))])

    sigma = THETA / DELTA
    rho = 1.0 / sigma
    rho_next = 1.0 / (2.0 * sigma - rho)
    sf = {t: (search, lo(t - 1)) for t in (1, 2, 3, 4)}
    sf["near"] = (search, NEAR_TAIL)
    for t, x in neighbours(pf, (1, 2, 3, 4), True, steps).items():
        start = get(uf, t)
        au = start + 0.5 * (get(qf, t) - x)
        begin = start * (1.0 / THETA)
        r1 = start - au * (1.0 / THETA)
        new = (rho_next * rho) * begin + (2.0 * rho_next / DELTA) * r1
        new = jnp.where(cf[t][0][KL : KL + 1, cf[t][1]] > 0.0, new, 0.0)
        if t in (2, 3):
            res[:, lo(t - 2)] = r1
            sol[:, lo(t - 2)] = begin + new
        put(sf, t, new)

    pf = {t: (pc2, at) for t, (_, at) in sf.items()}
    qf = {t: (qc2, lo(t - 2)) for t in (2, 3)}
    for t in (2, 3, 1, 4, "near"):
        sums = [(cf[t], into(pf, t))]
        if t in (2, 3):
            sums.append((ef[t], into(qf, t)))
        mix(links, get(sf, t), sums)
    for t, x in neighbours(sf, (2, 3), False, steps).items():
        mix(links, x, [(cf[t], into(qf, t, -1))])
    for t, x in neighbours(pf, (2, 3), False, steps).items():
        res[:, lo(t - 2)] = res[:, lo(t - 2)] - (get(sf, t) + 0.5 * (get(qf, t) - x))
    for f, field in enumerate((sol, res)):
        for j in range(OUT_TILES):
            n = (f * OUT_TILES + j) * OWN
            out_ref[:, n : n + OWN, :] = field[:, 128 * j : 128 * (j + 1)].reshape(GROUPS, OWN, 128)


def unpack_kernel(in_ref, table_ref, sol_hbm, res_hbm, halves, sems):
    flip = 1 - lax.rem(lax.axis_index("space"), 2)
    scale = 1.0 / mode_scale(table_ref[...])
    lane = lanes((OWN, 128))
    per = 128 // ZC
    copies = []
    for f, hbm in enumerate((sol_hbm, res_hbm)):
        for h in range(NZ // 128):
            for p in range(ROWS):
                plane, y = p // NY, p % NY
                row = (plane + flip * (1 - 2 * plane)) * NY + y
                j, i = p // per, p % per
                tile = None
                for n in range(per):
                    w = in_ref[per * h + n, (f * OUT_TILES + j) * OWN : (f * OUT_TILES + j + 1) * OWN, :]
                    w = turn(w, ZC * (n - i))
                    tile = w if n == 0 else jnp.where(lane >= ZC * n, w, tile)
                halves[f, h, pl.ds(row, OWN, stride=ROWS), :] = tile * scale
            copy = pltpu.make_async_copy(halves.at[f, h], hbm.at[:, pl.ds(128 * h, 128)], sems.at[f, h])
            copy.start()
            copies.append(copy)
    for copy in copies:
        copy.wait()


def whole(count):
    return [pl.BlockSpec(memory_space=pltpu.VMEM)] * count


def anywhere(count):
    return [pl.BlockSpec(memory_space=pltpu.HBM)] * count


def body(load, mean_coeff, kl_ratio, chaos_table):
    params = pltpu.CompilerParams(vmem_limit_bytes=VMEM)
    f32, bf16 = jnp.float32, jnp.bfloat16
    vmem = pltpu.VMEM
    halves = NZ // 128
    table = chaos_table.T
    send = pl.pallas_call(
        pack_kernel,
        out_shape=jax.ShapeDtypeStruct((GROUPS, SEND_ROWS, 128), f32),
        in_specs=anywhere(4),
        out_specs=pl.BlockSpec(memory_space=vmem),
        scratch_shapes=[
            vmem((halves, OWN * ROWS, 128), f32),
            vmem((ROWS, NZ), f32),
            vmem((KL * ROWS, NZ), f32),
            vmem((KL, MODES), jnp.int32),
            pltpu.SemaphoreType.DMA((3 + halves,)),
        ],
        compiler_params=pltpu.CompilerParams(vmem_limit_bytes=PACK_VMEM),
        name="pack",
    )(load.reshape(OWN * ROWS, NZ), mean_coeff.reshape(ROWS, NZ), kl_ratio.reshape(KL * ROWS, NZ), table)
    own = lax.all_to_all(send, "mode", 0, 0, tiled=True)
    count = lax.axis_size("space")
    on_chip = [e for i in range(0, count, 2) for e in ((i, i + 1), (i + 1, i))]
    off_chip = [e for i in range(1, count - 1, 2) for e in ((i, i + 1), (i + 1, i))]
    outer = lax.ppermute(own, "space", off_chip)
    inner = lax.ppermute(own, "space", on_chip)
    shapes = [
        ((COEF_ROWS, 2 * PLANE + 128), f32),
        ((MODES, 2 * PLANE), f32),
        ((KL * MODES, 2 * MODES), bf16),
        ((PLANE, PLANE + 4 * 128), bf16),
        ((128, 4 * PLANE + 128), bf16),
        ((128, 128), bf16),
    ]
    state = pl.pallas_call(
        prep_kernel,
        out_shape=[jax.ShapeDtypeStruct(*shape) for shape in shapes],
        in_specs=whole(2),
        out_specs=whole(len(shapes)),
        scratch_shapes=[vmem((MODES, MODES), f32)],
        compiler_params=params,
        cost_estimate=pl.CostEstimate(flops=1 << 34, bytes_accessed=1 << 22, transcendentals=0),
        name="step_prep",
    )(own, table)
    more = [
        ((COEF_ROWS, 2 * PLANE + 128), f32),
        ((COEF_ROWS, 2 * PLANE), f32),
        ((MODES, 2 * PLANE), f32),
        ((MODES, 2 * PLANE), f32),
    ]
    between = pl.pallas_call(
        between_kernel,
        out_shape=[jax.ShapeDtypeStruct(*shape) for shape in more],
        in_specs=whole(2 + len(shapes)),
        out_specs=whole(len(more)),
        scratch_shapes=[vmem((MODES, 128), f32)],
        compiler_params=params,
        cost_estimate=pl.CostEstimate(flops=1 << 10, bytes_accessed=1 << 10, transcendentals=0),
        name="step_between",
    )(own, inner, *state)
    back = pl.pallas_call(
        step_kernel,
        out_shape=jax.ShapeDtypeStruct((GROUPS, 2 * OUT_TILES * OWN, 128), f32),
        in_specs=whole(3 + len(shapes) + len(more)),
        out_specs=pl.BlockSpec(memory_space=vmem),
        scratch_shapes=[
            vmem((MODES, 256), f32),
            vmem((COEF_ROWS, 2 * PLANE + 128), f32),
            vmem((COEF_ROWS, 256), f32),
            vmem((COEF_ROWS, 2 * PLANE + 256), f32),
            vmem((MODES, 2 * PLANE + 256), f32),
            vmem((MODES, 2 * PLANE + 256), f32),
        ]
        + [vmem((MODES, 4 * PLANE + 128), f32)] * 2
        + [vmem((MODES, 2 * PLANE), f32)] * 3,
        compiler_params=params,
        cost_estimate=pl.CostEstimate(flops=2 << 30, bytes_accessed=1 << 22, transcendentals=0),
        name="step",
    )(own, inner, outer, *state, *between)
    back = lax.all_to_all(back, "mode", 0, 0, tiled=True)
    flat = jax.ShapeDtypeStruct((OWN * ROWS, NZ), f32)
    sol, res = pl.pallas_call(
        unpack_kernel,
        out_shape=(flat, flat),
        in_specs=whole(2),
        out_specs=tuple(anywhere(2)),
        scratch_shapes=[vmem((2, halves, OWN * ROWS, 128), f32), pltpu.SemaphoreType.DMA((2, halves))],
        compiler_params=params,
        name="unpack",
    )(back, table)
    return sol.reshape(load.shape), res.reshape(load.shape)


def solution(mesh):
    in_specs = (
        P("mode", "space", None, None),
        P("space", None, None),
        P(None, "space", None, None),
        P(),
    )
    out_specs = (P("mode", "space", None, None), P("mode", "space", None, None))
    return jax.shard_map(body, mesh=mesh, in_specs=in_specs, out_specs=out_specs, check_vma=False)
```

```python
import functools

import jax
import jax.numpy as jnp
from jax import lax
from jax.experimental import pallas as pl
from jax.experimental.pallas import tpu as pltpu
from jax.sharding import PartitionSpec as P

ITERS = 2
THETA = 24.5
DELTA = 23.5
KL = 10
MODES = 128
GROUPS = 8
OWN = MODES // GROUPS
NX_OWN = 2
NY = 8
NZ = 256
ROWS = NX_OWN * NY
ZC = NZ // GROUPS
HALO = 2
PLANE = NY * ZC
CORE_TILES = NX_OWN * PLANE // 128
RIM = 2 * HALO
RIM_PLANE = NY * RIM
SPARE = NX_OWN * RIM_PLANE
TERMS = KL + 1
COEF_ROWS = 16
SEND_ROWS = (CORE_TILES + 1) * OWN
OUT_TILES = CORE_TILES
BLOCK = 32
SQRT2 = 2.0**0.5
SQRT6 = 6.0**0.5
VMEM = 40 * 1024 * 1024


def lanes(shape):
    return lax.broadcasted_iota(jnp.int32, shape, len(shape) - 1)


def mode_scale(t):
    f = jnp.where(t >= 3, SQRT6, jnp.where(t == 2, SQRT2, 1.0)).astype(jnp.float32)
    f = jnp.max(f, axis=0, keepdims=True)
    shape = (OWN, MODES)
    mine = lanes(shape) == lax.broadcasted_iota(jnp.int32, shape, 0) + OWN * lax.axis_index("mode")
    return jnp.sum(jnp.where(mine, f, 0.0), axis=1, keepdims=True)


def turn(x, by):
    by = by % x.shape[1]
    return pltpu.roll(x, by, 1) if by else x


def edges_of(tiles, at, lane):
    out = []
    for e in range(GROUPS + 1):
        z = ZC * e - HALO
        total = None
        for n, tile in enumerate(tiles):
            lo, hi = max(z, 128 * n), min(z + RIM, 128 * (n + 1))
            if lo >= hi:
                continue
            w = turn(tile, at - z)
            w = jnp.where((lane >= at + lo - z) & (lane < at + hi - z), w, 0.0)
            total = w if total is None else total + w
        out.append(total)
    return out


def pack_kernel(load_hbm, mean_hbm, ratio_hbm, table_hbm, out_ref, halves, mean_ref, ratio_ref, table_ref, sems):
    copies = [
        pltpu.make_async_copy(ratio_hbm, ratio_ref, sems.at[0]),
        pltpu.make_async_copy(mean_hbm, mean_ref, sems.at[1]),
        pltpu.make_async_copy(table_hbm, table_ref, sems.at[2]),
    ] + [
        pltpu.make_async_copy(load_hbm.at[:, pl.ds(128 * h, 128)], halves.at[h], sems.at[3 + h])
        for h in range(NZ // 128)
    ]
    for copy in copies:
        copy.start()
    me = lax.axis_index("mode")
    flip = 1 - lax.rem(lax.axis_index("space"), 2)
    lane = lanes((OWN, 128))
    per = 128 // ZC
    for copy in copies:
        copy.wait()
    scale = mode_scale(table_ref[...])

    def row_of(p):
        plane, y = p // NY, lax.rem(p, NY)
        return (plane + flip * (1 - 2 * plane)) * NY + y

    coefs = []
    for i in range(2):
        row = row_of(2 * me + i)
        mean = mean_ref[pl.ds(row, 1), :]
        terms = [mean * ratio_ref[pl.ds(row + k * ROWS, 1), :] for k in range(KL)] + [mean]
        zero = jnp.zeros_like(mean)
        low = jnp.concatenate(terms + terms[:5], axis=0)
        mid = jnp.concatenate([zero] * 11 + terms[5:10], axis=0)
        top = jnp.concatenate([zero] * 11 + terms[10:] + [zero] * 4, axis=0)
        coefs.append([(c[:, :128], c[:, 128:]) for c in (low, mid, top)])
    lane8 = lanes((8, 128))
    sub8 = lax.broadcasted_iota(jnp.int32, (8, 128), 0)
    first = lax.rem(lane8, RIM) < HALO
    borders = [jnp.zeros((8, 128), jnp.float32)] * (GROUPS + 1)
    for i in range(2):
        for g in range(3):
            tiles = [c[8:, :] for c in coefs[i][g]]
            more = edges_of(tiles, SPARE + 2 * RIM * g + RIM * i, lane8)
            borders = [x + y for x, y in zip(borders, more)]
    base = []
    for d in range(GROUPS):
        own_cells = []
        for i in range(2):
            w = turn(coefs[i][0][d // per], SPARE + ZC * i - ZC * (d % per))
            own_cells.append(jnp.where((lane >= SPARE + ZC * i) & (lane < SPARE + ZC * (i + 1)), w, 0.0))
        own_cells = own_cells[0] + own_cells[1]
        low = jnp.where(sub8 < TERMS - 8, own_cells[8:, :], jnp.where(first, borders[d], borders[d + 1]))
        base.append(jnp.concatenate([own_cells[:8, :], low], axis=0))

    first = lax.rem(lane, RIM) < HALO
    borders = [jnp.zeros((OWN, 128), jnp.float32)] * (GROUPS + 1)
    for j in range(CORE_TILES):
        rows = []
        for i in range(per):
            row = row_of(jnp.int32(per * j + i))
            rows.append([halves[h, pl.ds(row, OWN, stride=ROWS), :] * scale for h in range(NZ // 128)])
            more = edges_of(rows[i], RIM * (per * j + i), lane)
            borders = [x + y for x, y in zip(borders, more)]
        for d in range(GROUPS):
            tile = None
            for i in range(per):
                w = turn(rows[i][d // per], ZC * (i - d % per))
                tile = w if i == 0 else jnp.where(lane >= ZC * i, w, tile)
            out_ref[d, OWN * j : OWN * (j + 1), :] = tile
    for d in range(GROUPS):
        out_ref[d, CORE_TILES * OWN :, :] = base[d] + jnp.where(first, borders[d], borders[d + 1])


def build_links(table_ref, links, pad):
    pad[...] = jnp.zeros_like(pad)
    pad[:KL, :] = table_ref[...].astype(jnp.float32)
    cols = pad[...]
    rows = jnp.transpose(cols)
    apart = jnp.zeros((MODES, MODES), jnp.float32)
    for k in range(KL):
        apart = apart + jnp.abs(rows[:, k : k + 1] - cols[k : k + 1, :])
    near = apart == 1.0
    for k in range(KL):
        mine = rows[:, k : k + 1]
        d = mine - cols[k : k + 1, :]
        t = jnp.where(near, jnp.where(d == -1.0, 1.0, jnp.where(d == 1.0, mine + jnp.zeros_like(d), 0.0)), 0.0)
        t = t.astype(jnp.bfloat16)
        for b in range(MODES // BLOCK):
            at = (KL * b + k) * BLOCK
            links[at : at + BLOCK, :MODES] = t[BLOCK * b : BLOCK * (b + 1), :]
            links[at : at + BLOCK, MODES:] = t[BLOCK * b : BLOCK * (b + 1), :]


def core_cell(l):
    return lax.div(l, ZC), lax.rem(l, ZC)


def rim_cell(l):
    zi = lax.rem(l, RIM)
    return lax.rem(lax.div(l, RIM), NY), jnp.where(zi < HALO, zi - HALO, zi + ZC - HALO)


def grid_of(shape, rows_of, cols_of):
    a = rows_of(lax.broadcasted_iota(jnp.int32, shape, 0))
    b = cols_of(lax.broadcasted_iota(jnp.int32, shape, 1))
    return sum(jnp.abs(x - y) for x, y in zip(a, b))


def build_steps(core_step, near_step, far_step):
    def fill(ref, to, apart, times=1):
        for n in range(times):
            ref[apart.shape[0] * n : apart.shape[0] * (n + 1), to : to + apart.shape[1]] = jnp.where(
                apart == 1, 1.0, 0.0
            ).astype(jnp.bfloat16)

    fill(core_step, 0, grid_of((PLANE, PLANE), core_cell, core_cell))
    for t in range(4):

        def rim_at(l, t=t):
            y, z = rim_cell(l)
            return y + jnp.where(lax.div(l, RIM_PLANE) == t, 0, 100), z

        fill(core_step, PLANE + 128 * t, grid_of((PLANE, 128), core_cell, rim_at))
        fill(near_step, PLANE * t, grid_of((128, PLANE), rim_at, core_cell), 2)

    def near(l):
        return (lax.div(l, RIM_PLANE) + 1,) + rim_cell(l)

    def far(l):
        t = lax.div(l, RIM_PLANE)
        return (jnp.where(t == 0, 5, jnp.where(t == 1, 0, 100)),) + rim_cell(l)

    fill(near_step, 4 * PLANE, grid_of((128, 128), near, near), 2)
    fill(far_step, 0, grid_of((128, 128), far, near), 2)


def tile_of(ref, j):
    return ref[:, OWN * j : OWN * (j + 1), :].reshape(MODES, 128)


def plane_of(ref, plane):
    half = PLANE // 128
    return jnp.concatenate([tile_of(ref, half * plane + h) for h in range(half)], axis=1)


def near_of(inner, own, outer):
    lane = lanes(own.shape)
    out = jnp.where((lane >= RIM_PLANE) & (lane < 3 * RIM_PLANE), turn(own, RIM_PLANE), 0.0)
    if inner is not None:
        out = jnp.where(lane < RIM_PLANE, inner, out)
    if outer is not None:
        out = jnp.where(lane < 3 * RIM_PLANE, out, turn(outer, 2 * RIM_PLANE))
    return out


def far_of(inner, outer):
    lane = lanes((inner if outer is None else outer).shape)
    inner = 0.0 if inner is None else inner
    outer = 0.0 if outer is None else outer
    return jnp.where(lane < RIM_PLANE, outer, jnp.where(lane < 2 * RIM_PLANE, inner, 0.0))


def slab_coefs(ref):
    lane = lanes((OWN, 128))
    raw = [ref[m, CORE_TILES * OWN :, :] for m in range(GROUPS)]
    core = [jnp.where(lane < SPARE, turn(raw[2 * j], -SPARE), raw[2 * j + 1]) for j in range(CORE_TILES)]
    lane8 = lanes((8, 128))
    parts = []
    for g in range(3):
        total = jnp.zeros((8, 128), jnp.float32)
        for m in range(GROUPS):
            lo = 2 * RIM * m
            w = turn(raw[m][8:, :], lo - SPARE - 2 * RIM * g)
            total = jnp.where((lane8 >= lo) & (lane8 < lo + 2 * RIM), w, total)
        parts.append(total[3:, :])
    rim = jnp.concatenate(parts + [jnp.zeros((1, 128), jnp.float32)], axis=0)
    return jnp.concatenate(core + [rim], axis=1)


def parts_of(x, count, axis=0):
    out = []
    for _ in range(count - 1):
        h = x.astype(jnp.bfloat16)
        out.append(h)
        x = x - h.astype(jnp.float32)
    return jnp.concatenate(out + [x.astype(jnp.bfloat16)], axis=axis)


def get(field, t):
    part = field[t]
    return part() if callable(part) else part[0][:, part[1]]


def put(field, t, x):
    ref, at = field[t]
    ref[:, at] = x


def product(x, matrix, parts=2):
    out = jnp.dot(parts_of(x, parts), matrix, preferred_element_type=jnp.float32)
    return sum(out[x.shape[0] * i : x.shape[0] * (i + 1)] for i in range(parts))


def from_rim(x, matrix):
    return jnp.dot(parts_of(x, 2, 1), matrix, preferred_element_type=jnp.float32)


def to_rim(x, t, core_step, parts=2):
    return product(x, core_step[:, PLANE + 128 * (t - 1) : PLANE + 128 * t], parts)


def neighbours(src, slots, steps, begun={}):
    core_step, near_step, far_step = steps
    out = {}
    near = get(src, "near")
    for t in slots:
        if t == "near":
            x = begun[t] + from_rim(near, near_step[:, 4 * PLANE :]) + from_rim(get(src, "far"), far_step[...])
            out[t] = x + to_rim(get(src, 4), 4, core_step)
        else:
            x = begun[t] if t in begun else product(get(src, t), core_step[:, :PLANE])
            x = x + from_rim(near, near_step[:, PLANE * (t - 1) : PLANE * t])
            out[t] = x + (get(src, t - 1) + get(src, t + 1))
    return out


def sum_coefs(dst, src, slots, rims, steps):
    core_step, near_step, far_step = steps
    near = get(src, "near")
    for t in slots:
        x = product(get(src, t), core_step[:, :PLANE], 3)
        x = x + product(near, near_step[:128, PLANE * (t - 1) : PLANE * t], 3)
        put(dst, t, x + (get(src, t - 1) + get(src, t + 1)) + 6.0 * get(src, t))
    if rims:
        x = product(near, near_step[:128, 4 * PLANE :], 3) + product(get(src, "far"), far_step[:128, :], 3)
        for t in (1, 2, 3, 4):
            x = x + to_rim(get(src, t), t, core_step, 3)
        put(dst, "near", x + 6.0 * near)


def mix(links, x, sums, kept=None, known=None):
    width = x.shape[1]
    pair = parts_of(x, 2) if known is None else None
    rows_of = [
        [jnp.broadcast_to(ref[k : k + 1, at], (8, width)) for k in range(TERMS)] for (ref, at), _ in sums
    ]
    split = lambda x: x.reshape(BLOCK // 8, 8, width)
    for b in range(MODES // BLOCK):
        rows = slice(BLOCK * b, BLOCK * (b + 1))
        at = slice(KL * BLOCK * b, KL * BLOCK * (b + 1))
        if known is None:
            mixed = jnp.dot(links[at, :], pair, preferred_element_type=jnp.float32)
        else:
            mixed = known[at, :]
        if kept is not None:
            kept[at, :] = mixed
        here = split(x[rows, :])
        totals = [here * weights[KL][None] for weights in rows_of]
        for k in range(KL):
            part = split(mixed[BLOCK * k : BLOCK * (k + 1), :])
            totals = [total + part * weights[k][None] for total, weights in zip(totals, rows_of)]
        for total, (_, finish) in zip(totals, sums):
            finish(rows, total.reshape(BLOCK, width))


def into(field, t, sign=0):
    ref, at = field[t]

    def finish(rows, total):
        if sign:
            total = ref[rows, at] + total if sign > 0 else ref[rows, at] - total
        ref[rows, at] = total

    return finish


def prep_kernel(own_ref, table_ref, coef, pc, mix3, links, core_step, near_step, far_step, pad):
    build_links(table_ref, links, pad)
    build_steps(core_step, near_step, far_step)
    coef[...] = slab_coefs(own_ref)
    for plane, kept in ((0, None), (1, mix3)):
        at = slice(PLANE * plane, PLANE * (plane + 1))
        mix(links, plane_of(own_ref, plane), [((coef, at), into({plane: (pc, at)}, plane))], kept)


def lo(n):
    return slice(PLANE * n, PLANE * (n + 1))


NEAR, FAR = slice(0, 128), slice(128, 256)
TAIL = slice(2 * PLANE, 2 * PLANE + 128)
FAR_TAIL = slice(2 * PLANE + 128, 2 * PLANE + 256)
BEGUN_U, BEGUN_P = slice(3 * PLANE, 3 * PLANE + 128), slice(3 * PLANE + 128, 3 * PLANE + 256)
NEAR_TAIL = slice(4 * PLANE, 4 * PLANE + 128)


def between_kernel(own_ref, inner_ref, coef_own, pc_own, mix3, links, core_step, near_step, far_step, coef_inner, ecoef, pc, qc, near, begun):
    steps = (core_step, near_step, far_step)
    uf = {0: functools.partial(plane_of, inner_ref, 1), 1: functools.partial(plane_of, inner_ref, 0)}
    uf.update({2: functools.partial(plane_of, own_ref, 0), 3: functools.partial(plane_of, own_ref, 1)})
    inner = tile_of(inner_ref, CORE_TILES)
    near[...] = near_of(inner, tile_of(own_ref, CORE_TILES), None)
    uf["near"] = (near, NEAR)
    uf[4] = lambda: jnp.zeros((MODES, PLANE), jnp.float32)
    coef_inner[...] = slab_coefs(inner_ref)
    cf = {0: (coef_inner, lo(1)), 1: (coef_inner, lo(0)), 2: (coef_own, lo(0)), 3: (coef_own, lo(1))}
    cf["near"] = lambda: near_of(coef_inner[:, TAIL], coef_own[:, TAIL], None)
    ef = {t: (ecoef, lo(t - 1)) for t in (1, 2)}
    sum_coefs(ef, cf, (1, 2), False, steps)
    pf = {0: (pc, lo(0)), 1: (pc, lo(1)), 2: (pc_own, lo(0)), 3: (pc_own, lo(1))}
    qf = {t: (qc, lo(t - 1)) for t in (1, 2, 3)}
    mix(links, get(uf, 1), [(cf[1], into(pf, 1)), (ef[1], into(qf, 1))])
    mix(links, get(uf, 2), [(ef[2], into(qf, 2))])
    mix(links, get(uf, 0), [(cf[0], into(pf, 0))])
    qc[:, lo(2)] = jnp.zeros((MODES, PLANE), jnp.float32)
    for t, x in neighbours(uf, (1, 2, 3), steps).items():
        mix(links, x, [(cf[t], into(qf, t, -1))])
    rim = from_rim(near[...], near_step[:, 4 * PLANE :]) + from_rim(far_of(inner, None), far_step[...])
    for t in (1, 2, 3):
        rim = rim + to_rim(get(uf, t), t, core_step)
    begun[:, BEGUN_U] = rim
    rim = jnp.zeros((MODES, 128), jnp.float32)
    for t in (1, 2, 3):
        x = get(pf, t)
        begun[:, lo(t - 1)] = product(x, core_step[:, :PLANE])
        rim = rim + to_rim(x, t, core_step)
    begun[:, BEGUN_P] = rim


def step_kernel(own_ref, inner_ref, outer_ref, coef_own, pc_own, mix3, links, core_step, near_step, far_step, coef_inner, ecoef_known, pc_known, qc_known, near_known, begun, out_ref, rims, coef_outer, coef_rims, ecoef, pc, qc, search, pc2, qc2, sol, res):
    steps = (core_step, near_step, far_step)
    uf = {}
    for t, (ref, plane) in enumerate(((inner_ref, 1), (inner_ref, 0), (own_ref, 0), (own_ref, 1), (outer_ref, 1), (outer_ref, 0))):
        uf[t] = functools.partial(plane_of, ref, plane)
    inner, outer = tile_of(inner_ref, CORE_TILES), tile_of(outer_ref, CORE_TILES)
    near_new = jnp.where(lanes((MODES, 128)) < 3 * RIM_PLANE, 0.0, turn(outer, 2 * RIM_PLANE))
    rims[:, NEAR] = near_known[...] + near_new
    rims[:, FAR] = far_of(inner, outer)
    uf.update(near=(rims, NEAR), far=(rims, FAR))

    coef_outer[...] = slab_coefs(outer_ref)
    coef_rims[:, NEAR] = near_of(coef_inner[:, TAIL], coef_own[:, TAIL], coef_outer[:, TAIL])
    coef_rims[:, FAR] = far_of(coef_inner[:, TAIL], coef_outer[:, TAIL])
    cf = {0: (coef_inner, lo(1)), 1: (coef_inner, lo(0)), 2: (coef_own, lo(0)), 3: (coef_own, lo(1))}
    cf.update({4: (coef_outer, lo(1)), 5: (coef_outer, lo(0)), "near": (coef_rims, NEAR), "far": (coef_rims, FAR)})
    ef = {t: (ecoef_known, lo(t - 1)) for t in (1, 2)}
    ef.update({3: (ecoef, lo(0)), 4: (ecoef, lo(1)), "near": (ecoef, TAIL)})

    pf = {0: (pc_known, lo(0)), 1: (pc_known, lo(1)), 2: (pc_own, lo(0)), 3: (pc_own, lo(1)), 4: (pc, lo(0)), 5: (pc, lo(1))}
    pf.update(near=(pc, TAIL), far=(pc, FAR_TAIL))
    qf = {1: (qc_known, lo(0)), 2: (qc_known, lo(1)), 3: (qc, lo(0)), 4: (qc, lo(1)), "near": (qc, TAIL)}
    all_rims = slice(TAIL.start, FAR_TAIL.stop)
    qc[:, lo(0)] = qc_known[:, lo(2)]
    mix(links, get(uf, 5), [(cf[5], into(pf, 5))])
    sum_coefs(ef, cf, (3, 4), True, steps)
    ecoef[:, FAR_TAIL] = jnp.zeros((COEF_ROWS, 128), jnp.float32)
    around = neighbours(uf, (4,), steps)[4]
    x = begun[:, BEGUN_U] + to_rim(get(uf, 4), 4, core_step)
    around_near = x + from_rim(near_new, near_step[:, 4 * PLANE :]) + from_rim(far_of(None, outer), far_step[...])
    rim_sums = [((coef_rims, slice(0, 256)), pc), ((ecoef, all_rims), qc)]
    mix(links, rims[...], [(weights, into({0: (ref, all_rims)}, 0)) for weights, ref in rim_sums])
    mix(links, get(uf, 4), [(cf[4], into(pf, 4)), (ef[4], into(qf, 4)), (cf[3], into(qf, 3, -1))])
    known = {t: begun[:, lo(t - 1)] for t in (1, 2, 3)}
    known["near"] = begun[:, BEGUN_P]
    around_p = neighbours(pf, (1, 2, 3, 4, "near"), steps, known)
    mix(links, around, [(cf[4], into(qf, 4, -1))])
    mix(links, around_near, [(cf["near"], into(qf, "near", -1))])
    mix(links, get(uf, 3), [(ef[3], into(qf, 3, 1))], known=mix3)

    sigma = THETA / DELTA
    rho = 1.0 / sigma
    rho_next = 1.0 / (2.0 * sigma - rho)
    sf = {t: (search, lo(t - 1)) for t in (1, 2, 3, 4)}
    sf["near"] = (search, NEAR_TAIL)
    for t, x in around_p.items():
        start = get(uf, t)
        au = start + 0.5 * (get(qf, t) - x)
        begin = start * (1.0 / THETA)
        r1 = start - au * (1.0 / THETA)
        new = (rho_next * rho) * begin + (2.0 * rho_next / DELTA) * r1
        new = jnp.where(cf[t][0][KL : KL + 1, cf[t][1]] > 0.0, new, 0.0)
        if t in (2, 3):
            res[:, lo(t - 2)] = r1
            sol[:, lo(t - 2)] = begin + new
        put(sf, t, new)

    pf = {t: (pc2, at) for t, (_, at) in sf.items()}
    qf = {t: (qc2, lo(t - 2)) for t in (2, 3)}
    around = neighbours(sf, (2, 3), steps)
    for t in (1, 2, 3, 4, "near"):
        sums = [(cf[t], into(pf, t))]
        if t in (2, 3):
            sums.append((ef[t], into(qf, t)))
        mix(links, get(sf, t), sums)
    around_p = neighbours(pf, (2, 3), steps)
    for t, x in around.items():
        mix(links, x, [(cf[t], into(qf, t, -1))])
    for t, x in around_p.items():
        res[:, lo(t - 2)] = res[:, lo(t - 2)] - (get(sf, t) + 0.5 * (get(qf, t) - x))
    for f, field in enumerate((sol, res)):
        for j in range(OUT_TILES):
            n = (f * OUT_TILES + j) * OWN
            out_ref[:, n : n + OWN, :] = field[:, 128 * j : 128 * (j + 1)].reshape(GROUPS, OWN, 128)


def unpack_kernel(in_ref, table_ref, sol_hbm, res_hbm, halves, sems):
    flip = 1 - lax.rem(lax.axis_index("space"), 2)
    scale = 1.0 / mode_scale(table_ref[...])
    lane = lanes((OWN, 128))
    per = 128 // ZC
    copies = []
    for f, hbm in enumerate((sol_hbm, res_hbm)):
        for h in range(NZ // 128):
            for p in range(ROWS):
                plane, y = p // NY, p % NY
                row = (plane + flip * (1 - 2 * plane)) * NY + y
                j, i = p // per, p % per
                tile = None
                for n in range(per):
                    w = in_ref[per * h + n, (f * OUT_TILES + j) * OWN : (f * OUT_TILES + j + 1) * OWN, :]
                    w = turn(w, ZC * (n - i))
                    tile = w if n == 0 else jnp.where(lane >= ZC * n, w, tile)
                halves[f, h, pl.ds(row, OWN, stride=ROWS), :] = tile * scale
            copy = pltpu.make_async_copy(halves.at[f, h], hbm.at[:, pl.ds(128 * h, 128)], sems.at[f, h])
            copy.start()
            copies.append(copy)
    for copy in copies:
        copy.wait()


def whole(count):
    return [pl.BlockSpec(memory_space=pltpu.VMEM)] * count


def anywhere(count):
    return [pl.BlockSpec(memory_space=pltpu.HBM)] * count


def body(load, mean_coeff, kl_ratio, chaos_table):
    params = pltpu.CompilerParams(vmem_limit_bytes=VMEM)
    f32, bf16 = jnp.float32, jnp.bfloat16
    vmem = pltpu.VMEM
    halves = NZ // 128
    table = chaos_table.T
    send = pl.pallas_call(
        pack_kernel,
        out_shape=jax.ShapeDtypeStruct((GROUPS, SEND_ROWS, 128), f32),
        in_specs=anywhere(4),
        out_specs=pl.BlockSpec(memory_space=vmem),
        scratch_shapes=[
            vmem((halves, OWN * ROWS, 128), f32),
            vmem((ROWS, NZ), f32),
            vmem((KL * ROWS, NZ), f32),
            vmem((KL, MODES), jnp.int32),
            pltpu.SemaphoreType.DMA((3 + halves,)),
        ],
        compiler_params=pltpu.CompilerParams(vmem_limit_bytes=VMEM),
        name="pack",
    )(*(pltpu.with_memory_space_constraint(x, pltpu.HBM) for x in (load.reshape(OWN * ROWS, NZ), mean_coeff.reshape(ROWS, NZ), kl_ratio.reshape(KL * ROWS, NZ), table)))
    own = lax.all_to_all(send, "mode", 0, 0, tiled=True)
    count = lax.axis_size("space")
    on_chip = [e for i in range(0, count, 2) for e in ((i, i + 1), (i + 1, i))]
    off_chip = [e for i in range(1, count - 1, 2) for e in ((i, i + 1), (i + 1, i))]
    outer = lax.ppermute(own, "space", off_chip)
    inner = lax.ppermute(own, "space", on_chip)
    shapes = [
        ((COEF_ROWS, 2 * PLANE + 128), f32),
        ((MODES, 2 * PLANE), f32),
        ((KL * MODES, PLANE), f32),
        ((KL * MODES, 2 * MODES), bf16),
        ((PLANE, PLANE + 4 * 128), bf16),
        ((256, 4 * PLANE + 128), bf16),
        ((256, 128), bf16),
    ]
    state = pl.pallas_call(
        prep_kernel,
        out_shape=[jax.ShapeDtypeStruct(*shape) for shape in shapes],
        in_specs=whole(2),
        out_specs=whole(len(shapes)),
        scratch_shapes=[vmem((MODES, MODES), f32)],
        compiler_params=params,
        cost_estimate=pl.CostEstimate(flops=1 << 34, bytes_accessed=1 << 22, transcendentals=0),
        name="step_prep",
    )(own, table)
    more = [
        ((COEF_ROWS, 2 * PLANE + 128), f32),
        ((COEF_ROWS, 2 * PLANE), f32),
        ((MODES, 2 * PLANE), f32),
        ((MODES, 3 * PLANE), f32),
        ((MODES, 128), f32),
        ((MODES, 3 * PLANE + 256), f32),
    ]
    between = pl.pallas_call(
        between_kernel,
        out_shape=[jax.ShapeDtypeStruct(*shape) for shape in more],
        in_specs=whole(2 + len(shapes)),
        out_specs=whole(len(more)),
        compiler_params=params,
        cost_estimate=pl.CostEstimate(flops=1 << 10, bytes_accessed=1 << 10, transcendentals=0),
        name="step_between",
    )(own, inner, *state)
    back = pl.pallas_call(
        step_kernel,
        out_shape=jax.ShapeDtypeStruct((GROUPS, 2 * OUT_TILES * OWN, 128), f32),
        in_specs=whole(3 + len(shapes) + len(more)),
        out_specs=pl.BlockSpec(memory_space=vmem),
        scratch_shapes=[
            vmem((MODES, 256), f32),
            vmem((COEF_ROWS, 2 * PLANE + 128), f32),
            vmem((COEF_ROWS, 256), f32),
            vmem((COEF_ROWS, 2 * PLANE + 256), f32),
            vmem((MODES, 2 * PLANE + 256), f32),
            vmem((MODES, 2 * PLANE + 256), f32),
        ]
        + [vmem((MODES, 4 * PLANE + 128), f32)] * 2
        + [vmem((MODES, 2 * PLANE), f32)] * 3,
        compiler_params=params,
        cost_estimate=pl.CostEstimate(flops=2 << 30, bytes_accessed=1 << 22, transcendentals=0),
        name="step",
    )(own, inner, outer, *state, *between)
    back = lax.all_to_all(back, "mode", 0, 0, tiled=True)
    flat = jax.ShapeDtypeStruct((OWN * ROWS, NZ), f32)
    sol, res = pl.pallas_call(
        unpack_kernel,
        out_shape=(flat, flat),
        in_specs=whole(2),
        out_specs=tuple(anywhere(2)),
        scratch_shapes=[vmem((2, halves, OWN * ROWS, 128), f32), pltpu.SemaphoreType.DMA((2, halves))],
        compiler_params=params,
        name="unpack",
    )(back, table)
    return sol.reshape(load.shape), res.reshape(load.shape)


def solution(mesh):
    in_specs = (
        P("mode", "space", None, None),
        P("space", None, None),
        P(None, "space", None, None),
        P(),
    )
    out_specs = (P("mode", "space", None, None), P("mode", "space", None, None))
    return jax.shard_map(body, mesh=mesh, in_specs=in_specs, out_specs=out_specs, check_vma=False)
```

```python
import functools

import jax
import jax.numpy as jnp
from jax import lax
from jax.experimental import pallas as pl
from jax.experimental.pallas import tpu as pltpu
from jax.sharding import PartitionSpec as P

ITERS = 2
THETA = 24.5
DELTA = 23.5
KL = 10
MODES = 128
GROUPS = 8
OWN = MODES // GROUPS
NX_OWN = 2
NY = 8
NZ = 256
ROWS = NX_OWN * NY
ZC = NZ // GROUPS
HALO = 2
PLANE = NY * ZC
CORE_TILES = NX_OWN * PLANE // 128
RIM = 2 * HALO
RIM_PLANE = NY * RIM
SPARE = NX_OWN * RIM_PLANE
TERMS = KL + 1
COEF_ROWS = 16
SEND_ROWS = (CORE_TILES + 1) * OWN
OUT_TILES = CORE_TILES
BLOCK = 32
SQRT2 = 2.0**0.5
SQRT6 = 6.0**0.5
VMEM = 40 * 1024 * 1024


def lanes(shape):
    return lax.broadcasted_iota(jnp.int32, shape, len(shape) - 1)


def mode_scale(t):
    f = jnp.where(t >= 3, SQRT6, jnp.where(t == 2, SQRT2, 1.0)).astype(jnp.float32)
    f = jnp.max(f, axis=0, keepdims=True)
    shape = (OWN, MODES)
    mine = lanes(shape) == lax.broadcasted_iota(jnp.int32, shape, 0) + OWN * lax.axis_index("mode")
    return jnp.sum(jnp.where(mine, f, 0.0), axis=1, keepdims=True)


def turn(x, by):
    by = by % x.shape[1]
    return pltpu.roll(x, by, 1) if by else x


def edges_of(tiles, at, lane):
    out = []
    for e in range(GROUPS + 1):
        z = ZC * e - HALO
        total = None
        for n, tile in enumerate(tiles):
            lo, hi = max(z, 128 * n), min(z + RIM, 128 * (n + 1))
            if lo >= hi:
                continue
            w = turn(tile, at - z)
            w = jnp.where((lane >= at + lo - z) & (lane < at + hi - z), w, 0.0)
            total = w if total is None else total + w
        out.append(total)
    return out


def pack_kernel(load_hbm, mean_hbm, ratio_hbm, table_hbm, out_ref, halves, mean_ref, ratio_ref, table_ref, sems):
    copies = [
        pltpu.make_async_copy(ratio_hbm, ratio_ref, sems.at[0]),
        pltpu.make_async_copy(mean_hbm, mean_ref, sems.at[1]),
        pltpu.make_async_copy(table_hbm, table_ref, sems.at[2]),
    ] + [
        pltpu.make_async_copy(load_hbm.at[:, pl.ds(128 * h, 128)], halves.at[h], sems.at[3 + h])
        for h in range(NZ // 128)
    ]
    for copy in copies:
        copy.start()
    me = lax.axis_index("mode")
    flip = 1 - lax.rem(lax.axis_index("space"), 2)
    lane = lanes((OWN, 128))
    per = 128 // ZC
    for copy in copies[:2]:
        copy.wait()

    def row_of(p):
        plane, y = p // NY, lax.rem(p, NY)
        return (plane + flip * (1 - 2 * plane)) * NY + y

    coefs = []
    for i in range(2):
        row = row_of(2 * me + i)
        mean = mean_ref[pl.ds(row, 1), :]
        terms = [mean * ratio_ref[pl.ds(row + k * ROWS, 1), :] for k in range(KL)] + [mean]
        zero = jnp.zeros_like(mean)
        low = jnp.concatenate(terms + terms[:5], axis=0)
        mid = jnp.concatenate([zero] * 11 + terms[5:10], axis=0)
        top = jnp.concatenate([zero] * 11 + terms[10:] + [zero] * 4, axis=0)
        coefs.append([(c[:, :128], c[:, 128:]) for c in (low, mid, top)])
    lane8 = lanes((8, 128))
    sub8 = lax.broadcasted_iota(jnp.int32, (8, 128), 0)
    first = (lane8 & (RIM - 1)) < HALO
    borders = [jnp.zeros((8, 128), jnp.float32)] * (GROUPS + 1)
    for i in range(2):
        for g in range(3):
            tiles = [c[8:, :] for c in coefs[i][g]]
            more = edges_of(tiles, SPARE + 2 * RIM * g + RIM * i, lane8)
            borders = [x + y for x, y in zip(borders, more)]
    base = []
    for d in range(GROUPS):
        own_cells = []
        for i in range(2):
            w = turn(coefs[i][0][d // per], SPARE + ZC * i - ZC * (d % per))
            own_cells.append(jnp.where((lane >= SPARE + ZC * i) & (lane < SPARE + ZC * (i + 1)), w, 0.0))
        own_cells = own_cells[0] + own_cells[1]
        low = jnp.where(sub8 < TERMS - 8, own_cells[8:, :], jnp.where(first, borders[d], borders[d + 1]))
        base.append(jnp.concatenate([own_cells[:8, :], low], axis=0))

    for copy in copies[2:]:
        copy.wait()
    scale = mode_scale(table_ref[...])
    first = (lane & (RIM - 1)) < HALO
    borders = [jnp.zeros((OWN, 128), jnp.float32)] * (GROUPS + 1)
    for j in range(CORE_TILES):
        rows = []
        for i in range(per):
            row = row_of(jnp.int32(per * j + i))
            rows.append([halves[h, pl.ds(row, OWN, stride=ROWS), :] * scale for h in range(NZ // 128)])
            more = edges_of(rows[i], RIM * (per * j + i), lane)
            borders = [x + y for x, y in zip(borders, more)]
        for d in range(GROUPS):
            tile = None
            for i in range(per):
                w = turn(rows[i][d // per], ZC * (i - d % per))
                tile = w if i == 0 else jnp.where(lane >= ZC * i, w, tile)
            out_ref[d, OWN * j : OWN * (j + 1), :] = tile
    for d in range(GROUPS):
        out_ref[d, CORE_TILES * OWN :, :] = base[d] + jnp.where(first, borders[d], borders[d + 1])


def build_links(table_ref, links, pad):
    pad[...] = jnp.zeros_like(pad)
    pad[:KL, :] = table_ref[...].astype(jnp.float32)
    cols = pad[...]
    rows = jnp.transpose(cols)
    apart = jnp.zeros((MODES, MODES), jnp.float32)
    for k in range(KL):
        apart = apart + jnp.abs(rows[:, k : k + 1] - cols[k : k + 1, :])
    near = apart == 1.0
    for k in range(KL):
        mine = rows[:, k : k + 1]
        d = mine - cols[k : k + 1, :]
        t = jnp.where(near, jnp.where(d == -1.0, 1.0, jnp.where(d == 1.0, mine + jnp.zeros_like(d), 0.0)), 0.0)
        t = t.astype(jnp.bfloat16)
        for b in range(MODES // BLOCK):
            at = (KL * b + k) * BLOCK
            links[at : at + BLOCK, :MODES] = t[BLOCK * b : BLOCK * (b + 1), :]
            links[at : at + BLOCK, MODES:] = t[BLOCK * b : BLOCK * (b + 1), :]


def core_cell(l):
    return l >> 5, l & (ZC - 1)


def rim_cell(l):
    zi = l & (RIM - 1)
    return (l >> 2) & (NY - 1), jnp.where(zi < HALO, zi - HALO, zi + ZC - HALO)


def grid_of(shape, rows_of, cols_of):
    a = rows_of(lax.broadcasted_iota(jnp.int32, shape, 0))
    b = cols_of(lax.broadcasted_iota(jnp.int32, shape, 1))
    return sum(jnp.abs(x - y) for x, y in zip(a, b))


def build_steps(core_step, near_step):
    def fill(ref, to, apart, times=1):
        for n in range(times):
            ref[apart.shape[0] * n : apart.shape[0] * (n + 1), to : to + apart.shape[1]] = jnp.where(
                apart == 1, 1.0, 0.0
            ).astype(jnp.bfloat16)

    fill(core_step, 0, grid_of((PLANE, PLANE), core_cell, core_cell))
    for t in (1, 2, 3, 4):

        def rim_at(l, t=t):
            y, z = rim_cell(l)
            return y + jnp.where((l >> 5) == t - 1, 0, 100), z

        if t in (2, 3):
            fill(core_step, PLANE + 128 * (t - 2), grid_of((PLANE, 128), core_cell, rim_at))
        fill(near_step, PLANE * (t - 1), grid_of((128, PLANE), rim_at, core_cell), 2)

    def near(l):
        return ((l >> 5),) + rim_cell(l)

    fill(near_step, 4 * PLANE, grid_of((128, 128), near, near), 2)


def tile_of(ref, j):
    return ref[:, OWN * j : OWN * (j + 1), :].reshape(MODES, 128)


def plane_of(ref, plane):
    half = PLANE // 128
    return jnp.concatenate([tile_of(ref, half * plane + h) for h in range(half)], axis=1)


def near_of(inner, own, outer):
    lane = lanes(own.shape)
    out = jnp.where((lane >= RIM_PLANE) & (lane < 3 * RIM_PLANE), turn(own, RIM_PLANE), 0.0)
    if inner is not None:
        out = jnp.where(lane < RIM_PLANE, inner, out)
    if outer is not None:
        out = jnp.where(lane < 3 * RIM_PLANE, out, turn(outer, 2 * RIM_PLANE))
    return out


def slab_coefs(ref):
    lane = lanes((OWN, 128))
    raw = [ref[m, CORE_TILES * OWN :, :] for m in range(GROUPS)]
    core = [jnp.where(lane < SPARE, turn(raw[2 * j], -SPARE), raw[2 * j + 1]) for j in range(CORE_TILES)]
    lane8 = lanes((8, 128))
    parts = []
    for g in range(3):
        total = jnp.zeros((8, 128), jnp.float32)
        for m in range(GROUPS):
            lo = 2 * RIM * m
            w = turn(raw[m][8:, :], lo - SPARE - 2 * RIM * g)
            total = jnp.where((lane8 >= lo) & (lane8 < lo + 2 * RIM), w, total)
        parts.append(total[3:, :])
    rim = jnp.concatenate(parts + [jnp.zeros((1, 128), jnp.float32)], axis=0)
    return jnp.concatenate(core + [rim], axis=1)


def parts_of(x, count, axis=0):
    out = []
    for _ in range(count - 1):
        h = x.astype(jnp.bfloat16)
        out.append(h)
        x = x - h.astype(jnp.float32)
    return jnp.concatenate(out + [x.astype(jnp.bfloat16)], axis=axis)


def get(field, t):
    part = field[t]
    return part() if callable(part) else part[0][:, part[1]]


def put(field, t, x):
    ref, at = field[t]
    ref[:, at] = x


def product(x, matrix, parts=2):
    out = jnp.dot(parts_of(x, parts), matrix, preferred_element_type=jnp.float32)
    return sum(out[x.shape[0] * i : x.shape[0] * (i + 1)] for i in range(parts))


def from_rim(x, matrix):
    return jnp.dot(parts_of(x, 2, 1), matrix, preferred_element_type=jnp.float32)


def to_rim(x, t, core_step, parts=2):
    return product(x, core_step[:, PLANE + 128 * (t - 2) : PLANE + 128 * (t - 1)], parts)


def neighbours(src, slots, steps, begun={}):
    core_step, near_step = steps
    out = {}
    near = get(src, "near")
    for t in slots:
        if t == "near":
            out[t] = begun[t] + from_rim(near, near_step[:, 4 * PLANE :])
        else:
            x = begun[t] if t in begun else product(get(src, t), core_step[:, :PLANE])
            x = x + from_rim(near, near_step[:, PLANE * (t - 1) : PLANE * t])
            out[t] = x + (get(src, t - 1) + get(src, t + 1))
    return out


def sum_coefs(dst, src, slots, steps):
    core_step, near_step = steps
    near = get(src, "near")
    for t in slots:
        x = product(get(src, t), core_step[:, :PLANE], 3)
        x = x + product(near, near_step[:128, PLANE * (t - 1) : PLANE * t], 3)
        put(dst, t, x + (get(src, t - 1) + get(src, t + 1)) + 6.0 * get(src, t))


def mix(links, x, sums, kept=None, known=None):
    width = x.shape[1]
    pair = parts_of(x, 2) if known is None else None
    rows_of = [
        [jnp.broadcast_to(ref[k : k + 1, at], (8, width)) for k in range(TERMS)] for (ref, at), _ in sums
    ]
    split = lambda x: x.reshape(BLOCK // 8, 8, width)
    for b in range(MODES // BLOCK):
        rows = slice(BLOCK * b, BLOCK * (b + 1))
        at = slice(KL * BLOCK * b, KL * BLOCK * (b + 1))
        if known is None:
            mixed = jnp.dot(links[at, :], pair, preferred_element_type=jnp.float32)
        else:
            mixed = known[at, :]
        if kept is not None:
            kept[at, :] = mixed
        here = split(x[rows, :])
        totals = [here * weights[KL][None] for weights in rows_of]
        for k in range(KL):
            part = split(mixed[BLOCK * k : BLOCK * (k + 1), :])
            totals = [total + part * weights[k][None] for total, weights in zip(totals, rows_of)]
        for total, (_, finish) in zip(totals, sums):
            finish(rows, total.reshape(BLOCK, width))


def into(field, t, sign=0):
    ref, at = field[t]

    def finish(rows, total):
        if sign:
            total = ref[rows, at] + total if sign > 0 else ref[rows, at] - total
        ref[rows, at] = total

    return finish


def prep_kernel(own_ref, table_ref, coef, pc, mix3, links, core_step, near_step, pad):
    build_links(table_ref, links, pad)
    build_steps(core_step, near_step)
    coef[...] = slab_coefs(own_ref)
    for plane, kept in ((0, None), (1, mix3)):
        at = slice(PLANE * plane, PLANE * (plane + 1))
        mix(links, plane_of(own_ref, plane), [((coef, at), into({plane: (pc, at)}, plane))], kept)


def lo(n):
    return slice(PLANE * n, PLANE * (n + 1))


NEAR, FAR = slice(0, 128), slice(128, 256)
TAIL = slice(2 * PLANE, 2 * PLANE + 128)
FAR_TAIL = slice(2 * PLANE + 128, 2 * PLANE + 256)
BEGUN_U, BEGUN_P = slice(3 * PLANE, 3 * PLANE + 128), slice(3 * PLANE + 128, 3 * PLANE + 256)
NEAR_TAIL = slice(4 * PLANE, 4 * PLANE + 128)


def between_kernel(own_ref, inner_ref, coef_own, pc_own, mix3, links, core_step, near_step, coef_inner, ecoef, pc, qc, near, begun):
    steps = (core_step, near_step)
    uf = {0: functools.partial(plane_of, inner_ref, 1), 1: functools.partial(plane_of, inner_ref, 0)}
    uf.update({2: functools.partial(plane_of, own_ref, 0), 3: functools.partial(plane_of, own_ref, 1)})
    inner = tile_of(inner_ref, CORE_TILES)
    near[...] = near_of(inner, tile_of(own_ref, CORE_TILES), None)
    uf["near"] = (near, NEAR)
    uf[4] = lambda: jnp.zeros((MODES, PLANE), jnp.float32)
    coef_inner[...] = slab_coefs(inner_ref)
    cf = {0: (coef_inner, lo(1)), 1: (coef_inner, lo(0)), 2: (coef_own, lo(0)), 3: (coef_own, lo(1))}
    cf["near"] = lambda: near_of(coef_inner[:, TAIL], coef_own[:, TAIL], None)
    ef = {t: (ecoef, lo(t - 1)) for t in (1, 2)}
    sum_coefs(ef, cf, (1, 2), steps)
    ecoef[:, TAIL] = to_rim(get(cf, 2), 2, core_step, 3) + to_rim(get(cf, 3), 3, core_step, 3)
    pf = {0: (pc, lo(0)), 1: (pc, lo(1)), 2: (pc_own, lo(0)), 3: (pc_own, lo(1))}
    qf = {t: (qc, lo(t - 1)) for t in (1, 2, 3)}
    mix(links, get(uf, 1), [(cf[1], into(pf, 1)), (ef[1], into(qf, 1))])
    mix(links, get(uf, 2), [(ef[2], into(qf, 2))])
    mix(links, get(uf, 0), [(cf[0], into(pf, 0))])
    qc[:, lo(2)] = jnp.zeros((MODES, PLANE), jnp.float32)
    for t, x in neighbours(uf, (1, 2, 3), steps).items():
        mix(links, x, [(cf[t], into(qf, t, -1))])
    rim = from_rim(near[...], near_step[:, 4 * PLANE :])
    begun[:, BEGUN_U] = rim + to_rim(get(uf, 2), 2, core_step) + to_rim(get(uf, 3), 3, core_step)
    for t in (1, 2, 3):
        begun[:, lo(t - 1)] = product(get(pf, t), core_step[:, :PLANE])
    begun[:, BEGUN_P] = to_rim(get(pf, 2), 2, core_step) + to_rim(get(pf, 3), 3, core_step)


def step_kernel(own_ref, inner_ref, outer_ref, coef_own, pc_own, mix3, links, core_step, near_step, coef_inner, ecoef_known, pc_known, qc_known, near_known, begun, out_ref, rims, coef_outer, coef_rims, ecoef, pc, qc, search, pc2, qc2, sol, res):
    steps = (core_step, near_step)
    uf = {}
    for t, (ref, plane) in enumerate(((inner_ref, 1), (inner_ref, 0), (own_ref, 0), (own_ref, 1), (outer_ref, 1), (outer_ref, 0))):
        uf[t] = functools.partial(plane_of, ref, plane)
    near_new = turn(tile_of(outer_ref, CORE_TILES), 2 * RIM_PLANE)
    near_new = jnp.where(lanes((MODES, 128)) < 3 * RIM_PLANE, 0.0, near_new)
    rims[:, NEAR] = near_known[...] + near_new
    uf["near"] = (rims, NEAR)

    coef_outer[...] = slab_coefs(outer_ref)
    near = near_of(coef_inner[:, TAIL], coef_own[:, TAIL], coef_outer[:, TAIL])
    coef_rims[:, NEAR] = near
    coef_rims[:, FAR] = near
    cf = {0: (coef_inner, lo(1)), 1: (coef_inner, lo(0)), 2: (coef_own, lo(0)), 3: (coef_own, lo(1))}
    cf.update({4: (coef_outer, lo(1)), 5: (coef_outer, lo(0)), "near": (coef_rims, NEAR)})
    ef = {t: (ecoef_known, lo(t - 1)) for t in (1, 2)}
    ef.update({3: (ecoef, lo(0)), 4: (ecoef, lo(1)), "near": (ecoef, TAIL)})

    pf = {0: (pc_known, lo(0)), 1: (pc_known, lo(1)), 2: (pc_own, lo(0)), 3: (pc_own, lo(1)), 4: (pc, lo(0)), 5: (pc, lo(1))}
    pf["near"] = (pc, TAIL)
    qf = {1: (qc_known, lo(0)), 2: (qc_known, lo(1)), 3: (qc, lo(0)), 4: (qc, lo(1)), "near": (qc, TAIL)}
    all_rims = slice(TAIL.start, FAR_TAIL.stop)
    qc[:, lo(0)] = qc_known[:, lo(2)]
    mix(links, get(uf, 5), [(cf[5], into(pf, 5))])
    sum_coefs(ef, cf, (3, 4), steps)
    ecoef[:, TAIL] = ecoef_known[:, TAIL] + product(near, near_step[:128, 4 * PLANE :], 3) + 6.0 * near
    ecoef[:, FAR_TAIL] = jnp.zeros((COEF_ROWS, 128), jnp.float32)
    around = neighbours(uf, (4,), steps)[4]
    rims[:, FAR] = begun[:, BEGUN_U] + from_rim(near_new, near_step[:, 4 * PLANE :])
    rim_sums = [((coef_rims, slice(0, 256)), pc), ((ecoef, all_rims), qc)]
    mix(links, rims[...], [(weights, into({0: (ref, all_rims)}, 0)) for weights, ref in rim_sums])
    mix(links, get(uf, 4), [(cf[4], into(pf, 4)), (ef[4], into(qf, 4)), (cf[3], into(qf, 3, -1))])
    known = {t: begun[:, lo(t - 1)] for t in (1, 2, 3)}
    known["near"] = begun[:, BEGUN_P]
    around_p = neighbours(pf, (1, 2, 3, 4, "near"), steps, known)
    mix(links, around, [(cf[4], into(qf, 4, -1))])
    mix(links, get(uf, 3), [(ef[3], into(qf, 3, 1))], known=mix3)

    sigma = THETA / DELTA
    rho = 1.0 / sigma
    rho_next = 1.0 / (2.0 * sigma - rho)
    sf = {t: (search, lo(t - 1)) for t in (1, 2, 3, 4)}
    sf["near"] = (search, NEAR_TAIL)
    for t, x in around_p.items():
        start = get(uf, t)
        q = get(qf, t) - (pc[:, FAR_TAIL] if t == "near" else 0.0)
        au = start + 0.5 * (q - x)
        begin = start * (1.0 / THETA)
        r1 = start - au * (1.0 / THETA)
        new = (rho_next * rho) * begin + (2.0 * rho_next / DELTA) * r1
        new = jnp.where(cf[t][0][KL : KL + 1, cf[t][1]] > 0.0, new, 0.0)
        if t in (2, 3):
            res[:, lo(t - 2)] = r1
            sol[:, lo(t - 2)] = begin + new
        put(sf, t, new)

    pf = {t: (pc2, at) for t, (_, at) in sf.items()}
    qf = {t: (qc2, lo(t - 2)) for t in (2, 3)}
    around = neighbours(sf, (2, 3), steps)
    for t in (1, 2, 3, 4, "near"):
        sums = [(cf[t], into(pf, t))]
        if t in (2, 3):
            sums.append((ef[t], into(qf, t)))
        mix(links, get(sf, t), sums)
    around_p = neighbours(pf, (2, 3), steps)
    for t, x in around.items():
        mix(links, x, [(cf[t], into(qf, t, -1))])
    for t, x in around_p.items():
        res[:, lo(t - 2)] = res[:, lo(t - 2)] - (get(sf, t) + 0.5 * (get(qf, t) - x))
    for f, field in enumerate((sol, res)):
        for j in range(OUT_TILES):
            n = (f * OUT_TILES + j) * OWN
            out_ref[:, n : n + OWN, :] = field[:, 128 * j : 128 * (j + 1)].reshape(GROUPS, OWN, 128)


def unpack_kernel(in_ref, table_ref, sol_hbm, res_hbm, halves, sems):
    flip = 1 - lax.rem(lax.axis_index("space"), 2)
    scale = 1.0 / mode_scale(table_ref[...])
    lane = lanes((OWN, 128))
    per = 128 // ZC
    copies = []
    for f, hbm in enumerate((sol_hbm, res_hbm)):
        for h in range(NZ // 128):
            for p in range(ROWS):
                plane, y = p // NY, p % NY
                row = (plane + flip * (1 - 2 * plane)) * NY + y
                j, i = p // per, p % per
                tile = None
                for n in range(per):
                    w = in_ref[per * h + n, (f * OUT_TILES + j) * OWN : (f * OUT_TILES + j + 1) * OWN, :]
                    w = turn(w, ZC * (n - i))
                    tile = w if n == 0 else jnp.where(lane >= ZC * n, w, tile)
                halves[f, h, pl.ds(row, OWN, stride=ROWS), :] = tile * scale
            copy = pltpu.make_async_copy(halves.at[f, h], hbm.at[:, pl.ds(128 * h, 128)], sems.at[f, h])
            copy.start()
            copies.append(copy)
    for copy in copies:
        copy.wait()


def whole(count):
    return [pl.BlockSpec(memory_space=pltpu.VMEM)] * count


def anywhere(count):
    return [pl.BlockSpec(memory_space=pltpu.HBM)] * count


def body(load, mean_coeff, kl_ratio, chaos_table):
    params = pltpu.CompilerParams(vmem_limit_bytes=VMEM)
    f32, bf16 = jnp.float32, jnp.bfloat16
    vmem = pltpu.VMEM
    halves = NZ // 128
    table = chaos_table.T
    send = pl.pallas_call(
        pack_kernel,
        out_shape=jax.ShapeDtypeStruct((GROUPS, SEND_ROWS, 128), f32),
        in_specs=anywhere(4),
        out_specs=pl.BlockSpec(memory_space=vmem),
        scratch_shapes=[
            vmem((halves, OWN * ROWS, 128), f32),
            vmem((ROWS, NZ), f32),
            vmem((KL * ROWS, NZ), f32),
            vmem((KL, MODES), jnp.int32),
            pltpu.SemaphoreType.DMA((3 + halves,)),
        ],
        compiler_params=pltpu.CompilerParams(vmem_limit_bytes=VMEM),
        name="pack",
    )(*(pltpu.with_memory_space_constraint(x, pltpu.HBM) for x in (load.reshape(OWN * ROWS, NZ), mean_coeff.reshape(ROWS, NZ), kl_ratio.reshape(KL * ROWS, NZ), table)))
    own = lax.all_to_all(send, "mode", 0, 0, tiled=True)
    count = lax.axis_size("space")
    on_chip = [e for i in range(0, count, 2) for e in ((i, i + 1), (i + 1, i))]
    off_chip = [e for i in range(1, count - 1, 2) for e in ((i, i + 1), (i + 1, i))]
    outer = lax.ppermute(own, "space", off_chip)
    inner = lax.ppermute(own, "space", on_chip)
    shapes = [
        ((COEF_ROWS, 2 * PLANE + 128), f32),
        ((MODES, 2 * PLANE), f32),
        ((KL * MODES, PLANE), f32),
        ((KL * MODES, 2 * MODES), bf16),
        ((PLANE, PLANE + 2 * 128), bf16),
        ((256, 4 * PLANE + 128), bf16),
    ]
    state = pl.pallas_call(
        prep_kernel,
        out_shape=[jax.ShapeDtypeStruct(*shape) for shape in shapes],
        in_specs=whole(2),
        out_specs=whole(len(shapes)),
        scratch_shapes=[vmem((MODES, MODES), f32)],
        compiler_params=params,
        cost_estimate=pl.CostEstimate(flops=1 << 34, bytes_accessed=1 << 22, transcendentals=0),
        name="step_prep",
    )(own, table)
    more = [
        ((COEF_ROWS, 2 * PLANE + 128), f32),
        ((COEF_ROWS, 2 * PLANE + 128), f32),
        ((MODES, 2 * PLANE), f32),
        ((MODES, 3 * PLANE), f32),
        ((MODES, 128), f32),
        ((MODES, 3 * PLANE + 256), f32),
    ]
    between = pl.pallas_call(
        between_kernel,
        out_shape=[jax.ShapeDtypeStruct(*shape) for shape in more],
        in_specs=whole(2 + len(shapes)),
        out_specs=whole(len(more)),
        compiler_params=params,
        cost_estimate=pl.CostEstimate(flops=1 << 10, bytes_accessed=1 << 10, transcendentals=0),
        name="step_between",
    )(own, inner, *state)
    back = pl.pallas_call(
        step_kernel,
        out_shape=jax.ShapeDtypeStruct((GROUPS, 2 * OUT_TILES * OWN, 128), f32),
        in_specs=whole(3 + len(shapes) + len(more)),
        out_specs=pl.BlockSpec(memory_space=vmem),
        scratch_shapes=[
            vmem((MODES, 256), f32),
            vmem((COEF_ROWS, 2 * PLANE + 128), f32),
            vmem((COEF_ROWS, 256), f32),
            vmem((COEF_ROWS, 2 * PLANE + 256), f32),
            vmem((MODES, 2 * PLANE + 256), f32),
            vmem((MODES, 2 * PLANE + 256), f32),
        ]
        + [vmem((MODES, 4 * PLANE + 128), f32)] * 2
        + [vmem((MODES, 2 * PLANE), f32)] * 3,
        compiler_params=params,
        cost_estimate=pl.CostEstimate(flops=2 << 30, bytes_accessed=1 << 22, transcendentals=0),
        name="step",
    )(own, inner, outer, *state, *between)
    back = lax.all_to_all(back, "mode", 0, 0, tiled=True)
    flat = jax.ShapeDtypeStruct((OWN * ROWS, NZ), f32)
    sol, res = pl.pallas_call(
        unpack_kernel,
        out_shape=(flat, flat),
        in_specs=whole(2),
        out_specs=tuple(anywhere(2)),
        scratch_shapes=[vmem((2, halves, OWN * ROWS, 128), f32), pltpu.SemaphoreType.DMA((2, halves))],
        compiler_params=params,
        name="unpack",
    )(back, table)
    return sol.reshape(load.shape), res.reshape(load.shape)


def solution(mesh):
    in_specs = (
        P("mode", "space", None, None),
        P("space", None, None),
        P(None, "space", None, None),
        P(),
    )
    out_specs = (P("mode", "space", None, None), P("mode", "space", None, None))
    return jax.shard_map(body, mesh=mesh, in_specs=in_specs, out_specs=out_specs, check_vma=False)
```

```python
import functools

import jax
import jax.numpy as jnp
from jax import lax
from jax.experimental import pallas as pl
from jax.experimental.pallas import tpu as pltpu
from jax.sharding import PartitionSpec as P

ITERS = 2
THETA = 24.5
DELTA = 23.5
KL = 10
MODES = 128
GROUPS = 8
OWN = MODES // GROUPS
NX_OWN = 2
NY = 8
NZ = 256
ROWS = NX_OWN * NY
ZC = NZ // GROUPS
HALO = 2
PLANE = NY * ZC
CORE_TILES = NX_OWN * PLANE // 128
RIM = 2 * HALO
RIM_PLANE = NY * RIM
SPARE = NX_OWN * RIM_PLANE
TERMS = KL + 1
COEF_ROWS = 16
SEND_ROWS = (CORE_TILES + 1) * OWN
OUT_TILES = CORE_TILES
BLOCK = 32
SQRT2 = 2.0**0.5
SQRT6 = 6.0**0.5
VMEM = 40 * 1024 * 1024


def lanes(shape):
    return lax.broadcasted_iota(jnp.int32, shape, len(shape) - 1)


def mode_scale(t):
    f = jnp.where(t >= 3, SQRT6, jnp.where(t == 2, SQRT2, 1.0)).astype(jnp.float32)
    f = jnp.max(f, axis=0, keepdims=True)
    shape = (OWN, MODES)
    mine = lanes(shape) == lax.broadcasted_iota(jnp.int32, shape, 0) + OWN * lax.axis_index("mode")
    return jnp.sum(jnp.where(mine, f, 0.0), axis=1, keepdims=True)


def turn(x, by):
    by = by % x.shape[1]
    return pltpu.roll(x, by, 1) if by else x


def edges_of(tiles, at, lane):
    out = []
    for e in range(GROUPS + 1):
        z = ZC * e - HALO
        total = None
        for n, tile in enumerate(tiles):
            lo, hi = max(z, 128 * n), min(z + RIM, 128 * (n + 1))
            if lo >= hi:
                continue
            w = turn(tile, at - z)
            w = jnp.where((lane >= at + lo - z) & (lane < at + hi - z), w, 0.0)
            total = w if total is None else total + w
        out.append(total)
    return out


def pack_kernel(load_hbm, mean_hbm, ratio_hbm, table_hbm, out_ref, halves, mean_ref, ratio_ref, table_ref, sems):
    copies = [
        pltpu.make_async_copy(ratio_hbm, ratio_ref, sems.at[0]),
        pltpu.make_async_copy(mean_hbm, mean_ref, sems.at[1]),
        pltpu.make_async_copy(table_hbm, table_ref, sems.at[2]),
    ] + [
        pltpu.make_async_copy(load_hbm.at[:, pl.ds(128 * h, 128)], halves.at[h], sems.at[3 + h])
        for h in range(NZ // 128)
    ]
    for copy in copies:
        copy.start()
    me = lax.axis_index("mode")
    flip = 1 - lax.rem(lax.axis_index("space"), 2)
    lane = lanes((OWN, 128))
    per = 128 // ZC
    for copy in copies[:2]:
        copy.wait()

    def row_of(p):
        plane, y = p // NY, lax.rem(p, NY)
        return (plane + flip * (1 - 2 * plane)) * NY + y

    coefs = []
    for i in range(2):
        row = row_of(2 * me + i)
        mean = mean_ref[pl.ds(row, 1), :]
        terms = [mean * ratio_ref[pl.ds(row + k * ROWS, 1), :] for k in range(KL)] + [mean]
        zero = jnp.zeros_like(mean)
        low = jnp.concatenate(terms + terms[:5], axis=0)
        mid = jnp.concatenate([zero] * 11 + terms[5:10], axis=0)
        top = jnp.concatenate([zero] * 11 + terms[10:] + [zero] * 4, axis=0)
        coefs.append([(c[:, :128], c[:, 128:]) for c in (low, mid, top)])
    lane8 = lanes((8, 128))
    sub8 = lax.broadcasted_iota(jnp.int32, (8, 128), 0)
    first = (lane8 & (RIM - 1)) < HALO
    borders = [jnp.zeros((8, 128), jnp.float32)] * (GROUPS + 1)
    for i in range(2):
        for g in range(3):
            tiles = [c[8:, :] for c in coefs[i][g]]
            more = edges_of(tiles, SPARE + 2 * RIM * g + RIM * i, lane8)
            borders = [x + y for x, y in zip(borders, more)]
    base = []
    for d in range(GROUPS):
        own_cells = []
        for i in range(2):
            w = turn(coefs[i][0][d // per], SPARE + ZC * i - ZC * (d % per))
            own_cells.append(jnp.where((lane >= SPARE + ZC * i) & (lane < SPARE + ZC * (i + 1)), w, 0.0))
        own_cells = own_cells[0] + own_cells[1]
        low = jnp.where(sub8 < TERMS - 8, own_cells[8:, :], jnp.where(first, borders[d], borders[d + 1]))
        base.append(jnp.concatenate([own_cells[:8, :], low], axis=0))

    for copy in copies[2:]:
        copy.wait()
    scale = mode_scale(table_ref[...])
    first = (lane & (RIM - 1)) < HALO
    borders = [jnp.zeros((OWN, 128), jnp.float32)] * (GROUPS + 1)
    for j in range(CORE_TILES):
        rows = []
        for i in range(per):
            row = row_of(jnp.int32(per * j + i))
            rows.append([halves[h, pl.ds(row, OWN, stride=ROWS), :] * scale for h in range(NZ // 128)])
            more = edges_of(rows[i], RIM * (per * j + i), lane)
            borders = [x + y for x, y in zip(borders, more)]
        for d in range(GROUPS):
            tile = None
            for i in range(per):
                w = turn(rows[i][d // per], ZC * (i - d % per))
                tile = w if i == 0 else jnp.where(lane >= ZC * i, w, tile)
            out_ref[d, OWN * j : OWN * (j + 1), :] = tile
    for d in range(GROUPS):
        out_ref[d, CORE_TILES * OWN :, :] = base[d] + jnp.where(first, borders[d], borders[d + 1])


def build_links(table_ref, links, pad):
    pad[...] = jnp.zeros_like(pad)
    pad[:KL, :] = table_ref[...].astype(jnp.float32)
    cols = pad[...]
    rows = jnp.transpose(cols)
    apart = jnp.zeros((MODES, MODES), jnp.float32)
    for k in range(KL):
        apart = apart + jnp.abs(rows[:, k : k + 1] - cols[k : k + 1, :])
    near = apart == 1.0
    for k in range(KL):
        mine = rows[:, k : k + 1]
        d = mine - cols[k : k + 1, :]
        t = jnp.where(near, jnp.where(d == -1.0, 1.0, jnp.where(d == 1.0, mine + jnp.zeros_like(d), 0.0)), 0.0)
        t = t.astype(jnp.bfloat16)
        for b in range(MODES // BLOCK):
            at = (KL * b + k) * BLOCK
            links[at : at + BLOCK, :MODES] = t[BLOCK * b : BLOCK * (b + 1), :]
            links[at : at + BLOCK, MODES:] = t[BLOCK * b : BLOCK * (b + 1), :]


def core_cell(l):
    return l >> 5, l & (ZC - 1)


def rim_cell(l):
    zi = l & (RIM - 1)
    return (l >> 2) & (NY - 1), jnp.where(zi < HALO, zi - HALO, zi + ZC - HALO)


def grid_of(shape, rows_of, cols_of):
    a = rows_of(lax.broadcasted_iota(jnp.int32, shape, 0))
    b = cols_of(lax.broadcasted_iota(jnp.int32, shape, 1))
    return sum(jnp.abs(x - y) for x, y in zip(a, b))


def build_steps(core_step, near_step):
    def fill(ref, to, apart, times=1):
        for n in range(times):
            ref[apart.shape[0] * n : apart.shape[0] * (n + 1), to : to + apart.shape[1]] = jnp.where(
                apart == 1, 1.0, 0.0
            ).astype(jnp.bfloat16)

    fill(core_step, 0, grid_of((PLANE, PLANE), core_cell, core_cell))
    for t in (1, 2, 3, 4):

        def rim_at(l, t=t):
            y, z = rim_cell(l)
            return y + jnp.where((l >> 5) == t - 1, 0, 100), z

        if t in (2, 3):
            fill(core_step, PLANE + 128 * (t - 2), grid_of((PLANE, 128), core_cell, rim_at))
        fill(near_step, PLANE * (t - 1), grid_of((128, PLANE), rim_at, core_cell), 2)

    def near(l):
        return ((l >> 5),) + rim_cell(l)

    fill(near_step, 4 * PLANE, grid_of((128, 128), near, near), 2)


def tile_of(ref, j):
    return ref[:, OWN * j : OWN * (j + 1), :].reshape(MODES, 128)


def plane_of(ref, plane):
    half = PLANE // 128
    return jnp.concatenate([tile_of(ref, half * plane + h) for h in range(half)], axis=1)


def near_of(inner, own, outer):
    lane = lanes(own.shape)
    out = jnp.where((lane >= RIM_PLANE) & (lane < 3 * RIM_PLANE), turn(own, RIM_PLANE), 0.0)
    if inner is not None:
        out = jnp.where(lane < RIM_PLANE, inner, out)
    if outer is not None:
        out = jnp.where(lane < 3 * RIM_PLANE, out, turn(outer, 2 * RIM_PLANE))
    return out


def slab_coefs(ref):
    lane = lanes((OWN, 128))
    raw = [ref[m, CORE_TILES * OWN :, :] for m in range(GROUPS)]
    core = [jnp.where(lane < SPARE, turn(raw[2 * j], -SPARE), raw[2 * j + 1]) for j in range(CORE_TILES)]
    lane8 = lanes((8, 128))
    parts = []
    for g in range(3):
        total = jnp.zeros((8, 128), jnp.float32)
        for m in range(GROUPS):
            lo = 2 * RIM * m
            w = turn(raw[m][8:, :], lo - SPARE - 2 * RIM * g)
            total = jnp.where((lane8 >= lo) & (lane8 < lo + 2 * RIM), w, total)
        parts.append(total[3:, :])
    rim = jnp.concatenate(parts + [jnp.zeros((1, 128), jnp.float32)], axis=0)
    return jnp.concatenate(core + [rim], axis=1)


def parts_of(x, count, axis=0):
    out = []
    for _ in range(count - 1):
        h = x.astype(jnp.bfloat16)
        out.append(h)
        x = x - h.astype(jnp.float32)
    return jnp.concatenate(out + [x.astype(jnp.bfloat16)], axis=axis)


def get(field, t):
    part = field[t]
    return part() if callable(part) else part[0][:, part[1]]


def put(field, t, x):
    ref, at = field[t]
    ref[:, at] = x


def product(x, matrix, parts=2):
    out = jnp.dot(parts_of(x, parts), matrix, preferred_element_type=jnp.float32)
    return sum(out[x.shape[0] * i : x.shape[0] * (i + 1)] for i in range(parts))


def from_rim(x, matrix):
    return jnp.dot(parts_of(x, 2, 1), matrix, preferred_element_type=jnp.float32)


def to_rim(x, t, core_step, parts=2):
    return product(x, core_step[:, PLANE + 128 * (t - 2) : PLANE + 128 * (t - 1)], parts)


def neighbours(src, slots, steps, begun={}):
    core_step, near_step = steps
    out = {}
    near = get(src, "near")
    for t in slots:
        if t == "near":
            out[t] = begun[t] + from_rim(near, near_step[:, 4 * PLANE :])
        else:
            x = begun[t] if t in begun else product(get(src, t), core_step[:, :PLANE])
            x = x + from_rim(near, near_step[:, PLANE * (t - 1) : PLANE * t])
            out[t] = x + (get(src, t - 1) + get(src, t + 1))
    return out


def sum_coefs(dst, src, slots, steps):
    core_step, near_step = steps
    near = get(src, "near")
    for t in slots:
        x = product(get(src, t), core_step[:, :PLANE], 3)
        x = x + product(near, near_step[:128, PLANE * (t - 1) : PLANE * t], 3)
        put(dst, t, x + (get(src, t - 1) + get(src, t + 1)) + 6.0 * get(src, t))


def mix(links, x, sums, kept=None, known=None):
    width = x.shape[1]
    pair = parts_of(x, 2) if known is None else None
    rows_of = [
        [jnp.broadcast_to(ref[k : k + 1, at], (8, width)) for k in range(TERMS)] for (ref, at), _ in sums
    ]
    split = lambda x: x.reshape(BLOCK // 8, 8, width)
    for b in range(MODES // BLOCK):
        rows = slice(BLOCK * b, BLOCK * (b + 1))
        at = slice(KL * BLOCK * b, KL * BLOCK * (b + 1))
        if known is None:
            mixed = jnp.dot(links[at, :], pair, preferred_element_type=jnp.float32)
        else:
            mixed = known[at, :]
        if kept is not None:
            kept[at, :] = mixed
        here = split(x[rows, :])
        totals = [here * weights[KL][None] for weights in rows_of]
        for k in range(KL):
            part = split(mixed[BLOCK * k : BLOCK * (k + 1), :])
            totals = [total + part * weights[k][None] for total, weights in zip(totals, rows_of)]
        for total, (_, finish) in zip(totals, sums):
            finish(rows, total.reshape(BLOCK, width))


def into(field, t, sign=0):
    ref, at = field[t]

    def finish(rows, total):
        if sign:
            total = ref[rows, at] + total if sign > 0 else ref[rows, at] - total
        ref[rows, at] = total

    return finish


def prep_kernel(own_ref, table_ref, coef, pc, mix3, links, core_step, near_step, pad):
    build_links(table_ref, links, pad)
    build_steps(core_step, near_step)
    coef[...] = slab_coefs(own_ref)
    for plane, kept in ((0, None), (1, mix3)):
        at = slice(PLANE * plane, PLANE * (plane + 1))
        mix(links, plane_of(own_ref, plane), [((coef, at), into({plane: (pc, at)}, plane))], kept)


def lo(n):
    return slice(PLANE * n, PLANE * (n + 1))


NEAR, FAR = slice(0, 128), slice(128, 256)
TAIL = slice(2 * PLANE, 2 * PLANE + 128)
FAR_TAIL = slice(2 * PLANE + 128, 2 * PLANE + 256)
BEGUN_U, BEGUN_P = slice(3 * PLANE, 3 * PLANE + 128), slice(3 * PLANE + 128, 3 * PLANE + 256)
NEAR_TAIL = slice(4 * PLANE, 4 * PLANE + 128)


def between_kernel(own_ref, inner_ref, coef_own, pc_own, mix3, links, core_step, near_step, coef_inner, ecoef, pc, qc, near, begun):
    steps = (core_step, near_step)
    uf = {0: functools.partial(plane_of, inner_ref, 1), 1: functools.partial(plane_of, inner_ref, 0)}
    uf.update({2: functools.partial(plane_of, own_ref, 0), 3: functools.partial(plane_of, own_ref, 1)})
    inner = tile_of(inner_ref, CORE_TILES)
    near[...] = near_of(inner, tile_of(own_ref, CORE_TILES), None)
    uf["near"] = (near, NEAR)
    uf[4] = lambda: jnp.zeros((MODES, PLANE), jnp.float32)
    coef_inner[...] = slab_coefs(inner_ref)
    cf = {0: (coef_inner, lo(1)), 1: (coef_inner, lo(0)), 2: (coef_own, lo(0)), 3: (coef_own, lo(1))}
    cf["near"] = lambda: near_of(coef_inner[:, TAIL], coef_own[:, TAIL], None)
    ef = {t: (ecoef, lo(t - 1)) for t in (1, 2)}
    sum_coefs(ef, cf, (1, 2), steps)
    ecoef[:, TAIL] = to_rim(get(cf, 2), 2, core_step, 3) + to_rim(get(cf, 3), 3, core_step, 3)
    pf = {0: (pc, lo(0)), 1: (pc, lo(1)), 2: (pc_own, lo(0)), 3: (pc_own, lo(1))}
    qf = {t: (qc, lo(t - 1)) for t in (1, 2, 3)}
    mix(links, get(uf, 1), [(cf[1], into(pf, 1)), (ef[1], into(qf, 1))])
    mix(links, get(uf, 2), [(ef[2], into(qf, 2))])
    mix(links, get(uf, 0), [(cf[0], into(pf, 0))])
    qc[:, lo(2)] = jnp.zeros((MODES, PLANE), jnp.float32)
    for t, x in neighbours(uf, (1, 2, 3), steps).items():
        mix(links, x, [(cf[t], into(qf, t, -1))])
    rim = from_rim(near[...], near_step[:, 4 * PLANE :])
    begun[:, BEGUN_U] = rim + to_rim(get(uf, 2), 2, core_step) + to_rim(get(uf, 3), 3, core_step)
    for t in (1, 2, 3):
        begun[:, lo(t - 1)] = product(get(pf, t), core_step[:, :PLANE])
    begun[:, BEGUN_P] = to_rim(get(pf, 2), 2, core_step) + to_rim(get(pf, 3), 3, core_step)


def step_kernel(own_ref, inner_ref, outer_ref, coef_own, pc_own, mix3, links, core_step, near_step, coef_inner, ecoef_known, pc_known, qc_known, near_known, begun, out_ref, rims, coef_outer, coef_rims, ecoef, pc, qc, search, pc2, qc2, sol, res, mix4):
    steps = (core_step, near_step)
    uf = {}
    for t, (ref, plane) in enumerate(((inner_ref, 1), (inner_ref, 0), (own_ref, 0), (own_ref, 1), (outer_ref, 1), (outer_ref, 0))):
        uf[t] = functools.partial(plane_of, ref, plane)
    near_new = turn(tile_of(outer_ref, CORE_TILES), 2 * RIM_PLANE)
    near_new = jnp.where(lanes((MODES, 128)) < 3 * RIM_PLANE, 0.0, near_new)
    rims[:, NEAR] = near_known[...] + near_new
    uf["near"] = (rims, NEAR)

    coef_outer[...] = slab_coefs(outer_ref)
    near = near_of(coef_inner[:, TAIL], coef_own[:, TAIL], coef_outer[:, TAIL])
    coef_rims[:, NEAR] = near
    coef_rims[:, FAR] = near
    cf = {0: (coef_inner, lo(1)), 1: (coef_inner, lo(0)), 2: (coef_own, lo(0)), 3: (coef_own, lo(1))}
    cf.update({4: (coef_outer, lo(1)), 5: (coef_outer, lo(0)), "near": (coef_rims, NEAR)})
    ef = {t: (ecoef_known, lo(t - 1)) for t in (1, 2)}
    ef.update({3: (ecoef, lo(0)), 4: (ecoef, lo(1)), "near": (ecoef, TAIL)})

    pf = {0: (pc_known, lo(0)), 1: (pc_known, lo(1)), 2: (pc_own, lo(0)), 3: (pc_own, lo(1)), 4: (pc, lo(0)), 5: (pc, lo(1))}
    pf["near"] = (pc, TAIL)
    qf = {1: (qc_known, lo(0)), 2: (qc_known, lo(1)), 3: (qc, lo(0)), 4: (qc, lo(1)), "near": (qc, TAIL)}
    all_rims = slice(TAIL.start, FAR_TAIL.stop)
    qc[:, lo(0)] = qc_known[:, lo(2)]
    mix(links, get(uf, 5), [(cf[5], into(pf, 5))])
    around = neighbours(uf, (4,), steps)[4]
    rims[:, FAR] = begun[:, BEGUN_U] + from_rim(near_new, near_step[:, 4 * PLANE :])
    rim_sums = [((coef_rims, slice(0, 256)), pc), ((ecoef, all_rims), qc)]
    mix(links, get(uf, 4), [(cf[4], into(pf, 4)), (cf[3], into(qf, 3, -1))], mix4)
    sum_coefs(ef, cf, (3, 4), steps)
    ecoef[:, TAIL] = ecoef_known[:, TAIL] + product(near, near_step[:128, 4 * PLANE :], 3) + 6.0 * near
    ecoef[:, FAR_TAIL] = jnp.zeros((COEF_ROWS, 128), jnp.float32)
    mix(links, rims[...], [(weights, into({0: (ref, all_rims)}, 0)) for weights, ref in rim_sums])
    known = {t: begun[:, lo(t - 1)] for t in (1, 2, 3)}
    known["near"] = begun[:, BEGUN_P]
    around_p = neighbours(pf, (1, 2, 3, 4, "near"), steps, known)
    qc[:, lo(1)] = jnp.zeros((MODES, PLANE), jnp.float32)
    mix(links, around, [(cf[4], into(qf, 4, -1))])
    mix(links, get(uf, 3), [(ef[3], into(qf, 3, 1))], known=mix3)
    mix(links, get(uf, 4), [(ef[4], into(qf, 4, 1))], known=mix4)

    sigma = THETA / DELTA
    rho = 1.0 / sigma
    rho_next = 1.0 / (2.0 * sigma - rho)
    sf = {t: (search, lo(t - 1)) for t in (1, 2, 3, 4)}
    sf["near"] = (search, NEAR_TAIL)
    for t, x in around_p.items():
        start = get(uf, t)
        q = get(qf, t) - (pc[:, FAR_TAIL] if t == "near" else 0.0)
        au = start + 0.5 * (q - x)
        begin = start * (1.0 / THETA)
        r1 = start - au * (1.0 / THETA)
        new = (rho_next * rho) * begin + (2.0 * rho_next / DELTA) * r1
        new = jnp.where(cf[t][0][KL : KL + 1, cf[t][1]] > 0.0, new, 0.0)
        if t in (2, 3):
            res[:, lo(t - 2)] = r1
            sol[:, lo(t - 2)] = begin + new
        put(sf, t, new)

    pf = {t: (pc2, at) for t, (_, at) in sf.items()}
    qf = {t: (qc2, lo(t - 2)) for t in (2, 3)}
    around = neighbours(sf, (2, 3), steps)
    for t in (1, 2, 3, 4, "near"):
        sums = [(cf[t], into(pf, t))]
        if t in (2, 3):
            sums.append((ef[t], into(qf, t)))
        mix(links, get(sf, t), sums)
    around_p = neighbours(pf, (2, 3), steps)
    for t, x in around.items():
        mix(links, x, [(cf[t], into(qf, t, -1))])
    for t, x in around_p.items():
        res[:, lo(t - 2)] = res[:, lo(t - 2)] - (get(sf, t) + 0.5 * (get(qf, t) - x))
    for f, field in enumerate((sol, res)):
        for j in range(OUT_TILES):
            n = (f * OUT_TILES + j) * OWN
            out_ref[:, n : n + OWN, :] = field[:, 128 * j : 128 * (j + 1)].reshape(GROUPS, OWN, 128)


def unpack_kernel(in_ref, table_ref, sol_hbm, res_hbm, halves, sems):
    flip = 1 - lax.rem(lax.axis_index("space"), 2)
    scale = 1.0 / mode_scale(table_ref[...])
    lane = lanes((OWN, 128))
    per = 128 // ZC
    copies = []
    for f, hbm in enumerate((sol_hbm, res_hbm)):
        for h in range(NZ // 128):
            for p in range(ROWS):
                plane, y = p // NY, p % NY
                row = (plane + flip * (1 - 2 * plane)) * NY + y
                j, i = p // per, p % per
                tile = None
                for n in range(per):
                    w = in_ref[per * h + n, (f * OUT_TILES + j) * OWN : (f * OUT_TILES + j + 1) * OWN, :]
                    w = turn(w, ZC * (n - i))
                    tile = w if n == 0 else jnp.where(lane >= ZC * n, w, tile)
                halves[f, h, pl.ds(row, OWN, stride=ROWS), :] = tile * scale
            copy = pltpu.make_async_copy(halves.at[f, h], hbm.at[:, pl.ds(128 * h, 128)], sems.at[f, h])
            copy.start()
            copies.append(copy)
    for copy in copies:
        copy.wait()


def whole(count):
    return [pl.BlockSpec(memory_space=pltpu.VMEM)] * count


def anywhere(count):
    return [pl.BlockSpec(memory_space=pltpu.HBM)] * count


def body(load, mean_coeff, kl_ratio, chaos_table):
    params = pltpu.CompilerParams(vmem_limit_bytes=VMEM)
    f32, bf16 = jnp.float32, jnp.bfloat16
    vmem = pltpu.VMEM
    halves = NZ // 128
    table = chaos_table.T
    send = pl.pallas_call(
        pack_kernel,
        out_shape=jax.ShapeDtypeStruct((GROUPS, SEND_ROWS, 128), f32),
        in_specs=anywhere(4),
        out_specs=pl.BlockSpec(memory_space=vmem),
        scratch_shapes=[
            vmem((halves, OWN * ROWS, 128), f32),
            vmem((ROWS, NZ), f32),
            vmem((KL * ROWS, NZ), f32),
            vmem((KL, MODES), jnp.int32),
            pltpu.SemaphoreType.DMA((3 + halves,)),
        ],
        compiler_params=pltpu.CompilerParams(vmem_limit_bytes=VMEM),
        name="pack",
    )(*(pltpu.with_memory_space_constraint(x, pltpu.HBM) for x in (load.reshape(OWN * ROWS, NZ), mean_coeff.reshape(ROWS, NZ), kl_ratio.reshape(KL * ROWS, NZ), table)))
    own = lax.all_to_all(send, "mode", 0, 0, tiled=True)
    count = lax.axis_size("space")
    on_chip = [e for i in range(0, count, 2) for e in ((i, i + 1), (i + 1, i))]
    off_chip = [e for i in range(1, count - 1, 2) for e in ((i, i + 1), (i + 1, i))]
    outer = lax.ppermute(own, "space", off_chip)
    inner = lax.ppermute(own, "space", on_chip)
    shapes = [
        ((COEF_ROWS, 2 * PLANE + 128), f32),
        ((MODES, 2 * PLANE), f32),
        ((KL * MODES, PLANE), f32),
        ((KL * MODES, 2 * MODES), bf16),
        ((PLANE, PLANE + 2 * 128), bf16),
        ((256, 4 * PLANE + 128), bf16),
    ]
    state = pl.pallas_call(
        prep_kernel,
        out_shape=[jax.ShapeDtypeStruct(*shape) for shape in shapes],
        in_specs=whole(2),
        out_specs=whole(len(shapes)),
        scratch_shapes=[vmem((MODES, MODES), f32)],
        compiler_params=params,
        cost_estimate=pl.CostEstimate(flops=1 << 34, bytes_accessed=1 << 22, transcendentals=0),
        name="step_prep",
    )(own, table)
    more = [
        ((COEF_ROWS, 2 * PLANE + 128), f32),
        ((COEF_ROWS, 2 * PLANE + 128), f32),
        ((MODES, 2 * PLANE), f32),
        ((MODES, 3 * PLANE), f32),
        ((MODES, 128), f32),
        ((MODES, 3 * PLANE + 256), f32),
    ]
    between = pl.pallas_call(
        between_kernel,
        out_shape=[jax.ShapeDtypeStruct(*shape) for shape in more],
        in_specs=whole(2 + len(shapes)),
        out_specs=whole(len(more)),
        compiler_params=params,
        cost_estimate=pl.CostEstimate(flops=1 << 10, bytes_accessed=1 << 10, transcendentals=0),
        name="step_between",
    )(own, inner, *state)
    back = pl.pallas_call(
        step_kernel,
        out_shape=jax.ShapeDtypeStruct((GROUPS, 2 * OUT_TILES * OWN, 128), f32),
        in_specs=whole(3 + len(shapes) + len(more)),
        out_specs=pl.BlockSpec(memory_space=vmem),
        scratch_shapes=[
            vmem((MODES, 256), f32),
            vmem((COEF_ROWS, 2 * PLANE + 128), f32),
            vmem((COEF_ROWS, 256), f32),
            vmem((COEF_ROWS, 2 * PLANE + 256), f32),
            vmem((MODES, 2 * PLANE + 256), f32),
            vmem((MODES, 2 * PLANE + 256), f32),
        ]
        + [vmem((MODES, 4 * PLANE + 128), f32)] * 2
        + [vmem((MODES, 2 * PLANE), f32)] * 3
        + [vmem((KL * MODES, PLANE), f32)],
        compiler_params=params,
        cost_estimate=pl.CostEstimate(flops=2 << 30, bytes_accessed=1 << 22, transcendentals=0),
        name="step",
    )(own, inner, outer, *state, *between)
    back = lax.all_to_all(back, "mode", 0, 0, tiled=True)
    flat = jax.ShapeDtypeStruct((OWN * ROWS, NZ), f32)
    sol, res = pl.pallas_call(
        unpack_kernel,
        out_shape=(flat, flat),
        in_specs=whole(2),
        out_specs=tuple(anywhere(2)),
        scratch_shapes=[vmem((2, halves, OWN * ROWS, 128), f32), pltpu.SemaphoreType.DMA((2, halves))],
        compiler_params=params,
        name="unpack",
    )(back, table)
    return sol.reshape(load.shape), res.reshape(load.shape)


def solution(mesh):
    in_specs = (
        P("mode", "space", None, None),
        P("space", None, None),
        P(None, "space", None, None),
        P(),
    )
    out_specs = (P("mode", "space", None, None), P("mode", "space", None, None))
    return jax.shard_map(body, mesh=mesh, in_specs=in_specs, out_specs=out_specs, check_vma=False)
```

```python
import functools

import jax
import jax.numpy as jnp
from jax import lax
from jax.experimental import pallas as pl
from jax.experimental.pallas import tpu as pltpu
from jax.sharding import PartitionSpec as P

ITERS = 2
THETA = 24.5
DELTA = 23.5
KL = 10
MODES = 128
GROUPS = 8
OWN = MODES // GROUPS
NX_OWN = 2
NY = 8
NZ = 256
ROWS = NX_OWN * NY
ZC = NZ // GROUPS
HALO = 2
PLANE = NY * ZC
CORE_TILES = NX_OWN * PLANE // 128
RIM = 2 * HALO
RIM_PLANE = NY * RIM
SPARE = NX_OWN * RIM_PLANE
TERMS = KL + 1
COEF_ROWS = 16
SEND_ROWS = (CORE_TILES + 1) * OWN
OUT_TILES = CORE_TILES
BLOCK = 32
SQRT2 = 2.0**0.5
SQRT6 = 6.0**0.5
VMEM = 40 * 1024 * 1024


def lanes(shape):
    return lax.broadcasted_iota(jnp.int32, shape, len(shape) - 1)


def mode_scale(t):
    f = jnp.where(t >= 3, SQRT6, jnp.where(t == 2, SQRT2, 1.0)).astype(jnp.float32)
    f = jnp.max(f, axis=0, keepdims=True)
    shape = (OWN, MODES)
    mine = lanes(shape) == lax.broadcasted_iota(jnp.int32, shape, 0) + OWN * lax.axis_index("mode")
    return jnp.sum(jnp.where(mine, f, 0.0), axis=1, keepdims=True)


def turn(x, by):
    by = by % x.shape[1]
    return pltpu.roll(x, by, 1) if by else x


def edges_of(tiles, at, lane):
    out = []
    for e in range(GROUPS + 1):
        z = ZC * e - HALO
        total = None
        for n, tile in enumerate(tiles):
            lo, hi = max(z, 128 * n), min(z + RIM, 128 * (n + 1))
            if lo >= hi:
                continue
            w = turn(tile, at - z)
            w = jnp.where((lane >= at + lo - z) & (lane < at + hi - z), w, 0.0)
            total = w if total is None else total + w
        out.append(total)
    return out


def pack_kernel(load_hbm, mean_hbm, ratio_hbm, table_hbm, out_ref, halves, mean_ref, ratio_ref, table_ref, sems):
    copies = [
        pltpu.make_async_copy(ratio_hbm, ratio_ref, sems.at[0]),
        pltpu.make_async_copy(mean_hbm, mean_ref, sems.at[1]),
        pltpu.make_async_copy(table_hbm, table_ref, sems.at[2]),
    ] + [
        pltpu.make_async_copy(load_hbm.at[:, pl.ds(128 * h, 128)], halves.at[h], sems.at[3 + h])
        for h in range(NZ // 128)
    ]
    for copy in copies:
        copy.start()
    me = lax.axis_index("mode")
    flip = 1 - lax.rem(lax.axis_index("space"), 2)
    lane = lanes((OWN, 128))
    per = 128 // ZC
    for copy in copies[:2]:
        copy.wait()

    def row_of(p):
        plane, y = p // NY, lax.rem(p, NY)
        return (plane + flip * (1 - 2 * plane)) * NY + y

    coefs = []
    for i in range(2):
        row = row_of(2 * me + i)
        mean = mean_ref[pl.ds(row, 1), :]
        terms = [mean * ratio_ref[pl.ds(row + k * ROWS, 1), :] for k in range(KL)] + [mean]
        zero = jnp.zeros_like(mean)
        low = jnp.concatenate(terms + terms[:5], axis=0)
        mid = jnp.concatenate([zero] * 11 + terms[5:10], axis=0)
        top = jnp.concatenate([zero] * 11 + terms[10:] + [zero] * 4, axis=0)
        coefs.append([(c[:, :128], c[:, 128:]) for c in (low, mid, top)])
    lane8 = lanes((8, 128))
    sub8 = lax.broadcasted_iota(jnp.int32, (8, 128), 0)
    first = (lane8 & (RIM - 1)) < HALO
    borders = [jnp.zeros((8, 128), jnp.float32)] * (GROUPS + 1)
    for i in range(2):
        for g in range(3):
            tiles = [c[8:, :] for c in coefs[i][g]]
            more = edges_of(tiles, SPARE + 2 * RIM * g + RIM * i, lane8)
            borders = [x + y for x, y in zip(borders, more)]
    base = []
    for d in range(GROUPS):
        own_cells = []
        for i in range(2):
            w = turn(coefs[i][0][d // per], SPARE + ZC * i - ZC * (d % per))
            own_cells.append(jnp.where((lane >= SPARE + ZC * i) & (lane < SPARE + ZC * (i + 1)), w, 0.0))
        own_cells = own_cells[0] + own_cells[1]
        low = jnp.where(sub8 < TERMS - 8, own_cells[8:, :], jnp.where(first, borders[d], borders[d + 1]))
        base.append(jnp.concatenate([own_cells[:8, :], low], axis=0))

    for copy in copies[2:]:
        copy.wait()
    scale = mode_scale(table_ref[...])
    first = (lane & (RIM - 1)) < HALO
    borders = [jnp.zeros((OWN, 128), jnp.float32)] * (GROUPS + 1)
    for j in range(CORE_TILES):
        rows = []
        for i in range(per):
            row = row_of(jnp.int32(per * j + i))
            rows.append([halves[h, pl.ds(row, OWN, stride=ROWS), :] * scale for h in range(NZ // 128)])
            more = edges_of(rows[i], RIM * (per * j + i), lane)
            borders = [x + y for x, y in zip(borders, more)]
        for d in range(GROUPS):
            tile = None
            for i in range(per):
                w = turn(rows[i][d // per], ZC * (i - d % per))
                tile = w if i == 0 else jnp.where(lane >= ZC * i, w, tile)
            out_ref[d, OWN * j : OWN * (j + 1), :] = tile
    for d in range(GROUPS):
        out_ref[d, CORE_TILES * OWN :, :] = base[d] + jnp.where(first, borders[d], borders[d + 1])


def build_links(table_ref, links, pad):
    pad[...] = jnp.zeros_like(pad)
    pad[:KL, :] = table_ref[...].astype(jnp.float32)
    cols = pad[...]
    rows = jnp.transpose(cols)
    apart = jnp.zeros((MODES, MODES), jnp.float32)
    for k in range(KL):
        apart = apart + jnp.abs(rows[:, k : k + 1] - cols[k : k + 1, :])
    near = apart == 1.0
    for k in range(KL):
        mine = rows[:, k : k + 1]
        d = mine - cols[k : k + 1, :]
        t = jnp.where(near, jnp.where(d == -1.0, 1.0, jnp.where(d == 1.0, mine + jnp.zeros_like(d), 0.0)), 0.0)
        t = t.astype(jnp.bfloat16)
        for b in range(MODES // BLOCK):
            at = (KL * b + k) * BLOCK
            links[at : at + BLOCK, :MODES] = t[BLOCK * b : BLOCK * (b + 1), :]
            links[at : at + BLOCK, MODES:] = t[BLOCK * b : BLOCK * (b + 1), :]


def core_cell(l):
    return l >> 5, l & (ZC - 1)


def rim_cell(l):
    zi = l & (RIM - 1)
    return (l >> 2) & (NY - 1), jnp.where(zi < HALO, zi - HALO, zi + ZC - HALO)


def grid_of(shape, rows_of, cols_of):
    a = rows_of(lax.broadcasted_iota(jnp.int32, shape, 0))
    b = cols_of(lax.broadcasted_iota(jnp.int32, shape, 1))
    return sum(jnp.abs(x - y) for x, y in zip(a, b))


def build_steps(core_step, near_step):
    def fill(ref, to, apart, times=1):
        for n in range(times):
            ref[apart.shape[0] * n : apart.shape[0] * (n + 1), to : to + apart.shape[1]] = jnp.where(
                apart == 1, 1.0, 0.0
            ).astype(jnp.bfloat16)

    fill(core_step, 0, grid_of((PLANE, PLANE), core_cell, core_cell))
    for t in (1, 2, 3, 4):

        def rim_at(l, t=t):
            y, z = rim_cell(l)
            return y + jnp.where((l >> 5) == t - 1, 0, 100), z

        if t in (2, 3):
            fill(core_step, PLANE + 128 * (t - 2), grid_of((PLANE, 128), core_cell, rim_at))
        fill(near_step, PLANE * (t - 1), grid_of((128, PLANE), rim_at, core_cell), 2)

    def near(l):
        return ((l >> 5),) + rim_cell(l)

    fill(near_step, 4 * PLANE, grid_of((128, 128), near, near), 2)


def tile_of(ref, j):
    return ref[:, OWN * j : OWN * (j + 1), :].reshape(MODES, 128)


def plane_of(ref, plane):
    half = PLANE // 128
    return jnp.concatenate([tile_of(ref, half * plane + h) for h in range(half)], axis=1)


def near_of(inner, own, outer):
    lane = lanes(own.shape)
    out = jnp.where((lane >= RIM_PLANE) & (lane < 3 * RIM_PLANE), turn(own, RIM_PLANE), 0.0)
    if inner is not None:
        out = jnp.where(lane < RIM_PLANE, inner, out)
    if outer is not None:
        out = jnp.where(lane < 3 * RIM_PLANE, out, turn(outer, 2 * RIM_PLANE))
    return out


def slab_coefs(ref):
    lane = lanes((OWN, 128))
    raw = [ref[m, CORE_TILES * OWN :, :] for m in range(GROUPS)]
    core = [jnp.where(lane < SPARE, turn(raw[2 * j], -SPARE), raw[2 * j + 1]) for j in range(CORE_TILES)]
    lane8 = lanes((8, 128))
    parts = []
    for g in range(3):
        total = jnp.zeros((8, 128), jnp.float32)
        for m in range(GROUPS):
            lo = 2 * RIM * m
            w = turn(raw[m][8:, :], lo - SPARE - 2 * RIM * g)
            total = jnp.where((lane8 >= lo) & (lane8 < lo + 2 * RIM), w, total)
        parts.append(total[3:, :])
    rim = jnp.concatenate(parts + [jnp.zeros((1, 128), jnp.float32)], axis=0)
    return jnp.concatenate(core + [rim], axis=1)


def parts_of(x, count, axis=0):
    out = []
    for _ in range(count - 1):
        h = x.astype(jnp.bfloat16)
        out.append(h)
        x = x - h.astype(jnp.float32)
    return jnp.concatenate(out + [x.astype(jnp.bfloat16)], axis=axis)


def get(field, t):
    part = field[t]
    return part() if callable(part) else part[0][:, part[1]]


def put(field, t, x):
    ref, at = field[t]
    ref[:, at] = x


def product(x, matrix, parts=2):
    out = jnp.dot(parts_of(x, parts), matrix, preferred_element_type=jnp.float32)
    return sum(out[x.shape[0] * i : x.shape[0] * (i + 1)] for i in range(parts))


def from_rim(x, matrix):
    return jnp.dot(parts_of(x, 2, 1), matrix, preferred_element_type=jnp.float32)


def to_rim(x, t, core_step, parts=2):
    return product(x, core_step[:, PLANE + 128 * (t - 2) : PLANE + 128 * (t - 1)], parts)


def neighbours(src, slots, steps, begun={}):
    core_step, near_step = steps
    out = {}
    near = get(src, "near")
    for t in slots:
        if t == "near":
            out[t] = begun[t] + from_rim(near, near_step[:, 4 * PLANE :])
        else:
            x = begun[t] if t in begun else product(get(src, t), core_step[:, :PLANE])
            x = x + from_rim(near, near_step[:, PLANE * (t - 1) : PLANE * t])
            out[t] = x + (get(src, t - 1) + get(src, t + 1))
    return out


def sum_coefs(dst, src, slots, steps):
    core_step, near_step = steps
    near = get(src, "near")
    for t in slots:
        x = product(get(src, t), core_step[:, :PLANE], 3)
        x = x + product(near, near_step[:128, PLANE * (t - 1) : PLANE * t], 3)
        put(dst, t, x + (get(src, t - 1) + get(src, t + 1)) + 6.0 * get(src, t))


def mix(links, x, sums, kept=None, known=None):
    width = x.shape[1]
    pair = parts_of(x, 2) if known is None else None
    rows_of = [
        [jnp.broadcast_to(ref[k : k + 1, at], (8, width)) for k in range(TERMS)] for (ref, at), _ in sums
    ]
    split = lambda x: x.reshape(BLOCK // 8, 8, width)
    for b in range(MODES // BLOCK):
        rows = slice(BLOCK * b, BLOCK * (b + 1))
        at = slice(KL * BLOCK * b, KL * BLOCK * (b + 1))
        if known is None:
            mixed = jnp.dot(links[at, :], pair, preferred_element_type=jnp.float32)
        else:
            mixed = known[at, :]
        if kept is not None:
            kept[at, :] = mixed
        here = split(x[rows, :])
        totals = [here * weights[KL][None] for weights in rows_of]
        for k in range(KL):
            part = split(mixed[BLOCK * k : BLOCK * (k + 1), :])
            totals = [total + part * weights[k][None] for total, weights in zip(totals, rows_of)]
        for total, (_, finish) in zip(totals, sums):
            finish(rows, total.reshape(BLOCK, width))


def into(field, t, sign=0):
    ref, at = field[t]

    def finish(rows, total):
        if sign:
            total = ref[rows, at] + total if sign > 0 else ref[rows, at] - total
        ref[rows, at] = total

    return finish


def prep_kernel(own_ref, table_ref, coef, pc, mix3, links, core_step, near_step, pad):
    build_links(table_ref, links, pad)
    build_steps(core_step, near_step)
    coef[...] = slab_coefs(own_ref)
    for plane, kept in ((0, None), (1, mix3)):
        at = slice(PLANE * plane, PLANE * (plane + 1))
        mix(links, plane_of(own_ref, plane), [((coef, at), into({plane: (pc, at)}, plane))], kept)


def lo(n):
    return slice(PLANE * n, PLANE * (n + 1))


NEAR, FAR = slice(0, 128), slice(128, 256)
TAIL = slice(2 * PLANE, 2 * PLANE + 128)
FAR_TAIL = slice(2 * PLANE + 128, 2 * PLANE + 256)
BEGUN_U, BEGUN_P = slice(3 * PLANE, 3 * PLANE + 128), slice(3 * PLANE + 128, 3 * PLANE + 256)
NEAR_TAIL = slice(4 * PLANE, 4 * PLANE + 128)


def between_kernel(own_ref, inner_ref, coef_own, pc_own, mix3, links, core_step, near_step, coef_inner, ecoef, pc, qc, near, begun):
    steps = (core_step, near_step)
    uf = {0: functools.partial(plane_of, inner_ref, 1), 1: functools.partial(plane_of, inner_ref, 0)}
    uf.update({2: functools.partial(plane_of, own_ref, 0), 3: functools.partial(plane_of, own_ref, 1)})
    inner = tile_of(inner_ref, CORE_TILES)
    near[...] = near_of(inner, tile_of(own_ref, CORE_TILES), None)
    uf["near"] = (near, NEAR)
    uf[4] = lambda: jnp.zeros((MODES, PLANE), jnp.float32)
    coef_inner[...] = slab_coefs(inner_ref)
    cf = {0: (coef_inner, lo(1)), 1: (coef_inner, lo(0)), 2: (coef_own, lo(0)), 3: (coef_own, lo(1))}
    cf["near"] = lambda: near_of(coef_inner[:, TAIL], coef_own[:, TAIL], None)
    ef = {t: (ecoef, lo(t - 1)) for t in (1, 2)}
    pf = {0: (pc, lo(0)), 1: (pc, lo(1)), 2: (pc_own, lo(0)), 3: (pc_own, lo(1))}
    qf = {t: (qc, lo(t - 1)) for t in (1, 2, 3)}
    mix(links, get(uf, 0), [(cf[0], into(pf, 0))])
    around = neighbours(uf, (1, 2, 3), steps)
    sum_coefs(ef, cf, (1, 2), steps)
    ecoef[:, TAIL] = to_rim(get(cf, 2), 2, core_step, 3) + to_rim(get(cf, 3), 3, core_step, 3)
    mix(links, get(uf, 1), [(cf[1], into(pf, 1)), (ef[1], into(qf, 1))])
    mix(links, get(uf, 2), [(ef[2], into(qf, 2))])
    qc[:, lo(2)] = jnp.zeros((MODES, PLANE), jnp.float32)
    for t, x in around.items():
        mix(links, x, [(cf[t], into(qf, t, -1))])
    rim = from_rim(near[...], near_step[:, 4 * PLANE :])
    begun[:, BEGUN_U] = rim + to_rim(get(uf, 2), 2, core_step) + to_rim(get(uf, 3), 3, core_step)
    for t in (1, 2, 3):
        begun[:, lo(t - 1)] = product(get(pf, t), core_step[:, :PLANE])
    begun[:, BEGUN_P] = to_rim(get(pf, 2), 2, core_step) + to_rim(get(pf, 3), 3, core_step)


def step_kernel(own_ref, inner_ref, outer_ref, coef_own, pc_own, mix3, links, core_step, near_step, coef_inner, ecoef_known, pc_known, qc_known, near_known, begun, out_ref, rims, coef_outer, coef_rims, ecoef, pc, qc, search, pc2, qc2, sol, res, mix4):
    steps = (core_step, near_step)
    uf = {}
    for t, (ref, plane) in enumerate(((inner_ref, 1), (inner_ref, 0), (own_ref, 0), (own_ref, 1), (outer_ref, 1), (outer_ref, 0))):
        uf[t] = functools.partial(plane_of, ref, plane)
    near_new = turn(tile_of(outer_ref, CORE_TILES), 2 * RIM_PLANE)
    near_new = jnp.where(lanes((MODES, 128)) < 3 * RIM_PLANE, 0.0, near_new)
    rims[:, NEAR] = near_known[...] + near_new
    uf["near"] = (rims, NEAR)

    coef_outer[...] = slab_coefs(outer_ref)
    near = near_of(coef_inner[:, TAIL], coef_own[:, TAIL], coef_outer[:, TAIL])
    coef_rims[:, NEAR] = near
    coef_rims[:, FAR] = near
    cf = {0: (coef_inner, lo(1)), 1: (coef_inner, lo(0)), 2: (coef_own, lo(0)), 3: (coef_own, lo(1))}
    cf.update({4: (coef_outer, lo(1)), 5: (coef_outer, lo(0)), "near": (coef_rims, NEAR)})
    ef = {t: (ecoef_known, lo(t - 1)) for t in (1, 2)}
    ef.update({3: (ecoef, lo(0)), 4: (ecoef, lo(1)), "near": (ecoef, TAIL)})

    pf = {0: (pc_known, lo(0)), 1: (pc_known, lo(1)), 2: (pc_own, lo(0)), 3: (pc_own, lo(1)), 4: (pc, lo(0)), 5: (pc, lo(1))}
    pf["near"] = (pc, TAIL)
    qf = {1: (qc_known, lo(0)), 2: (qc_known, lo(1)), 3: (qc, lo(0)), 4: (qc, lo(1)), "near": (qc, TAIL)}
    all_rims = slice(TAIL.start, FAR_TAIL.stop)
    qc[:, lo(0)] = qc_known[:, lo(2)]
    mix(links, get(uf, 5), [(cf[5], into(pf, 5))])
    around = neighbours(uf, (4,), steps)[4]
    rims[:, FAR] = begun[:, BEGUN_U] + from_rim(near_new, near_step[:, 4 * PLANE :])
    rim_sums = [((coef_rims, slice(0, 256)), pc), ((ecoef, all_rims), qc)]
    mix(links, get(uf, 4), [(cf[4], into(pf, 4)), (cf[3], into(qf, 3, -1))], mix4)
    sum_coefs(ef, cf, (3, 4), steps)
    ecoef[:, TAIL] = ecoef_known[:, TAIL] + product(near, near_step[:128, 4 * PLANE :], 3) + 6.0 * near
    ecoef[:, FAR_TAIL] = jnp.zeros((COEF_ROWS, 128), jnp.float32)
    mix(links, rims[...], [(weights, into({0: (ref, all_rims)}, 0)) for weights, ref in rim_sums])
    known = {t: begun[:, lo(t - 1)] for t in (1, 2, 3)}
    known["near"] = begun[:, BEGUN_P]
    around_p = neighbours(pf, (1, 2, 3, 4, "near"), steps, known)
    qc[:, lo(1)] = jnp.zeros((MODES, PLANE), jnp.float32)
    mix(links, around, [(cf[4], into(qf, 4, -1))])
    mix(links, get(uf, 3), [(ef[3], into(qf, 3, 1))], known=mix3)
    mix(links, get(uf, 4), [(ef[4], into(qf, 4, 1))], known=mix4)

    sigma = THETA / DELTA
    rho = 1.0 / sigma
    rho_next = 1.0 / (2.0 * sigma - rho)
    sf = {t: (search, lo(t - 1)) for t in (1, 2, 3, 4)}
    sf["near"] = (search, NEAR_TAIL)
    for t, x in around_p.items():
        start = get(uf, t)
        q = get(qf, t) - (pc[:, FAR_TAIL] if t == "near" else 0.0)
        au = start + 0.5 * (q - x)
        begin = start * (1.0 / THETA)
        r1 = start - au * (1.0 / THETA)
        new = (rho_next * rho) * begin + (2.0 * rho_next / DELTA) * r1
        new = jnp.where(cf[t][0][KL : KL + 1, cf[t][1]] > 0.0, new, 0.0)
        if t in (2, 3):
            res[:, lo(t - 2)] = r1
            sol[:, lo(t - 2)] = begin + new
        put(sf, t, new)

    pf = {t: (pc2, at) for t, (_, at) in sf.items()}
    qf = {t: (qc2, lo(t - 2)) for t in (2, 3)}
    around = neighbours(sf, (2, 3), steps)
    for t in (1, 2, 3, 4, "near"):
        sums = [(cf[t], into(pf, t))]
        if t in (2, 3):
            sums.append((ef[t], into(qf, t)))
        mix(links, get(sf, t), sums)
    around_p = neighbours(pf, (2, 3), steps)
    for t, x in around.items():
        mix(links, x, [(cf[t], into(qf, t, -1))])
    for t, x in around_p.items():
        res[:, lo(t - 2)] = res[:, lo(t - 2)] - (get(sf, t) + 0.5 * (get(qf, t) - x))
    for f, field in enumerate((sol, res)):
        for j in range(OUT_TILES):
            n = (f * OUT_TILES + j) * OWN
            out_ref[:, n : n + OWN, :] = field[:, 128 * j : 128 * (j + 1)].reshape(GROUPS, OWN, 128)


def unpack_kernel(in_ref, table_ref, sol_hbm, res_hbm, halves, sems):
    flip = 1 - lax.rem(lax.axis_index("space"), 2)
    scale = 1.0 / mode_scale(table_ref[...])
    lane = lanes((OWN, 128))
    per = 128 // ZC
    copies = []
    for f, hbm in enumerate((sol_hbm, res_hbm)):
        for h in range(NZ // 128):
            for p in range(ROWS):
                plane, y = p // NY, p % NY
                row = (plane + flip * (1 - 2 * plane)) * NY + y
                j, i = p // per, p % per
                tile = None
                for n in range(per):
                    w = in_ref[per * h + n, (f * OUT_TILES + j) * OWN : (f * OUT_TILES + j + 1) * OWN, :]
                    w = turn(w, ZC * (n - i))
                    tile = w if n == 0 else jnp.where(lane >= ZC * n, w, tile)
                halves[f, h, pl.ds(row, OWN, stride=ROWS), :] = tile * scale
            copy = pltpu.make_async_copy(halves.at[f, h], hbm.at[:, pl.ds(128 * h, 128)], sems.at[f, h])
            copy.start()
            copies.append(copy)
    for copy in copies:
        copy.wait()


def whole(count):
    return [pl.BlockSpec(memory_space=pltpu.VMEM)] * count


def anywhere(count):
    return [pl.BlockSpec(memory_space=pltpu.HBM)] * count


def body(load, mean_coeff, kl_ratio, chaos_table):
    params = pltpu.CompilerParams(vmem_limit_bytes=VMEM)
    f32, bf16 = jnp.float32, jnp.bfloat16
    vmem = pltpu.VMEM
    halves = NZ // 128
    table = chaos_table.T
    send = pl.pallas_call(
        pack_kernel,
        out_shape=jax.ShapeDtypeStruct((GROUPS, SEND_ROWS, 128), f32),
        in_specs=anywhere(4),
        out_specs=pl.BlockSpec(memory_space=vmem),
        scratch_shapes=[
            vmem((halves, OWN * ROWS, 128), f32),
            vmem((ROWS, NZ), f32),
            vmem((KL * ROWS, NZ), f32),
            vmem((KL, MODES), jnp.int32),
            pltpu.SemaphoreType.DMA((3 + halves,)),
        ],
        compiler_params=pltpu.CompilerParams(vmem_limit_bytes=VMEM),
        name="pack",
    )(*(pltpu.with_memory_space_constraint(x, pltpu.HBM) for x in (load.reshape(OWN * ROWS, NZ), mean_coeff.reshape(ROWS, NZ), kl_ratio.reshape(KL * ROWS, NZ), table)))
    own = lax.all_to_all(send, "mode", 0, 0, tiled=True)
    count = lax.axis_size("space")
    on_chip = [e for i in range(0, count, 2) for e in ((i, i + 1), (i + 1, i))]
    off_chip = [e for i in range(1, count - 1, 2) for e in ((i, i + 1), (i + 1, i))]
    outer = lax.ppermute(own, "space", off_chip)
    inner = lax.ppermute(own, "space", on_chip)
    shapes = [
        ((COEF_ROWS, 2 * PLANE + 128), f32),
        ((MODES, 2 * PLANE), f32),
        ((KL * MODES, PLANE), f32),
        ((KL * MODES, 2 * MODES), bf16),
        ((PLANE, PLANE + 2 * 128), bf16),
        ((256, 4 * PLANE + 128), bf16),
    ]
    state = pl.pallas_call(
        prep_kernel,
        out_shape=[jax.ShapeDtypeStruct(*shape) for shape in shapes],
        in_specs=whole(2),
        out_specs=whole(len(shapes)),
        scratch_shapes=[vmem((MODES, MODES), f32)],
        compiler_params=params,
        cost_estimate=pl.CostEstimate(flops=1 << 34, bytes_accessed=1 << 22, transcendentals=0),
        name="step_prep",
    )(own, table)
    more = [
        ((COEF_ROWS, 2 * PLANE + 128), f32),
        ((COEF_ROWS, 2 * PLANE + 128), f32),
        ((MODES, 2 * PLANE), f32),
        ((MODES, 3 * PLANE), f32),
        ((MODES, 128), f32),
        ((MODES, 3 * PLANE + 256), f32),
    ]
    between = pl.pallas_call(
        between_kernel,
        out_shape=[jax.ShapeDtypeStruct(*shape) for shape in more],
        in_specs=whole(2 + len(shapes)),
        out_specs=whole(len(more)),
        compiler_params=params,
        cost_estimate=pl.CostEstimate(flops=1 << 10, bytes_accessed=1 << 10, transcendentals=0),
        name="step_between",
    )(own, inner, *state)
    back = pl.pallas_call(
        step_kernel,
        out_shape=jax.ShapeDtypeStruct((GROUPS, 2 * OUT_TILES * OWN, 128), f32),
        in_specs=whole(3 + len(shapes) + len(more)),
        out_specs=pl.BlockSpec(memory_space=vmem),
        scratch_shapes=[
            vmem((MODES, 256), f32),
            vmem((COEF_ROWS, 2 * PLANE + 128), f32),
            vmem((COEF_ROWS, 256), f32),
            vmem((COEF_ROWS, 2 * PLANE + 256), f32),
            vmem((MODES, 2 * PLANE + 256), f32),
            vmem((MODES, 2 * PLANE + 256), f32),
        ]
        + [vmem((MODES, 4 * PLANE + 128), f32)] * 2
        + [vmem((MODES, 2 * PLANE), f32)] * 3
        + [vmem((KL * MODES, PLANE), f32)],
        compiler_params=params,
        cost_estimate=pl.CostEstimate(flops=2 << 30, bytes_accessed=1 << 22, transcendentals=0),
        name="step",
    )(own, inner, outer, *state, *between)
    back = lax.all_to_all(back, "mode", 0, 0, tiled=True)
    flat = jax.ShapeDtypeStruct((OWN * ROWS, NZ), f32)
    sol, res = pl.pallas_call(
        unpack_kernel,
        out_shape=(flat, flat),
        in_specs=whole(2),
        out_specs=tuple(anywhere(2)),
        scratch_shapes=[vmem((2, halves, OWN * ROWS, 128), f32), pltpu.SemaphoreType.DMA((2, halves))],
        compiler_params=params,
        name="unpack",
    )(back, table)
    return sol.reshape(load.shape), res.reshape(load.shape)


def solution(mesh):
    in_specs = (
        P("mode", "space", None, None),
        P("space", None, None),
        P(None, "space", None, None),
        P(),
    )
    out_specs = (P("mode", "space", None, None), P("mode", "space", None, None))
    return jax.shard_map(body, mesh=mesh, in_specs=in_specs, out_specs=out_specs, check_vma=False)
```

```python
import functools

import jax
import jax.numpy as jnp
from jax import lax
from jax.experimental import pallas as pl
from jax.experimental.pallas import tpu as pltpu
from jax.sharding import PartitionSpec as P

ITERS = 2
THETA = 24.5
DELTA = 23.5
KL = 10
MODES = 128
GROUPS = 8
OWN = MODES // GROUPS
NX_OWN = 2
NY = 8
NZ = 256
ROWS = NX_OWN * NY
ZC = NZ // GROUPS
HALO = 2
PLANE = NY * ZC
CORE_TILES = NX_OWN * PLANE // 128
RIM = 2 * HALO
RIM_PLANE = NY * RIM
SPARE = NX_OWN * RIM_PLANE
TERMS = KL + 1
COEF_ROWS = 16
SEND_ROWS = (CORE_TILES + 1) * OWN
OUT_TILES = CORE_TILES
BLOCK = 32
SQRT2 = 2.0**0.5
SQRT6 = 6.0**0.5
VMEM = 40 * 1024 * 1024


def lanes(shape):
    return lax.broadcasted_iota(jnp.int32, shape, len(shape) - 1)


def mode_scale(t):
    f = jnp.where(t >= 3, SQRT6, jnp.where(t == 2, SQRT2, 1.0)).astype(jnp.float32)
    f = jnp.max(f, axis=0, keepdims=True)
    shape = (OWN, MODES)
    mine = lanes(shape) == lax.broadcasted_iota(jnp.int32, shape, 0) + OWN * lax.axis_index("mode")
    return jnp.sum(jnp.where(mine, f, 0.0), axis=1, keepdims=True)


def turn(x, by):
    by = by % x.shape[1]
    return pltpu.roll(x, by, 1) if by else x


def edges_of(tiles, at, lane):
    out = []
    for e in range(GROUPS + 1):
        z = ZC * e - HALO
        total = None
        for n, tile in enumerate(tiles):
            lo, hi = max(z, 128 * n), min(z + RIM, 128 * (n + 1))
            if lo >= hi:
                continue
            w = turn(tile, at - z)
            w = jnp.where((lane >= at + lo - z) & (lane < at + hi - z), w, 0.0)
            total = w if total is None else total + w
        out.append(total)
    return out


def pack_kernel(load_hbm, mean_hbm, ratio_hbm, table_hbm, out_ref, halves, mean_ref, ratio_ref, table_ref, sems):
    copies = [
        pltpu.make_async_copy(ratio_hbm, ratio_ref, sems.at[0]),
        pltpu.make_async_copy(mean_hbm, mean_ref, sems.at[1]),
        pltpu.make_async_copy(table_hbm, table_ref, sems.at[2]),
    ] + [
        pltpu.make_async_copy(load_hbm.at[:, pl.ds(128 * h, 128)], halves.at[h], sems.at[3 + h])
        for h in range(NZ // 128)
    ]
    for copy in copies:
        copy.start()
    me = lax.axis_index("mode")
    flip = 1 - lax.rem(lax.axis_index("space"), 2)
    lane = lanes((OWN, 128))
    per = 128 // ZC
    for copy in copies[:2]:
        copy.wait()

    def row_of(p):
        plane, y = p // NY, lax.rem(p, NY)
        return (plane + flip * (1 - 2 * plane)) * NY + y

    coefs = []
    for i in range(2):
        row = row_of(2 * me + i)
        mean = mean_ref[pl.ds(row, 1), :]
        terms = [mean * ratio_ref[pl.ds(row + k * ROWS, 1), :] for k in range(KL)] + [mean]
        zero = jnp.zeros_like(mean)
        low = jnp.concatenate(terms + terms[:5], axis=0)
        mid = jnp.concatenate([zero] * 11 + terms[5:10], axis=0)
        top = jnp.concatenate([zero] * 11 + terms[10:] + [zero] * 4, axis=0)
        coefs.append([(c[:, :128], c[:, 128:]) for c in (low, mid, top)])
    lane8 = lanes((8, 128))
    sub8 = lax.broadcasted_iota(jnp.int32, (8, 128), 0)
    first = (lane8 & (RIM - 1)) < HALO
    borders = [jnp.zeros((8, 128), jnp.float32)] * (GROUPS + 1)
    for i in range(2):
        for g in range(3):
            tiles = [c[8:, :] for c in coefs[i][g]]
            more = edges_of(tiles, SPARE + 2 * RIM * g + RIM * i, lane8)
            borders = [x + y for x, y in zip(borders, more)]
    base = []
    for d in range(GROUPS):
        own_cells = []
        for i in range(2):
            w = turn(coefs[i][0][d // per], SPARE + ZC * i - ZC * (d % per))
            own_cells.append(jnp.where((lane >= SPARE + ZC * i) & (lane < SPARE + ZC * (i + 1)), w, 0.0))
        own_cells = own_cells[0] + own_cells[1]
        low = jnp.where(sub8 < TERMS - 8, own_cells[8:, :], jnp.where(first, borders[d], borders[d + 1]))
        base.append(jnp.concatenate([own_cells[:8, :], low], axis=0))

    for copy in copies[2:]:
        copy.wait()
    scale = mode_scale(table_ref[...])
    first = (lane & (RIM - 1)) < HALO
    borders = [jnp.zeros((OWN, 128), jnp.float32)] * (GROUPS + 1)
    for j in range(CORE_TILES):
        rows = []
        for i in range(per):
            row = row_of(jnp.int32(per * j + i))
            rows.append([halves[h, pl.ds(row, OWN, stride=ROWS), :] * scale for h in range(NZ // 128)])
            more = edges_of(rows[i], RIM * (per * j + i), lane)
            borders = [x + y for x, y in zip(borders, more)]
        for d in range(GROUPS):
            tile = None
            for i in range(per):
                w = turn(rows[i][d // per], ZC * (i - d % per))
                tile = w if i == 0 else jnp.where(lane >= ZC * i, w, tile)
            out_ref[d, OWN * j : OWN * (j + 1), :] = tile
    for d in range(GROUPS):
        out_ref[d, CORE_TILES * OWN :, :] = base[d] + jnp.where(first, borders[d], borders[d + 1])


def build_links(table_ref, links, pad):
    pad[...] = jnp.zeros_like(pad)
    pad[:KL, :] = table_ref[...].astype(jnp.float32)
    cols = pad[...]
    rows = jnp.transpose(cols)
    apart = jnp.zeros((MODES, MODES), jnp.float32)
    for k in range(KL):
        apart = apart + jnp.abs(rows[:, k : k + 1] - cols[k : k + 1, :])
    near = apart == 1.0
    for k in range(KL):
        mine = rows[:, k : k + 1]
        d = mine - cols[k : k + 1, :]
        t = jnp.where(near, jnp.where(d == -1.0, 1.0, jnp.where(d == 1.0, mine + jnp.zeros_like(d), 0.0)), 0.0)
        t = t.astype(jnp.bfloat16)
        for b in range(MODES // BLOCK):
            at = (KL * b + k) * BLOCK
            links[at : at + BLOCK, :MODES] = t[BLOCK * b : BLOCK * (b + 1), :]
            links[at : at + BLOCK, MODES:] = t[BLOCK * b : BLOCK * (b + 1), :]


def core_cell(l):
    return l >> 5, l & (ZC - 1)


def rim_cell(l):
    zi = l & (RIM - 1)
    return (l >> 2) & (NY - 1), jnp.where(zi < HALO, zi - HALO, zi + ZC - HALO)


def grid_of(shape, rows_of, cols_of):
    a = rows_of(lax.broadcasted_iota(jnp.int32, shape, 0))
    b = cols_of(lax.broadcasted_iota(jnp.int32, shape, 1))
    return sum(jnp.abs(x - y) for x, y in zip(a, b))


def build_steps(core_step, near_step):
    def fill(ref, to, apart, times=1):
        for n in range(times):
            ref[apart.shape[0] * n : apart.shape[0] * (n + 1), to : to + apart.shape[1]] = jnp.where(
                apart == 1, 1.0, 0.0
            ).astype(jnp.bfloat16)

    fill(core_step, 0, grid_of((PLANE, PLANE), core_cell, core_cell))
    for t in (1, 2, 3, 4):

        def rim_at(l, t=t):
            y, z = rim_cell(l)
            return y + jnp.where((l >> 5) == t - 1, 0, 100), z

        if t in (2, 3):
            fill(core_step, PLANE + 128 * (t - 2), grid_of((PLANE, 128), core_cell, rim_at))
        fill(near_step, PLANE * (t - 1), grid_of((128, PLANE), rim_at, core_cell), 2)

    def near(l):
        return ((l >> 5),) + rim_cell(l)

    fill(near_step, 4 * PLANE, grid_of((128, 128), near, near), 2)


def tile_of(ref, j):
    return ref[:, OWN * j : OWN * (j + 1), :].reshape(MODES, 128)


def plane_of(ref, plane):
    half = PLANE // 128
    return jnp.concatenate([tile_of(ref, half * plane + h) for h in range(half)], axis=1)


def near_of(inner, own, outer):
    lane = lanes(own.shape)
    out = jnp.where((lane >= RIM_PLANE) & (lane < 3 * RIM_PLANE), turn(own, RIM_PLANE), 0.0)
    if inner is not None:
        out = jnp.where(lane < RIM_PLANE, inner, out)
    if outer is not None:
        out = jnp.where(lane < 3 * RIM_PLANE, out, turn(outer, 2 * RIM_PLANE))
    return out


def slab_coefs(ref):
    lane = lanes((OWN, 128))
    raw = [ref[m, CORE_TILES * OWN :, :] for m in range(GROUPS)]
    core = [jnp.where(lane < SPARE, turn(raw[2 * j], -SPARE), raw[2 * j + 1]) for j in range(CORE_TILES)]
    lane8 = lanes((8, 128))
    parts = []
    for g in range(3):
        total = jnp.zeros((8, 128), jnp.float32)
        for m in range(GROUPS):
            lo = 2 * RIM * m
            w = turn(raw[m][8:, :], lo - SPARE - 2 * RIM * g)
            total = jnp.where((lane8 >= lo) & (lane8 < lo + 2 * RIM), w, total)
        parts.append(total[3:, :])
    rim = jnp.concatenate(parts + [jnp.zeros((1, 128), jnp.float32)], axis=0)
    return jnp.concatenate(core + [rim], axis=1)


def parts_of(x, count, axis=0):
    out = []
    for _ in range(count - 1):
        h = x.astype(jnp.bfloat16)
        out.append(h)
        x = x - h.astype(jnp.float32)
    return jnp.concatenate(out + [x.astype(jnp.bfloat16)], axis=axis)


def get(field, t):
    part = field[t]
    return part() if callable(part) else part[0][:, part[1]]


def put(field, t, x):
    ref, at = field[t]
    ref[:, at] = x


def product(x, matrix, parts=2):
    out = jnp.dot(parts_of(x, parts), matrix, preferred_element_type=jnp.float32)
    return sum(out[x.shape[0] * i : x.shape[0] * (i + 1)] for i in range(parts))


def from_rim(x, matrix):
    return jnp.dot(parts_of(x, 2, 1), matrix, preferred_element_type=jnp.float32)


def to_rim(x, t, core_step, parts=2):
    return product(x, core_step[:, PLANE + 128 * (t - 2) : PLANE + 128 * (t - 1)], parts)


def neighbours(src, slots, steps, begun={}):
    core_step, near_step = steps
    out = {}
    near = get(src, "near")
    for t in slots:
        if t == "near":
            out[t] = begun[t] + from_rim(near, near_step[:, 4 * PLANE :])
        else:
            x = begun[t] if t in begun else product(get(src, t), core_step[:, :PLANE])
            x = x + from_rim(near, near_step[:, PLANE * (t - 1) : PLANE * t])
            out[t] = x + (get(src, t - 1) + get(src, t + 1))
    return out


def sum_coefs(dst, src, slots, steps):
    core_step, near_step = steps
    near = get(src, "near")
    for t in slots:
        x = product(get(src, t), core_step[:, :PLANE], 3)
        x = x + product(near, near_step[:128, PLANE * (t - 1) : PLANE * t], 3)
        put(dst, t, x + (get(src, t - 1) + get(src, t + 1)) + 6.0 * get(src, t))


def mix(links, x, sums, kept=None, known=None):
    width = x.shape[1]
    pair = parts_of(x, 2) if known is None else None
    rows_of = [
        [jnp.broadcast_to(ref[k : k + 1, at], (8, width)) for k in range(TERMS)] for (ref, at), _ in sums
    ]
    split = lambda x: x.reshape(BLOCK // 8, 8, width)
    for b in range(MODES // BLOCK):
        rows = slice(BLOCK * b, BLOCK * (b + 1))
        at = slice(KL * BLOCK * b, KL * BLOCK * (b + 1))
        if known is None:
            mixed = jnp.dot(links[at, :], pair, preferred_element_type=jnp.float32)
        else:
            mixed = known[at, :]
        if kept is not None:
            kept[at, :] = mixed
        here = split(x[rows, :])
        totals = [here * weights[KL][None] for weights in rows_of]
        for k in range(KL):
            part = split(mixed[BLOCK * k : BLOCK * (k + 1), :])
            totals = [total + part * weights[k][None] for total, weights in zip(totals, rows_of)]
        for total, (_, finish) in zip(totals, sums):
            finish(rows, total.reshape(BLOCK, width))


def into(field, t, sign=0):
    ref, at = field[t]

    def finish(rows, total):
        if sign:
            total = ref[rows, at] + total if sign > 0 else ref[rows, at] - total
        ref[rows, at] = total

    return finish


def prep_kernel(own_ref, table_ref, coef, pc, mix3, links, core_step, near_step, pad):
    build_links(table_ref, links, pad)
    coef[...] = slab_coefs(own_ref)
    for plane, kept in ((0, None), (1, mix3)):
        at = slice(PLANE * plane, PLANE * (plane + 1))
        mix(links, plane_of(own_ref, plane), [((coef, at), into({plane: (pc, at)}, plane))], kept)
    build_steps(core_step, near_step)


def lo(n):
    return slice(PLANE * n, PLANE * (n + 1))


NEAR, FAR = slice(0, 128), slice(128, 256)
TAIL = slice(2 * PLANE, 2 * PLANE + 128)
FAR_TAIL = slice(2 * PLANE + 128, 2 * PLANE + 256)
BEGUN_U, BEGUN_P = slice(3 * PLANE, 3 * PLANE + 128), slice(3 * PLANE + 128, 3 * PLANE + 256)
NEAR_TAIL = slice(4 * PLANE, 4 * PLANE + 128)


def between_kernel(own_ref, inner_ref, coef_own, pc_own, mix3, links, core_step, near_step, coef_inner, ecoef, pc, qc, near, begun):
    steps = (core_step, near_step)
    uf = {0: functools.partial(plane_of, inner_ref, 1), 1: functools.partial(plane_of, inner_ref, 0)}
    uf.update({2: functools.partial(plane_of, own_ref, 0), 3: functools.partial(plane_of, own_ref, 1)})
    inner = tile_of(inner_ref, CORE_TILES)
    near[...] = near_of(inner, tile_of(own_ref, CORE_TILES), None)
    uf["near"] = (near, NEAR)
    uf[4] = lambda: jnp.zeros((MODES, PLANE), jnp.float32)
    coef_inner[...] = slab_coefs(inner_ref)
    cf = {0: (coef_inner, lo(1)), 1: (coef_inner, lo(0)), 2: (coef_own, lo(0)), 3: (coef_own, lo(1))}
    cf["near"] = lambda: near_of(coef_inner[:, TAIL], coef_own[:, TAIL], None)
    ef = {t: (ecoef, lo(t - 1)) for t in (1, 2)}
    pf = {0: (pc, lo(0)), 1: (pc, lo(1)), 2: (pc_own, lo(0)), 3: (pc_own, lo(1))}
    qf = {t: (qc, lo(t - 1)) for t in (1, 2, 3)}
    mix(links, get(uf, 0), [(cf[0], into(pf, 0))])
    around = neighbours(uf, (1, 2, 3), steps)
    sum_coefs(ef, cf, (1, 2), steps)
    ecoef[:, TAIL] = to_rim(get(cf, 2), 2, core_step, 3) + to_rim(get(cf, 3), 3, core_step, 3)
    mix(links, get(uf, 1), [(cf[1], into(pf, 1)), (ef[1], into(qf, 1))])
    mix(links, get(uf, 2), [(ef[2], into(qf, 2))])
    qc[:, lo(2)] = jnp.zeros((MODES, PLANE), jnp.float32)
    for t, x in around.items():
        mix(links, x, [(cf[t], into(qf, t, -1))])
    rim = from_rim(near[...], near_step[:, 4 * PLANE :])
    begun[:, BEGUN_U] = rim + to_rim(get(uf, 2), 2, core_step) + to_rim(get(uf, 3), 3, core_step)
    for t in (1, 2, 3):
        begun[:, lo(t - 1)] = product(get(pf, t), core_step[:, :PLANE])
    begun[:, BEGUN_P] = to_rim(get(pf, 2), 2, core_step) + to_rim(get(pf, 3), 3, core_step)


def step_kernel(own_ref, inner_ref, outer_ref, coef_own, pc_own, mix3, links, core_step, near_step, coef_inner, ecoef_known, pc_known, qc_known, near_known, begun, out_ref, rims, coef_outer, coef_rims, ecoef, pc, qc, search, pc2, qc2, sol, res, mix4):
    steps = (core_step, near_step)
    uf = {}
    for t, (ref, plane) in enumerate(((inner_ref, 1), (inner_ref, 0), (own_ref, 0), (own_ref, 1), (outer_ref, 1), (outer_ref, 0))):
        uf[t] = functools.partial(plane_of, ref, plane)
    near_new = turn(tile_of(outer_ref, CORE_TILES), 2 * RIM_PLANE)
    near_new = jnp.where(lanes((MODES, 128)) < 3 * RIM_PLANE, 0.0, near_new)
    rims[:, NEAR] = near_known[...] + near_new
    uf["near"] = (rims, NEAR)

    coef_outer[...] = slab_coefs(outer_ref)
    near = near_of(coef_inner[:, TAIL], coef_own[:, TAIL], coef_outer[:, TAIL])
    coef_rims[:, NEAR] = near
    coef_rims[:, FAR] = near
    cf = {0: (coef_inner, lo(1)), 1: (coef_inner, lo(0)), 2: (coef_own, lo(0)), 3: (coef_own, lo(1))}
    cf.update({4: (coef_outer, lo(1)), 5: (coef_outer, lo(0)), "near": (coef_rims, NEAR)})
    ef = {t: (ecoef_known, lo(t - 1)) for t in (1, 2)}
    ef.update({3: (ecoef, lo(0)), 4: (ecoef, lo(1)), "near": (ecoef, TAIL)})

    pf = {0: (pc_known, lo(0)), 1: (pc_known, lo(1)), 2: (pc_own, lo(0)), 3: (pc_own, lo(1)), 4: (pc, lo(0)), 5: (pc, lo(1))}
    pf["near"] = (pc, TAIL)
    qf = {1: (qc_known, lo(0)), 2: (qc_known, lo(1)), 3: (qc, lo(0)), 4: (qc, lo(1)), "near": (qc, TAIL)}
    all_rims = slice(TAIL.start, FAR_TAIL.stop)
    qc[:, lo(0)] = qc_known[:, lo(2)]
    mix(links, get(uf, 5), [(cf[5], into(pf, 5))])
    around = neighbours(uf, (4,), steps)[4]
    rims[:, FAR] = begun[:, BEGUN_U] + from_rim(near_new, near_step[:, 4 * PLANE :])
    rim_sums = [((coef_rims, slice(0, 256)), pc), ((ecoef, all_rims), qc)]
    mix(links, get(uf, 4), [(cf[4], into(pf, 4)), (cf[3], into(qf, 3, -1))], mix4)
    sum_coefs(ef, cf, (3, 4), steps)
    ecoef[:, TAIL] = ecoef_known[:, TAIL] + product(near, near_step[:128, 4 * PLANE :], 3) + 6.0 * near
    ecoef[:, FAR_TAIL] = jnp.zeros((COEF_ROWS, 128), jnp.float32)
    mix(links, rims[...], [(weights, into({0: (ref, all_rims)}, 0)) for weights, ref in rim_sums])
    known = {t: begun[:, lo(t - 1)] for t in (1, 2, 3)}
    known["near"] = begun[:, BEGUN_P]
    around_p = neighbours(pf, (1, 2, 3, 4, "near"), steps, known)
    qc[:, lo(1)] = jnp.zeros((MODES, PLANE), jnp.float32)
    mix(links, around, [(cf[4], into(qf, 4, -1))])
    mix(links, get(uf, 3), [(ef[3], into(qf, 3, 1))], known=mix3)
    mix(links, get(uf, 4), [(ef[4], into(qf, 4, 1))], known=mix4)

    sigma = THETA / DELTA
    rho = 1.0 / sigma
    rho_next = 1.0 / (2.0 * sigma - rho)
    sf = {t: (search, lo(t - 1)) for t in (1, 2, 3, 4)}
    sf["near"] = (search, NEAR_TAIL)
    for t, x in around_p.items():
        start = get(uf, t)
        q = get(qf, t) - (pc[:, FAR_TAIL] if t == "near" else 0.0)
        au = start + 0.5 * (q - x)
        begin = start * (1.0 / THETA)
        r1 = start - au * (1.0 / THETA)
        new = (rho_next * rho) * begin + (2.0 * rho_next / DELTA) * r1
        new = jnp.where(cf[t][0][KL : KL + 1, cf[t][1]] > 0.0, new, 0.0)
        if t in (2, 3):
            res[:, lo(t - 2)] = r1
            sol[:, lo(t - 2)] = begin + new
        put(sf, t, new)

    pf = {t: (pc2, at) for t, (_, at) in sf.items()}
    qf = {t: (qc2, lo(t - 2)) for t in (2, 3)}
    around = neighbours(sf, (2, 3), steps)
    for t in (1, 2, 3, 4, "near"):
        sums = [(cf[t], into(pf, t))]
        if t in (2, 3):
            sums.append((ef[t], into(qf, t)))
        mix(links, get(sf, t), sums)
    around_p = neighbours(pf, (2, 3), steps)
    for t, x in around.items():
        mix(links, x, [(cf[t], into(qf, t, -1))])
    for t, x in around_p.items():
        res[:, lo(t - 2)] = res[:, lo(t - 2)] - (get(sf, t) + 0.5 * (get(qf, t) - x))
    for f, field in enumerate((sol, res)):
        for j in range(OUT_TILES):
            n = (f * OUT_TILES + j) * OWN
            out_ref[:, n : n + OWN, :] = field[:, 128 * j : 128 * (j + 1)].reshape(GROUPS, OWN, 128)


def unpack_kernel(in_ref, table_ref, sol_hbm, res_hbm, halves, sems):
    flip = 1 - lax.rem(lax.axis_index("space"), 2)
    scale = 1.0 / mode_scale(table_ref[...])
    lane = lanes((OWN, 128))
    per = 128 // ZC
    copies = []
    for f, hbm in enumerate((sol_hbm, res_hbm)):
        for h in range(NZ // 128):
            for p in range(ROWS):
                plane, y = p // NY, p % NY
                row = (plane + flip * (1 - 2 * plane)) * NY + y
                j, i = p // per, p % per
                tile = None
                for n in range(per):
                    w = in_ref[per * h + n, (f * OUT_TILES + j) * OWN : (f * OUT_TILES + j + 1) * OWN, :]
                    w = turn(w, ZC * (n - i))
                    tile = w if n == 0 else jnp.where(lane >= ZC * n, w, tile)
                halves[f, h, pl.ds(row, OWN, stride=ROWS), :] = tile * scale
            copy = pltpu.make_async_copy(halves.at[f, h], hbm.at[:, pl.ds(128 * h, 128)], sems.at[f, h])
            copy.start()
            copies.append(copy)
    for copy in copies:
        copy.wait()


def whole(count):
    return [pl.BlockSpec(memory_space=pltpu.VMEM)] * count


def anywhere(count):
    return [pl.BlockSpec(memory_space=pltpu.HBM)] * count


def body(load, mean_coeff, kl_ratio, chaos_table):
    params = pltpu.CompilerParams(vmem_limit_bytes=VMEM)
    f32, bf16 = jnp.float32, jnp.bfloat16
    vmem = pltpu.VMEM
    halves = NZ // 128
    table = chaos_table.T
    send = pl.pallas_call(
        pack_kernel,
        out_shape=jax.ShapeDtypeStruct((GROUPS, SEND_ROWS, 128), f32),
        in_specs=anywhere(4),
        out_specs=pl.BlockSpec(memory_space=vmem),
        scratch_shapes=[
            vmem((halves, OWN * ROWS, 128), f32),
            vmem((ROWS, NZ), f32),
            vmem((KL * ROWS, NZ), f32),
            vmem((KL, MODES), jnp.int32),
            pltpu.SemaphoreType.DMA((3 + halves,)),
        ],
        compiler_params=pltpu.CompilerParams(vmem_limit_bytes=VMEM),
        name="pack",
    )(*(pltpu.with_memory_space_constraint(x, pltpu.HBM) for x in (load.reshape(OWN * ROWS, NZ), mean_coeff.reshape(ROWS, NZ), kl_ratio.reshape(KL * ROWS, NZ), table)))
    own = lax.all_to_all(send, "mode", 0, 0, tiled=True)
    count = lax.axis_size("space")
    on_chip = [e for i in range(0, count, 2) for e in ((i, i + 1), (i + 1, i))]
    off_chip = [e for i in range(1, count - 1, 2) for e in ((i, i + 1), (i + 1, i))]
    outer = lax.ppermute(own, "space", off_chip)
    inner = lax.ppermute(own, "space", on_chip)
    shapes = [
        ((COEF_ROWS, 2 * PLANE + 128), f32),
        ((MODES, 2 * PLANE), f32),
        ((KL * MODES, PLANE), f32),
        ((KL * MODES, 2 * MODES), bf16),
        ((PLANE, PLANE + 2 * 128), bf16),
        ((256, 4 * PLANE + 128), bf16),
    ]
    state = pl.pallas_call(
        prep_kernel,
        out_shape=[jax.ShapeDtypeStruct(*shape) for shape in shapes],
        in_specs=whole(2),
        out_specs=whole(len(shapes)),
        scratch_shapes=[vmem((MODES, MODES), f32)],
        compiler_params=params,
        cost_estimate=pl.CostEstimate(flops=1 << 34, bytes_accessed=1 << 22, transcendentals=0),
        name="step_prep",
    )(own, table)
    more = [
        ((COEF_ROWS, 2 * PLANE + 128), f32),
        ((COEF_ROWS, 2 * PLANE + 128), f32),
        ((MODES, 2 * PLANE), f32),
        ((MODES, 3 * PLANE), f32),
        ((MODES, 128), f32),
        ((MODES, 3 * PLANE + 256), f32),
    ]
    between = pl.pallas_call(
        between_kernel,
        out_shape=[jax.ShapeDtypeStruct(*shape) for shape in more],
        in_specs=whole(2 + len(shapes)),
        out_specs=whole(len(more)),
        compiler_params=params,
        cost_estimate=pl.CostEstimate(flops=1 << 10, bytes_accessed=1 << 10, transcendentals=0),
        name="step_between",
    )(own, inner, *state)
    back = pl.pallas_call(
        step_kernel,
        out_shape=jax.ShapeDtypeStruct((GROUPS, 2 * OUT_TILES * OWN, 128), f32),
        in_specs=whole(3 + len(shapes) + len(more)),
        out_specs=pl.BlockSpec(memory_space=vmem),
        scratch_shapes=[
            vmem((MODES, 256), f32),
            vmem((COEF_ROWS, 2 * PLANE + 128), f32),
            vmem((COEF_ROWS, 256), f32),
            vmem((COEF_ROWS, 2 * PLANE + 256), f32),
            vmem((MODES, 2 * PLANE + 256), f32),
            vmem((MODES, 2 * PLANE + 256), f32),
        ]
        + [vmem((MODES, 4 * PLANE + 128), f32)] * 2
        + [vmem((MODES, 2 * PLANE), f32)] * 3
        + [vmem((KL * MODES, PLANE), f32)],
        compiler_params=params,
        cost_estimate=pl.CostEstimate(flops=2 << 30, bytes_accessed=1 << 22, transcendentals=0),
        name="step",
    )(own, inner, outer, *state, *between)
    back = lax.all_to_all(back, "mode", 0, 0, tiled=True)
    flat = jax.ShapeDtypeStruct((OWN * ROWS, NZ), f32)
    sol, res = pl.pallas_call(
        unpack_kernel,
        out_shape=(flat, flat),
        in_specs=whole(2),
        out_specs=tuple(anywhere(2)),
        scratch_shapes=[vmem((2, halves, OWN * ROWS, 128), f32), pltpu.SemaphoreType.DMA((2, halves))],
        compiler_params=params,
        name="unpack",
    )(back, table)
    return sol.reshape(load.shape), res.reshape(load.shape)


def solution(mesh):
    in_specs = (
        P("mode", "space", None, None),
        P("space", None, None),
        P(None, "space", None, None),
        P(),
    )
    out_specs = (P("mode", "space", None, None), P("mode", "space", None, None))
    return jax.shard_map(body, mesh=mesh, in_specs=in_specs, out_specs=out_specs, check_vma=False)
```
